32 devices in a mesh: seq: 8 (over z, x), stream: 4 (over y, core).
Axes of the slice: x: 2, y: 2, z: 4, core: 2. Of those that a mesh axis runs over, the one named last changes fastest.
Arguments:
- inputs: bfloat16 [4, 4096, 2304], P('stream', 'seq'), may hold values from -12 to 12
- boundary: int32 [4, 4096], P('stream', 'seq'), may hold values from 0 to 1, as said below
- start_state: float32 [4, 2304], P('stream'), may hold values from -3 to 3
- weight: float32 [2, 2304, 6912], P(None, ('seq', 'stream')), may hold values from -0.09375 to 0.09375
- gate_bias: float32 [6912], P(('seq', 'stream')), may hold values from -3 to 8
- first_weight: float32 [2, 2304, 6912], P(None, ('seq', 'stream')), may hold values from -1 to 1
- second_weight: float32 [2, 2304, 6912], P(None, ('seq', 'stream')), may hold values from 0 to 1
- first_bias: float32 [6912], P(('seq', 'stream')), may hold values from -1 to 1
- second_bias: float32 [6912], P(('seq', 'stream')), may hold values from 0 to 1
- cotangent: bfloat16 [4, 4096, 2304], P('stream', 'seq'), may hold values from -6 to 6
- final_cotangent: float32 [4, 2304], P('stream'), may hold values from -6 to 6
Outputs:
- hidden: bfloat16 [4, 4096, 2304], P('stream', 'seq')
- final_state: float32 [4, 2304], P('stream', 'seq')
- input_gradient: bfloat16 [4, 4096, 2304], P('stream', 'seq')
- weight_gradient: float32 [2, 2304, 6912], P(None, ('seq', 'stream'))
- bias_gradient: float32 [6912], P(('seq', 'stream'))
- gradient_norm: float32 [], replicated
- new_weight: float32 [2, 2304, 6912], P(None, ('seq', 'stream'))
- new_first_weight: float32 [2, 2304, 6912], P(None, ('seq', 'stream'))
- new_second_weight: float32 [2, 2304, 6912], P(None, ('seq', 'stream'))
- new_bias: float32 [6912], P(('seq', 'stream'))
- new_first_bias: float32 [6912], P(('seq', 'stream'))
- new_second_bias: float32 [6912], P(('seq', 'stream'))
The draws below stay inside these ranges and needn't reach their ends.
Inputs may be any that keep to these rules, and one draw needn't show every extreme that they name: `boundary`: 1 marks the first token of a document; position 0 of every stream holds 0; in every draw one stream holds no 1 at all.
All inputs are finite; a program needn't handle non-finite values.
Results may differ from the reference program's by a relative error of at most 0.007.
Values may be sent and summed in bfloat16 or wider, within the bound.
No kernel may reach another device: no remote copies, remote signals or barrier semaphores. Data moves between devices by JAX's collectives and lax.ppermute only.
A program may use at most 640 MiB of HBM per device.

```python
import math
import jax
import jax.numpy as jnp
from jax import lax

D = 2304
TOK_DEV = 512
STEP = 10
LENGTH = 4096
STREAMS = 4
GATES = 6912
N_SEQ = 8
N_STREAM = 4


def moment_unit():
    return (6.0 * D * D + 3.0 * D) ** (-0.5)


def draw_inputs(key, part):
    key = jax.random.fold_in(key, 1)
    channel = jnp.arange(D) // (D // (N_SEQ * N_STREAM))
    along_seq = (channel // N_STREAM).astype(jnp.float32) / max(N_SEQ - 1, 1)
    along_stream = (channel % N_STREAM).astype(jnp.float32) / max(N_STREAM - 1, 1)
    growth = 2.0
    noise = jnp.clip(jax.random.normal(key, (STREAMS, LENGTH, D), jnp.float32), -6.0, 6.0)
    scales = jnp.sqrt((1.0 + growth * along_seq) * (1.0 + growth * along_stream)) / (1.0 + growth / 2.0)
    return (noise * scales).astype(jnp.bfloat16)


def draw_boundary(key, part):
    key = jax.random.fold_in(key, 2)
    key_whole, key_marks = jax.random.split(key)
    whole = jax.random.randint(key_whole, (), 0, STREAMS)
    marks = (jax.random.randint(key_marks, (STREAMS, LENGTH), 0, 2 * TOK_DEV) == 0).astype(jnp.int32)
    stream_ids = jnp.arange(STREAMS)[:, None]
    position = jnp.arange(LENGTH)[None, :]
    marks = jnp.where(position == 0, 0, marks)
    marks = jnp.where(stream_ids == whole, 0, marks)
    forced = (stream_ids == (whole + 1) % STREAMS) & (position == LENGTH // 2)
    return jnp.where(forced, 1, marks).astype(jnp.int32)


def draw_gate_bias(key, part):
    key = jax.random.fold_in(key, 3)
    key_outer, key_forget = jax.random.split(key)
    outer = 0.7 * jnp.clip(jax.random.normal(key_outer, (2, D), jnp.float32), -3.0, 3.0)
    lower = math.log(30.0)
    upper = math.log(4.0 * LENGTH)
    spans = jax.random.uniform(key_forget, (D,), jnp.float32, lower, upper)
    forget_bias = jnp.log(jnp.exp(spans) - 1.0) - 6.0
    return jnp.concatenate([outer[0], forget_bias, outer[1]]).astype(jnp.float32)


def first_moment(key, shape):
    noise = jnp.clip(jax.random.normal(key, shape, jnp.float32), -4.0, 4.0)
    return (0.111 * moment_unit() * noise).astype(jnp.float32)


def second_moment(key, shape):
    factor = jnp.exp(jax.random.uniform(key, shape, jnp.float32, 0.0, math.log(4.0)))
    return (0.0526 * moment_unit() * moment_unit() * factor).astype(jnp.float32)


def draw_first_weight(key, part):
    key = jax.random.fold_in(key, 4)
    return first_moment(key, (2, D, GATES))


def draw_second_weight(key, part):
    key = jax.random.fold_in(key, 5)
    return second_moment(key, (2, D, GATES))


def draw_first_bias(key, part):
    key = jax.random.fold_in(key, 6)
    return first_moment(key, (GATES,))


def draw_second_bias(key, part):
    key = jax.random.fold_in(key, 7)
    return second_moment(key, (GATES,))


def level_of(key, extent, shards, least, high):
    def one(dim, blocks):
        draws = jax.random.uniform(jax.random.fold_in(jax.random.fold_in(key, 6), dim), (blocks,), jnp.float32, least / len(shards), high / len(shards))
        return jnp.repeat(jnp.exp(draws), extent[dim] // blocks).reshape((-1,) + (1,) * (len(extent) - dim - 1))

    factor_of = one(*shards[0])
    for cut in shards[1:]:
        factor_of = factor_of * one(*cut)
    return factor_of


def centred(stream_key, dims, scale, limit, cuts=(), held_as=jnp.bfloat16):
    values = scale * jax.random.normal(stream_key, dims, jnp.float32)
    if cuts:
        values = values * level_of(stream_key, dims, cuts, -0.22, 0.18)
    return jnp.clip(values, -limit, limit).astype(held_as)


def setup_inputs(seed: int = 0) -> dict:
    arg_keys = jax.random.split(jax.random.key(seed), 12)
    return {
        "inputs": draw_inputs(jax.random.fold_in(arg_keys[11], 71), 0),
        "boundary": draw_boundary(jax.random.fold_in(arg_keys[11], 71), 0),
        "start_state": centred(arg_keys[2], (STREAMS, D), 0.5, 3.0, ((0, 4),), jnp.float32),
        "weight": centred(arg_keys[3], (2, D, GATES), (2 * D) ** -0.5, 0.09375, ((1, 32),), jnp.float32),
        "gate_bias": draw_gate_bias(jax.random.fold_in(arg_keys[11], 71), 0),
        "first_weight": draw_first_weight(jax.random.fold_in(arg_keys[11], 71), 0),
        "second_weight": draw_second_weight(jax.random.fold_in(arg_keys[11], 71), 0),
        "first_bias": draw_first_bias(jax.random.fold_in(arg_keys[11], 71), 0),
        "second_bias": draw_second_bias(jax.random.fold_in(arg_keys[11], 71), 0),
        "cotangent": centred(arg_keys[9], (STREAMS, LENGTH, D), 1.0, 6.0, ((0, 4), (1, 8))),
        "final_cotangent": centred(arg_keys[10], (STREAMS, D), 1.0, 6.0, ((0, 4),), jnp.float32),
    }


@jax.custom_vjp
def low(v):
    return lax.optimization_barrier(v.astype(jnp.bfloat16)).astype(jnp.float32)

@jax.custom_vjp
def low_back(v):
    return v

def low_keep(v):
    return (low(v), None)

def low_pass(kept, grad):
    return (grad,)

def back_keep(v):
    return (v, None)

def back_low(kept, grad):
    return (low(grad),)
low.defvjp(low_keep, low_pass)
low_back.defvjp(back_keep, back_low)
BETA_ONE = 0.9
BETA_TWO = 0.95
EPSILON = 1e-08
RATE_WEIGHT = 0.01
RATE_BIAS = 1.0
DECAY_RATE = 0.1
CLIP_NORM = 1.0
FORGET_SHIFT = 6.0

def advance(carried, summary):
    carried = summary[0] * carried + summary[1]
    return (carried, carried)

def stream_forward(values, matrix, offsets, start_row, keeping):
    model_width = values.shape[1]
    weight_low = low(matrix)
    bias_low = low(offsets)
    previous = jnp.concatenate([jnp.zeros_like(values[:1]), values[:-1]], axis=0) * keeping[:, None]
    gates = jnp.dot(values, weight_low[0], precision=lax.Precision.HIGHEST)
    gates = gates + jnp.dot(previous, weight_low[1], precision=lax.Precision.HIGHEST) + bias_low
    gates = low_back(gates)
    candidate = jnp.tanh(gates[:, :model_width])
    forget = jax.nn.sigmoid(gates[:, model_width:2 * model_width] + FORGET_SHIFT)
    output_gate = jax.nn.sigmoid(gates[:, 2 * model_width:])
    retain = forget * keeping[:, None]
    fresh = (1.0 - forget) * candidate
    final_row, memory = lax.scan(advance, start_row, (retain, fresh))
    return (output_gate * memory, final_row)

def adamw(master, gradient, moment_one, moment_two, rate):
    moment_one = BETA_ONE * moment_one + (1.0 - BETA_ONE) * gradient
    moment_two = BETA_TWO * moment_two + (1.0 - BETA_TWO) * gradient * gradient
    step_size = moment_one / (1.0 - BETA_ONE ** STEP) / (jnp.sqrt(moment_two / (1.0 - BETA_TWO ** STEP)) + EPSILON)
    return (master - rate * (step_size + DECAY_RATE * master), moment_one, moment_two)

def reference(inputs, boundary, start_state, weight, gate_bias, first_weight, second_weight, first_bias, second_bias, cotangent, final_cotangent):
    keeping = (1 - boundary).astype(jnp.float32)

    def per_stream(totals, items):
        stream_in, stream_keep, stream_start, stream_cot, stream_final = items

        def forward(values, matrix, offsets):
            return stream_forward(values, matrix, offsets, stream_start, stream_keep)
        outputs, pullback = jax.vjp(forward, stream_in.astype(jnp.float32), weight, gate_bias)
        grad_values, grad_matrix, grad_offsets = pullback((stream_cot.astype(jnp.float32), stream_final))
        new_totals = (totals[0] + grad_matrix, totals[1] + grad_offsets)
        return (new_totals, (outputs[0].astype(jnp.bfloat16), outputs[1], grad_values.astype(jnp.bfloat16)))
    initial = (jnp.zeros_like(weight), jnp.zeros_like(gate_bias))
    sums, results = lax.scan(per_stream, initial, (inputs, keeping, start_state, cotangent, final_cotangent))
    raw_weight, raw_bias = sums
    hidden, final_state, input_gradient = results
    gradient_norm = jnp.sqrt(jnp.sum(raw_weight * raw_weight) + jnp.sum(raw_bias * raw_bias))
    clip_factor = jnp.minimum(1.0, CLIP_NORM / (gradient_norm + 1e-06))
    weight_gradient = clip_factor * raw_weight
    bias_gradient = clip_factor * raw_bias
    new_weight, new_first_weight, new_second_weight = adamw(weight, weight_gradient, first_weight, second_weight, RATE_WEIGHT)
    new_bias, new_first_bias, new_second_bias = adamw(gate_bias, bias_gradient, first_bias, second_bias, RATE_BIAS)
    return (hidden, final_state, input_gradient, weight_gradient, bias_gradient, gradient_norm, new_weight, new_first_weight, new_second_weight, new_bias, new_first_bias, new_second_bias)
```

```python
import functools
import jax
import jax.numpy as jnp
from jax import lax
from jax.experimental import pallas as pl
from jax.experimental.pallas import tpu as pltpu
from jax.sharding import PartitionSpec as P

STEP = 10
BETA_ONE = 0.9
BETA_TWO = 0.95
EPSILON = 1e-08
RATE_WEIGHT = 0.01
RATE_BIAS = 1.0
DECAY_RATE = 0.1
CLIP_NORM = 1.0
FORGET_SHIFT = 6.0

AXES = ("seq", "stream")
LANES = 128
MEMBERS = 8
HEAD = 16
EDGE = HEAD - 1
BF16 = jnp.bfloat16
F32 = jnp.float32
VMEM_LIMIT = 60 * 1024 * 1024


def params():
    return pltpu.CompilerParams(vmem_limit_bytes=VMEM_LIMIT)


def in_vmem(count):
    return [pl.BlockSpec(memory_space=pltpu.VMEM)] * count


def dot_f32(a, b, dims):
    return lax.dot_general(a, b, (dims, ((), ())), preferred_element_type=F32)


class Place:
    def __init__(self):
        self.n_seq = lax.axis_size("seq")
        self.n_stream = lax.axis_size("stream")
        self.depth = self.n_seq // 2
        self.wide = self.n_stream // 4
        self.count = self.n_seq * self.n_stream
        self.seq = lax.axis_index("seq")
        self.stream = lax.axis_index("stream")
        self.linear = self.seq * self.n_stream + self.stream
        self.member = (self.seq % 2) * 4 + self.stream % 4
        self.high = self.seq // 2
        self.group_bits = [1, 2, self.n_stream]
        self.deep_bits = [self.n_stream * (2 << b) for b in range(self.depth.bit_length() - 1)]
        self.wide_bits = [4 << b for b in range(self.wide.bit_length() - 1)]

    def flip(self, block, mask):
        return lax.ppermute(block, AXES, [(n, n ^ mask) for n in range(self.count)])

    def member_mask(self, p):
        return (p & 3) | ((p >> 2) * self.n_stream)

    def gather_flips(self, block, bits):
        for bit in bits:
            block = jnp.concatenate([block, self.flip(block, bit)], axis=0)
        return block

    def sum_flips(self, value, bits):
        for bit in bits:
            value = value + self.flip(value, bit)
        return value

    def exchange(self, even, odd):
        sibling = self.flip(odd, 1)
        pairs = [jnp.stack([even[i], sibling[i]]) for i in range(4)]
        return [pairs[0]] + [self.flip(pairs[i], self.member_mask(2 * i)) for i in (1, 2, 3)]


def sizes(width):
    whole = width // (MEMBERS * LANES)
    rest = width // MEMBERS - whole * LANES
    assert whole == 2 and 0 < 3 * rest <= LANES and LANES % rest == 0
    return whole, rest


def lane_index(shape):
    return lax.broadcasted_iota(jnp.int32, shape, len(shape) - 1)


def pack_weight_kernel(width, member_ref, weight_ref, even_ref, odd_ref):
    rest = sizes(width)[1]
    taps, rows, _ = weight_ref.shape
    per_tile = LANES // rest
    lane = lane_index((rows, LANES))
    for p in range(MEMBERS):
        out = (even_ref, odd_ref)[p % 2]
        to = member_ref[0] ^ p
        column = 0
        for tile in range(2):
            for tap in range(taps):
                for gate in range(3):
                    start = pl.multiple_of(gate * width + (tile * MEMBERS + to) * LANES, LANES)
                    out[p // 2, :, pl.ds(column, LANES)] = weight_ref[tap, :, pl.ds(start, LANES)].astype(BF16)
                    column += LANES
                if tile == 1:
                    mixed = jnp.zeros((rows, LANES), F32)
                    for gate in range(3):
                        start = pl.multiple_of(gate * width + (2 * MEMBERS + to // per_tile) * LANES, LANES)
                        part = weight_ref[tap, :, pl.ds(start, LANES)]
                        part = pltpu.roll(part, lax.rem((gate - to % per_tile) * rest + LANES, LANES), 1)
                        inside = (lane >= gate * rest) & (lane < (gate + 1) * rest)
                        mixed = jnp.where(inside, part, mixed)
                    out[p // 2, :, pl.ds(column, LANES)] = mixed.astype(BF16)
                    column += LANES


def pack_weight(weight, member):
    taps, rows, columns = weight.shape
    shape = jax.ShapeDtypeStruct((4, rows, 14 * LANES), BF16)
    return pl.pallas_call(
        functools.partial(pack_weight_kernel, columns // 3),
        out_shape=(shape, shape),
        in_specs=[pl.BlockSpec(memory_space=pltpu.SMEM)] + in_vmem(1),
        out_specs=tuple(in_vmem(2)),
        compiler_params=params(),
        name="pack_weight",
    )(member, weight)


def place_weight_kernel(split, member_ref, own_ref, y_ref, x_ref, both_ref, first_ref, second_ref):
    for p in range(MEMBERS):
        block = (own_ref, y_ref, x_ref, both_ref)[p // 2][p % 2]
        first_ref[member_ref[0] ^ p] = block[:, :split]
        second_ref[member_ref[0] ^ p] = block[:, split:]


def place_weight(pairs, member, split):
    _, rows, columns = pairs[0].shape
    return pl.pallas_call(
        functools.partial(place_weight_kernel, split),
        out_shape=(
            jax.ShapeDtypeStruct((MEMBERS, rows, split), BF16),
            jax.ShapeDtypeStruct((MEMBERS, rows, columns - split), BF16),
        ),
        in_specs=[pl.BlockSpec(memory_space=pltpu.SMEM)] + in_vmem(4),
        out_specs=tuple(in_vmem(2)),
        compiler_params=params(),
        name="place_weight",
    )(member, *pairs)


def pick_gradient_kernel(member_ref, first_ref, second_ref, even_ref, odd_ref):
    split = first_ref.shape[-1]
    for p in range(MEMBERS):
        out = (even_ref, odd_ref)[p % 2]
        out[p // 2, :, pl.ds(0, split)] = first_ref[member_ref[0] ^ p]
        out[p // 2, :, pl.ds(split, second_ref.shape[-1])] = second_ref[member_ref[0] ^ p]


def pick_gradient(first, second, member):
    rows = first.shape[1]
    shape = jax.ShapeDtypeStruct((4, rows, first.shape[2] + second.shape[2]), BF16)
    return pl.pallas_call(
        pick_gradient_kernel,
        out_shape=(shape, shape),
        in_specs=[pl.BlockSpec(memory_space=pltpu.SMEM)] + in_vmem(2),
        out_specs=tuple(in_vmem(2)),
        compiler_params=params(),
        name="pick_gradient",
    )(member, first, second)


def place_gradient_kernel(width, member_ref, own_ref, y_ref, x_ref, both_ref, out_ref):
    rest = sizes(width)[1]
    taps, rows, _ = out_ref.shape
    per_tile = LANES // rest
    lane = lane_index((rows, LANES))
    for p in range(MEMBERS):
        block_ref = (own_ref, y_ref, x_ref, both_ref)[p // 2]
        source = member_ref[0] ^ p
        column = 0
        for tile in range(2):
            for tap in range(taps):
                for gate in range(3):
                    start = pl.multiple_of(gate * width + (tile * MEMBERS + source) * LANES, LANES)
                    out_ref[tap, :, pl.ds(start, LANES)] = block_ref[p % 2, :, pl.ds(column, LANES)].astype(F32)
                    column += LANES
                if tile == 1:
                    mixed = block_ref[p % 2, :, pl.ds(column, LANES)].astype(F32)
                    column += LANES
                    for gate in range(3):
                        start = pl.multiple_of(gate * width + (2 * MEMBERS + source // per_tile) * LANES, LANES)
                        first = (source % per_tile) * rest
                        part = pltpu.roll(mixed, lax.rem(first - gate * rest + LANES, LANES), 1)
                        inside = (lane >= first) & (lane < first + rest)
                        old = out_ref[tap, :, pl.ds(start, LANES)]
                        out_ref[tap, :, pl.ds(start, LANES)] = jnp.where(inside, part, old)


def place_gradient(pairs, member, shape):
    return pl.pallas_call(
        functools.partial(place_gradient_kernel, shape[2] // 3),
        out_shape=jax.ShapeDtypeStruct(shape, F32),
        in_specs=[pl.BlockSpec(memory_space=pltpu.SMEM)] + in_vmem(4),
        out_specs=pl.BlockSpec(memory_space=pltpu.VMEM),
        compiler_params=params(),
        name="place_gradient",
    )(member, *pairs)


def pack_channels_kernel(width, member_ref, values_ref, even_ref, odd_ref):
    rest = sizes(width)[1]
    per_tile = LANES // rest
    for p in range(MEMBERS):
        out = (even_ref, odd_ref)[p % 2]
        to = member_ref[0] ^ p
        for tile in range(2):
            start = pl.multiple_of((tile * MEMBERS + to) * LANES, LANES)
            out[p // 2, :, pl.ds(tile * LANES, LANES)] = values_ref[:, pl.ds(start, LANES)]
        start = pl.multiple_of((2 * MEMBERS + to // per_tile) * LANES, LANES)
        part = values_ref[:, pl.ds(start, LANES)].astype(F32)
        part = pltpu.roll(part, lax.rem(LANES - (to % per_tile) * rest, LANES), 1)
        out[p // 2, :, pl.ds(2 * LANES, LANES)] = part.astype(BF16)


def pack_channels(values, member):
    rows, width = values.shape
    shape = jax.ShapeDtypeStruct((4, rows, 3 * LANES), BF16)
    return pl.pallas_call(
        functools.partial(pack_channels_kernel, width),
        out_shape=(shape, shape),
        in_specs=[pl.BlockSpec(memory_space=pltpu.SMEM)] + in_vmem(1),
        out_specs=tuple(in_vmem(2)),
        compiler_params=params(),
        name="pack_channels",
    )(member, values)


def place_channels_kernel(width, member_ref, own_ref, y_ref, x_ref, both_ref, out_ref):
    rest = sizes(width)[1]
    rows, _ = out_ref.shape
    per_tile = LANES // rest
    lane = lane_index((rows, LANES))
    for p in range(MEMBERS):
        block_ref = (own_ref, y_ref, x_ref, both_ref)[p // 2]
        source = member_ref[0] ^ p
        for tile in range(2):
            start = pl.multiple_of((tile * MEMBERS + source) * LANES, LANES)
            out_ref[:, pl.ds(start, LANES)] = block_ref[p % 2, :, pl.ds(tile * LANES, LANES)]
        start = pl.multiple_of((2 * MEMBERS + source // per_tile) * LANES, LANES)
        first = (source % per_tile) * rest
        part = pltpu.roll(block_ref[p % 2, :, pl.ds(2 * LANES, LANES)].astype(F32), first, 1)
        inside = (lane >= first) & (lane < first + rest)
        old = out_ref[:, pl.ds(start, LANES)].astype(F32)
        out_ref[:, pl.ds(start, LANES)] = jnp.where(inside, part, old).astype(BF16)


def place_channels(pairs, member, width):
    return pl.pallas_call(
        functools.partial(place_channels_kernel, width),
        out_shape=jax.ShapeDtypeStruct((pairs[0].shape[1], width), BF16),
        in_specs=[pl.BlockSpec(memory_space=pltpu.SMEM)] + in_vmem(4),
        out_specs=pl.BlockSpec(memory_space=pltpu.VMEM),
        compiler_params=params(),
        name="place_channels",
    )(member, *pairs)


def row_block(rows):
    for block in (176, 48, 16):
        if rows % block == 0:
            return block
    return rows


def tile_columns(tiles, taps_first):
    return 3 * LANES if tiles == 1 else 4 * LANES


def forward_kernel(tiles, rest, x_ref, w_ref, bias_ref, keep_ref, cot_ref, act_ref, sum_ref, both, cot_f32, carry, before):
    step = pl.program_id(0)
    block = x_ref.shape[1]
    rows = MEMBERS * block
    half = w_ref.shape[1] // 2
    lane = lane_index((MEMBERS, LANES))

    x = x_ref[...].reshape(rows, x_ref.shape[2])

    def multiply(i, _):
        at = pl.ds(pl.multiple_of(i * 256, 256), 256)
        result = dot_f32(x, w_ref[:, at], ((1,), (0,)))
        both[2 * i] = result[:, :LANES]
        both[2 * i + 1] = result[:, LANES:]
        return 0

    lax.fori_loop(0, w_ref.shape[1] // 256, multiply, 0)
    for tile in range(tiles):
        cot_f32[tile] = cot_ref[:, :, pl.ds(tile * LANES, LANES)].reshape(rows, LANES).astype(F32)
    count = half // LANES

    @pl.when(step == 0)
    def _():
        for tile in range(tiles):
            carry[3 * tile] = jnp.ones((MEMBERS, LANES), F32)
            carry[3 * tile + 1] = jnp.zeros((MEMBERS, LANES), F32)
            carry[3 * tile + 2] = jnp.zeros((MEMBERS, LANES), F32)
        for i in range(count):
            before[i] = both[count + i, pl.ds(EDGE, MEMBERS, stride=block), :]

    act = act_ref

    def token(k, state):
        sums, earlier = state
        rows_at = pl.ds(k, MEMBERS, stride=block)
        keep = keep_ref[k]
        later = tuple(both[count + i, rows_at, :] for i in range(count))
        gates = [
            both[i, rows_at, :] + keep * earlier[i] + bias_ref[:, pl.ds(i * LANES, LANES)]
            for i in range(count)
        ]
        new = []
        outs = []
        for tile in range(tiles):
            at = lambda g: gates[3 * tile + g]
            if tile == 0:
                z = jnp.tanh(at(0))
                u = 1.0 / (1.0 + jnp.exp(at(1) + FORGET_SHIFT))
                o = 1.0 / (1.0 + jnp.exp(-at(2)))
                outs += [z, u, o]
            else:
                mixed = at(0)
                z = jnp.tanh(mixed)
                s = 1.0 / (1.0 + jnp.exp(jnp.where(lane < 2 * rest, mixed + FORGET_SHIFT, -mixed)))
                outs += [jnp.where(lane < rest, z, s)]
                u = pltpu.roll(s, LANES - rest, 1)
                o = pltpu.roll(s, LANES - 2 * rest, 1)
            a = keep * (1.0 - u)
            total, local, back = sums[3 * tile : 3 * tile + 3]
            cot = cot_f32[tile, rows_at, :]
            total = total * a
            new += [total, a * local + u * z, back + total * (cot * o)]
        for i, value in enumerate(outs):
            act[k, :, pl.ds(i * LANES, LANES)] = value
        return tuple(new), later

    start = (tuple(carry[i] for i in range(3 * tiles)), tuple(before[i] for i in range(count)))
    low = jnp.where(step == 0, HEAD, 0)
    sums, earlier = lax.fori_loop(low, block, token, start)
    for i in range(3 * tiles):
        carry[i] = sums[i]
        sum_ref[i] = sums[i]
    for i in range(count):
        before[i] = earlier[i]


def forward(x, w, bias, keep, cot, tiles, rest):
    members, length, width = x.shape
    block = row_block(length)
    half = w.shape[1] // 2
    lanes = cot.shape[2]
    return pl.pallas_call(
        functools.partial(forward_kernel, tiles, rest),
        grid=(length // block,),
        out_shape=(
            jax.ShapeDtypeStruct((length, members, half), F32),
            jax.ShapeDtypeStruct((3 * tiles, members, LANES), F32),
        ),
        in_specs=[
            pl.BlockSpec((members, block, width), lambda i: (0, i, 0)),
            pl.BlockSpec(memory_space=pltpu.VMEM),
            pl.BlockSpec(memory_space=pltpu.VMEM),
            pl.BlockSpec((block, members, LANES), lambda i: (i, 0, 0)),
            pl.BlockSpec((members, block, lanes), lambda i: (0, i, 0)),
        ],
        out_specs=(
            pl.BlockSpec((block, members, half), lambda i: (i, 0, 0)),
            pl.BlockSpec((3 * tiles, members, LANES), lambda i: (0, 0, 0)),
        ),
        scratch_shapes=[
            pltpu.VMEM((2 * half // LANES, members * block, LANES), F32),
            pltpu.VMEM((tiles, members * block, LANES), F32),
            pltpu.VMEM((3 * tiles, members, LANES), F32),
            pltpu.VMEM((half // LANES, members, LANES), F32),
        ],
        compiler_params=params(),
        cost_estimate=pl.CostEstimate(
            flops=4 * members * length * width * half,
            bytes_accessed=2 * x.size + 2 * w.size + 4 * members * length * half,
            transcendentals=members * length * half,
        ),
        name="forward",
    )(x, w, bias, keep, cot)


def backward_kernel(
    tiles, rest, blocks, act_ref, keep_ref, cot_ref, enter_ref, arrive_ref, final_ref,
    hidden_ref, grads_ref, bias_ref, memory, cot_f32, wide, hold, carry, after,
):
    step = pl.program_id(0)
    block = act_ref.shape[0]
    half = act_ref.shape[2]
    rows = MEMBERS * block
    lane = lane_index((MEMBERS, LANES))
    which = jnp.where(step < blocks, step, 2 * blocks - 1 - step)
    base = which * block
    for tile in range(tiles):
        cot_f32[tile] = cot_ref[:, :, pl.ds(tile * LANES, LANES)].reshape(rows, LANES).astype(F32)
    count = half // LANES
    low = jnp.where(which == 0, HEAD, 0)

    def values(k, tile):
        at = lambda i: act_ref[k, :, pl.ds(i * LANES, LANES)]
        if tile == 0:
            return at(0), at(1), at(2)
        mixed = at(3)
        return mixed, pltpu.roll(mixed, LANES - rest, 1), pltpu.roll(mixed, LANES - 2 * rest, 1)

    @pl.when(step == 0)
    def _():
        for tile in range(tiles):
            memory[EDGE, tile] = enter_ref[tile]
            carry[tile] = enter_ref[tile]

    @pl.when(step < blocks)
    def _():
        def token(k, state):
            keep = keep_ref[k]
            new = []
            for tile in range(tiles):
                z, u, o = values(k, tile)
                m = keep * (1.0 - u) * state[tile] + u * z
                memory[base + k, tile] = m
                hold[tile, pl.ds(k, MEMBERS, stride=block), :] = o * m
                new.append(m)
            return tuple(new)

        state = lax.fori_loop(low, block, token, tuple(carry[t] for t in range(tiles)))
        for tile in range(tiles):
            carry[tile] = state[tile]

        @pl.when(step == 0)
        def _():
            for tile in range(tiles):
                rest_of = final_ref[tile]
                for row in range(3):
                    part = rest_of.astype(BF16).astype(F32)
                    hold[tile, pl.ds(row, MEMBERS, stride=block), :] = part
                    rest_of = rest_of - part
                for row in range(3, HEAD):
                    hold[tile, pl.ds(row, MEMBERS, stride=block), :] = jnp.zeros_like(part)

        for tile in range(tiles):
            hidden_ref[:, :, pl.ds(tile * LANES, LANES)] = hold[tile].astype(BF16).reshape(MEMBERS, block, LANES)

    @pl.when(step == blocks)
    def _():
        for tile in range(tiles):
            carry[tile] = arrive_ref[tile]
        after[...] = jnp.zeros_like(after)
        bias_ref[...] = jnp.zeros_like(bias_ref)

    @pl.when(step >= blocks)
    def _():
        def token(i, state):
            k = block - 1 - i
            arriving, shifted, totals = state
            rows_at = pl.ds(k, MEMBERS, stride=block)
            keep = keep_ref[k]
            new, parts = [], []
            for tile in range(tiles):
                z, u, o = values(k, tile)
                f = 1.0 - u
                cot = cot_f32[tile, rows_at, :]
                held = keep * memory[base + k - 1, tile]
                m = memory[base + k, tile]
                grad = cot * o
                adjoint = grad + arriving[tile]
                new.append(keep * f * adjoint)
                scaled = adjoint * u
                one = [scaled * (1.0 - z * z), scaled * (held - z) * f, grad * m * (1.0 - o)]
                if tile == 1:
                    one = [
                        jnp.where(lane < rest, one[0], jnp.where(lane < 2 * rest, pltpu.roll(one[1], rest, 1), jnp.where(lane < 3 * rest, pltpu.roll(one[2], 2 * rest, 1), 0.0)))
                    ]
                parts += one
            for i, part in enumerate(parts):
                wide[i, rows_at, :] = part
                wide[count + i, rows_at, :] = shifted[i]
            return tuple(new), tuple(keep * part for part in parts), tuple(t + p for t, p in zip(totals, parts))

        state = (
            tuple(carry[t] for t in range(tiles)),
            tuple(after[i] for i in range(count)),
            tuple(bias_ref[:, pl.ds(i * LANES, LANES)] for i in range(count)),
        )
        arriving, shifted, totals = lax.fori_loop(0, block - low, token, state)
        for tile in range(tiles):
            carry[tile] = arriving[tile]
        for i in range(count):
            after[i] = shifted[i]
            bias_ref[:, pl.ds(i * LANES, LANES)] = totals[i]

        @pl.when(which == 0)
        def _():
            for row in range(HEAD):
                for i in range(2 * count):
                    wide[i, pl.ds(row, MEMBERS, stride=block), :] = jnp.zeros((MEMBERS, LANES), F32)
            for i in range(count):
                wide[count + i, pl.ds(EDGE, MEMBERS, stride=block), :] = shifted[i]

        for i in range(2 * count):
            grads_ref[:, :, pl.ds(i * LANES, LANES)] = wide[i].astype(BF16).reshape(MEMBERS, block, LANES)


def backward(act, keep, cot, enter, arrive, final, tiles, rest):
    length, members, half = act.shape
    block = row_block(length)
    blocks = length // block
    lanes = cot.shape[2]
    turn = lambda i: jnp.where(i < blocks, i, 2 * blocks - 1 - i)
    return pl.pallas_call(
        functools.partial(backward_kernel, tiles, rest, blocks),
        grid=(2 * blocks,),
        out_shape=(
            jax.ShapeDtypeStruct((members, length, lanes), BF16),
            jax.ShapeDtypeStruct((members, length, 2 * half), BF16),
            jax.ShapeDtypeStruct((members, half), F32),
        ),
        in_specs=[
            pl.BlockSpec((block, members, half), lambda i: (turn(i), 0, 0)),
            pl.BlockSpec((block, members, LANES), lambda i: (turn(i), 0, 0)),
            pl.BlockSpec((members, block, lanes), lambda i: (0, turn(i), 0)),
            *in_vmem(3),
        ],
        out_specs=(
            pl.BlockSpec((members, block, lanes), lambda i: (0, jnp.minimum(i, blocks - 1), 0)),
            pl.BlockSpec((members, block, 2 * half), lambda i: (0, jnp.minimum(2 * blocks - 1 - i, blocks - 1), 0)),
            pl.BlockSpec((members, half), lambda i: (0, 0)),
        ),
        scratch_shapes=[
            pltpu.VMEM((length, tiles, members, LANES), F32),
            pltpu.VMEM((tiles, members * block, LANES), F32),
            pltpu.VMEM((2 * half // LANES, members * block, LANES), F32),
            pltpu.VMEM((tiles, members * block, LANES), F32),
            pltpu.VMEM((tiles, members, LANES), F32),
            pltpu.VMEM((half // LANES, members, LANES), F32),
        ],
        compiler_params=params(),
        cost_estimate=pl.CostEstimate(
            flops=60 * members * length * half,
            bytes_accessed=8 * act.size + 4 * members * length * half,
            transcendentals=0,
        ),
        name="backward",
    )(act, keep, cot, enter, arrive, final)


def adamw(master, gradient, moment_one, moment_two, rate):
    moment_one = BETA_ONE * moment_one + (1.0 - BETA_ONE) * gradient
    moment_two = BETA_TWO * moment_two + (1.0 - BETA_TWO) * gradient * gradient
    step_size = (
        moment_one
        / (1.0 - BETA_ONE**STEP)
        / (jnp.sqrt(moment_two / (1.0 - BETA_TWO**STEP)) + EPSILON)
    )
    return (master - rate * (step_size + DECAY_RATE * master), moment_one, moment_two)


def three_parts(value):
    parts = []
    for _ in range(3):
        part = lax.reduce_precision(value, 8, 7)
        parts.append(part.astype(BF16))
        value = value - part
    return parts


def channel_tiles(vector, member, rest):
    width = vector.shape[-1]
    axis = vector.ndim - 1
    pieces = [
        lax.dynamic_slice_in_dim(vector, member * LANES, LANES, axis),
        lax.dynamic_slice_in_dim(vector, (MEMBERS + member) * LANES, LANES, axis),
        lax.dynamic_slice_in_dim(vector, 2 * MEMBERS * LANES + member * rest, rest, axis),
    ]
    return pieces


def widen(part):
    return jnp.pad(part, [(0, 0)] * (part.ndim - 1) + [(0, LANES - part.shape[-1])])


def on_device(
    inputs,
    boundary,
    start_state,
    weight,
    gate_bias,
    first_weight,
    second_weight,
    first_bias,
    second_bias,
    cotangent,
    final_cotangent,
):
    here = Place()
    tokens, width = inputs.shape[1:]
    rest = sizes(width)[1]
    member = here.member.astype(jnp.int32).reshape(1)
    taps, own_rows, columns = weight.shape
    split = 6 * LANES
    group_rows = MEMBERS * own_rows
    length = HEAD + tokens
    deep_groups = [[lo + 2 * h for h in range(here.depth)] for lo in range(2)]
    wide_groups = [[jl + 4 * h for h in range(here.wide)] for jl in range(4)]

    pairs = here.exchange(*pack_weight(weight, member))
    parts = place_weight(pairs, member, split)

    def all_rows(part):
        cols = part.shape[-1]
        if here.wide > 1:
            part = lax.all_gather(part, "stream", axis=0, axis_index_groups=wide_groups)
            part = part.reshape(here.wide, 2, 4 * own_rows, cols).swapaxes(0, 1)
        part = part.reshape(-1, cols)
        return lax.all_gather(part, "seq", axis=0, tiled=True, axis_index_groups=deep_groups)

    weights = [all_rows(part) for part in parts]

    edge = lax.ppermute(inputs[0, -1:, :], "seq", [(i, i + 1) for i in range(here.n_seq - 1)])
    keeping = (1 - boundary[0]).astype(BF16)
    head = jnp.concatenate(
        [jnp.pad(keeping, (0, width - tokens))[None]]
        + [part for part in three_parts(start_state)]
        + [part for part in three_parts(final_cotangent)]
        + [jnp.zeros((HEAD - 8, width), BF16), edge],
        axis=0,
    )
    own = jnp.concatenate([head, inputs[0]], axis=0)
    middle = (length // 32) * 16
    from_y = here.flip(own, here.member_mask(2))
    from_x = here.flip(own, here.member_mask(4))
    both_low = here.flip(from_y[:middle], here.member_mask(4))
    both_high = here.flip(from_x[middle:], here.member_mask(2))
    from_both = jnp.concatenate([both_low, both_high], axis=0)
    mine = [own, from_y, from_x, from_both]
    theirs = [here.flip(piece, 1) for piece in mine]
    x_all = jnp.stack([piece for pair in zip(mine, theirs) for piece in pair])

    cot_own = jnp.concatenate([jnp.zeros((HEAD, width), BF16), cotangent[0]], axis=0)
    cot_all = jnp.concatenate(here.exchange(*pack_channels(cot_own, member)), axis=0)
    cots = [cot_all[:, :, :LANES], cot_all[:, :, LANES:]]

    keep = x_all[:, 0, :tokens].astype(F32).T
    keep = jnp.pad(keep, ((HEAD, 0), (0, 0)))
    keep = jnp.broadcast_to(keep[:, :, None], (length, MEMBERS, LANES))
    head_all = x_all[:, 1:7].astype(F32)
    starts = channel_tiles(head_all[:, 0] + head_all[:, 1] + head_all[:, 2], here.member, rest)
    finals = channel_tiles(head_all[:, 3] + head_all[:, 4] + head_all[:, 5], here.member, rest)
    all_bits = [1 << b for b in range(here.count.bit_length() - 1)]
    bias_all = here.gather_flips(gate_bias.astype(BF16)[None], all_bits)
    order = here.linear ^ jnp.arange(here.count)
    bias_all = jnp.take(bias_all, order, axis=0).astype(F32).reshape(3, width)
    bias_parts = channel_tiles(bias_all, here.member, rest)
    biases = [
        bias_parts[0].reshape(1, 3 * LANES),
        jnp.concatenate([bias_parts[1].reshape(1, 3 * LANES), widen(bias_parts[2].reshape(1, 3 * rest))], axis=1),
    ]
    lower = ((jnp.arange(MEMBERS) >> 2) ^ (here.seq % 2)) == 0

    def both_halves(value):
        other = jnp.concatenate([value[4:], value[:4]], axis=0)
        mask = lower[:, None]
        return jnp.where(mask, value, other), jnp.where(mask, other, value)

    gradients, outs = [], []
    for chunk in range(2):
        tiles = chunk + 1
        act, summary = forward(x_all, weights[chunk], biases[chunk], keep, cots[chunk], tiles, rest)
        every = here.gather_flips(summary[None], here.deep_bits)
        enters, arrives, ends = [], [], []
        for tile in range(tiles):
            where = chunk + tile
            state, back = widen(starts[where]), widen(finals[where])
            enter, arrive = state, back
            for z in range(here.depth):
                part = jnp.take(every, z ^ here.high, axis=0)
                a_low, a_high = both_halves(part[3 * tile])
                b_low, b_high = both_halves(part[3 * tile + 1])
                between = a_low * state + b_low
                enter = jnp.where(z == here.high, jnp.where(lower[:, None], state, between), enter)
                state = a_high * between + b_high
            for z in reversed(range(here.depth)):
                part = jnp.take(every, z ^ here.high, axis=0)
                a_low, a_high = both_halves(part[3 * tile])
                c_low, c_high = both_halves(part[3 * tile + 2])
                between = a_high * back + c_high
                arrive = jnp.where(z == here.high, jnp.where(lower[:, None], between, back), arrive)
                back = a_low * between + c_low
            enters.append(enter)
            arrives.append(arrive)
            ends.append(state)
        hidden, grads, bias_grad = backward(
            act, keep, cots[chunk], jnp.stack(enters), jnp.stack(arrives), jnp.stack(ends), tiles, rest
        )
        flat = grads.reshape(MEMBERS * length, -1)
        local = dot_f32(x_all.reshape(MEMBERS * length, width), flat, ((0,), (0,))).astype(BF16)
        cols = local.shape[-1]
        summed = lax.psum_scatter(local, "seq", scatter_dimension=0, tiled=True, axis_index_groups=deep_groups)
        if here.wide > 1:
            summed = summed.reshape(2, here.wide, 4 * own_rows, cols).swapaxes(0, 1).reshape(-1, cols)
            summed = lax.psum_scatter(summed, "stream", scatter_dimension=0, tiled=True, axis_index_groups=wide_groups)
        gradients.append(summed.reshape(MEMBERS, own_rows, cols))
        outs.append((hidden, flat, jnp.sum(bias_grad, axis=0)))

    hidden_all = jnp.concatenate([outs[0][0], outs[1][0]], axis=-1)
    hidden_own = place_channels(here.exchange(hidden_all[0::2], hidden_all[1::2]), member, width)
    hidden = hidden_own[None, HEAD:]
    whole_final = jnp.sum(hidden_own[:3].astype(F32), axis=0, keepdims=True)
    own_columns = width // here.n_seq
    final_state = lax.dynamic_slice_in_dim(whole_final, here.seq * own_columns, own_columns, 1)

    back_all = dot_f32(outs[0][1], weights[0], ((1,), (1,))) + dot_f32(outs[1][1], weights[1], ((1,), (1,)))
    back_all = back_all.astype(BF16).reshape(4, 2, length, width)
    even, odd = back_all[:, 0], back_all[:, 1]
    pair_sum = even.astype(F32) + here.flip(odd, 1).astype(F32)
    sent = pair_sum.astype(BF16)
    input_sum = pair_sum[0]
    for i in (1, 2, 3):
        input_sum = input_sum + here.flip(sent[i], here.member_mask(2 * i)).astype(F32)
    from_next = lax.ppermute(input_sum[EDGE:HEAD], "seq", [(i + 1, i) for i in range(here.n_seq - 1)])
    last = lax.broadcasted_iota(jnp.int32, (tokens, 1), 0) == tokens - 1
    input_gradient = (input_sum[HEAD:] + jnp.where(last, from_next, 0.0)).astype(BF16)[None]

    bias_sum = jnp.concatenate([outs[0][2], outs[1][2]])[None]
    bias_sum = here.sum_flips(bias_sum, here.deep_bits + here.wide_bits)
    bias_squares = jnp.sum(bias_sum * bias_sum)
    bias_every = here.gather_flips(bias_sum, here.group_bits)
    bias_every = jnp.take(bias_every, here.member ^ jnp.arange(MEMBERS), axis=0)
    tile_a = bias_every[:, : 3 * LANES].reshape(MEMBERS, 3, LANES)
    tile_b = bias_every[:, 3 * LANES : 6 * LANES].reshape(MEMBERS, 3, LANES)
    tile_c = bias_every[:, 6 * LANES : 6 * LANES + 3 * rest].reshape(MEMBERS, 3, rest)
    natural = jnp.concatenate([t.swapaxes(0, 1).reshape(3, -1) for t in (tile_a, tile_b, tile_c)], axis=1)
    own_bias = gate_bias.shape[0]
    bias_raw = lax.dynamic_slice_in_dim(natural.reshape(-1), here.linear * own_bias, own_bias, 0)

    squares = sum(jnp.sum(jnp.square(g.astype(F32))) for g in gradients)
    first_plane = (here.high == 0) & (here.stream // 4 == 0)
    squares = squares + jnp.where(first_plane, bias_squares, 0.0)
    squares = here.sum_flips(jnp.broadcast_to(squares, (8, LANES)), all_bits)
    gradient_norm = jnp.sqrt(squares[0, 0])
    clip_factor = jnp.minimum(1.0, CLIP_NORM / (gradient_norm + 1e-06))
    raw = place_gradient(here.exchange(*pick_gradient(*gradients, member)), member, weight.shape)
    weight_gradient = clip_factor * raw
    bias_gradient = clip_factor * bias_raw
    new_weight, new_first_weight, new_second_weight = adamw(
        weight, weight_gradient, first_weight, second_weight, RATE_WEIGHT
    )
    new_bias, new_first_bias, new_second_bias = adamw(
        gate_bias, bias_gradient, first_bias, second_bias, RATE_BIAS
    )
    return (
        hidden,
        final_state,
        input_gradient,
        weight_gradient,
        bias_gradient,
        gradient_norm,
        new_weight,
        new_first_weight,
        new_second_weight,
        new_bias,
        new_first_bias,
        new_second_bias,
    )


def solution(mesh):
    placed = (
        P("stream", "seq", None),
        P("stream", "seq"),
        P("stream", None),
        P(None, ("seq", "stream"), None),
        P(("seq", "stream")),
        P(None, ("seq", "stream"), None),
        P(None, ("seq", "stream"), None),
        P(("seq", "stream")),
        P(("seq", "stream")),
        P("stream", "seq", None),
        P("stream", None),
    )
    return jax.shard_map(
        on_device,
        mesh=mesh,
        in_specs=placed,
        out_specs=(
            P("stream", "seq", None),
            P("stream", "seq"),
            P("stream", "seq", None),
            P(None, ("seq", "stream"), None),
            P(("seq", "stream")),
            P(),
            P(None, ("seq", "stream"), None),
            P(None, ("seq", "stream"), None),
            P(None, ("seq", "stream"), None),
            P(("seq", "stream")),
            P(("seq", "stream")),
            P(("seq", "stream")),
        ),
        check_vma=False,
    )
```

```python
import functools
import jax
import jax.numpy as jnp
from jax import lax
from jax.experimental import pallas as pl
from jax.experimental.pallas import tpu as pltpu
from jax.sharding import PartitionSpec as P

STEP = 10
BETA_ONE = 0.9
BETA_TWO = 0.95
EPSILON = 1e-08
RATE_WEIGHT = 0.01
RATE_BIAS = 1.0
DECAY_RATE = 0.1
CLIP_NORM = 1.0
FORGET_SHIFT = 6.0

AXES = ("seq", "stream")
LANES = 128
MEMBERS = 8
TAIL = 16
BF16 = jnp.bfloat16
F32 = jnp.float32
VMEM_LIMIT = 60 * 1024 * 1024


def params():
    return pltpu.CompilerParams(vmem_limit_bytes=VMEM_LIMIT)


def in_vmem(count):
    return [pl.BlockSpec(memory_space=pltpu.VMEM)] * count


def dot_f32(a, b, dims):
    return lax.dot_general(a, b, (dims, ((), ())), preferred_element_type=F32)


class Place:
    def __init__(self):
        self.n_seq = lax.axis_size("seq")
        self.n_stream = lax.axis_size("stream")
        self.depth = self.n_seq // 2
        self.wide = self.n_stream // 4
        self.count = self.n_seq * self.n_stream
        self.seq = lax.axis_index("seq")
        self.stream = lax.axis_index("stream")
        self.linear = self.seq * self.n_stream + self.stream
        self.member = (self.seq % 2) * 4 + self.stream % 4
        self.high = self.seq // 2
        self.group_bits = [1, 2, self.n_stream]
        self.deep_bits = [self.n_stream * (2 << b) for b in range(self.depth.bit_length() - 1)]
        self.wide_bits = [4 << b for b in range(self.wide.bit_length() - 1)]

    def flip(self, block, mask):
        return lax.ppermute(block, AXES, [(n, n ^ mask) for n in range(self.count)])

    def member_mask(self, p):
        return (p & 3) | ((p >> 2) * self.n_stream)

    def gather_flips(self, block, bits):
        for bit in bits:
            block = jnp.concatenate([block, self.flip(block, bit)], axis=0)
        return block

    def sum_flips(self, value, bits):
        for bit in bits:
            value = value + self.flip(value, bit)
        return value

    def pair_up(self, even, odd):
        sibling = self.flip(odd, 1)
        return [jnp.stack([even[i], sibling[i]]) for i in range(4)]

    def send_pairs(self, pairs):
        return [pairs[0]] + [self.flip(pairs[i], self.member_mask(2 * i)) for i in (1, 2, 3)]

    def exchange(self, even, odd):
        return self.send_pairs(self.pair_up(even, odd))


def after(value, *others):
    return pl.pallas_call(
        lambda *refs: None,
        out_shape=jax.ShapeDtypeStruct(value.shape, value.dtype),
        in_specs=[pl.BlockSpec(memory_space=pl.ANY)] * (1 + len(others)),
        out_specs=pl.BlockSpec(memory_space=pl.ANY),
        input_output_aliases={0: 0},
        name="after",
    )(value, *others)


def copy_kernel(in_ref, out_ref):
    out_ref[...] = in_ref[...]


def copied(value):
    rows, width = value.shape
    spec = pl.BlockSpec((rows // 4, width), lambda i: (i, 0))
    return pl.pallas_call(
        copy_kernel,
        grid=(4,),
        out_shape=jax.ShapeDtypeStruct(value.shape, value.dtype),
        in_specs=[spec],
        out_specs=spec,
        name="copied",
    )(value)


def blank(shape, dtype):
    return pl.pallas_call(
        lambda out_ref: None,
        out_shape=jax.ShapeDtypeStruct(shape, dtype),
        out_specs=pl.BlockSpec(memory_space=pl.ANY),
        name="blank",
    )()


def waiting(kernel, operands, others):
    skip = operands + len(others)
    return lambda *refs: kernel(*refs[:operands], *refs[skip:])


def unseen(others):
    return [pl.BlockSpec(memory_space=pl.ANY)] * len(others)


def sizes(width):
    whole = width // (MEMBERS * LANES)
    rest = width // MEMBERS - whole * LANES
    assert whole == 2 and 0 < 3 * rest <= LANES and LANES % rest == 0
    return whole, rest


def lane_index(shape):
    return lax.broadcasted_iota(jnp.int32, shape, len(shape) - 1)


def pack_weight_kernel(width, member_ref, weight_ref, even_ref, odd_ref):
    rest = sizes(width)[1]
    taps, rows, _ = weight_ref.shape
    per_tile = LANES // rest
    lane = lane_index((rows, LANES))
    for p in range(MEMBERS):
        to = member_ref[0] ^ p
        out = (even_ref, odd_ref)[p % 2]
        column = 0
        for tile in range(2):
            for tap in range(taps):
                for gate in range(3):
                    start = pl.multiple_of(gate * width + (tile * MEMBERS + to) * LANES, LANES)
                    out[p // 2, :, pl.ds(column, LANES)] = weight_ref[tap, :, pl.ds(start, LANES)].astype(BF16)
                    column += LANES
                if tile == 0:
                    mixed = jnp.zeros((rows, LANES), F32)
                    for gate in range(3):
                        start = pl.multiple_of(gate * width + (2 * MEMBERS + to // per_tile) * LANES, LANES)
                        part = weight_ref[tap, :, pl.ds(start, LANES)]
                        part = pltpu.roll(part, lax.rem((gate - to % per_tile) * rest + LANES, LANES), 1)
                        inside = (lane >= gate * rest) & (lane < (gate + 1) * rest)
                        mixed = jnp.where(inside, part, mixed)
                    out[p // 2, :, pl.ds(column, LANES)] = mixed.astype(BF16)
                    column += LANES


def pack_weight(weight, member):
    taps, rows, columns = weight.shape
    shape = jax.ShapeDtypeStruct((4, rows, 14 * LANES), BF16)
    return pl.pallas_call(
        functools.partial(pack_weight_kernel, columns // 3),
        out_shape=(shape, shape),
        in_specs=[pl.BlockSpec(memory_space=pltpu.SMEM)] + in_vmem(1),
        out_specs=tuple(in_vmem(2)),
        compiler_params=params(),
        name="pack_weight",
    )(member, weight)


def place_weight_kernel(split, member_ref, own_ref, y_ref, x_ref, both_ref, first_ref, second_ref):
    for p in range(MEMBERS):
        block = (own_ref, y_ref, x_ref, both_ref)[p // 2][p % 2]
        first_ref[member_ref[0] ^ p] = block[:, :split]
        second_ref[member_ref[0] ^ p] = block[:, split:]


def place_weight(pairs, member, split, *others):
    _, rows, columns = pairs[0].shape
    return pl.pallas_call(
        waiting(functools.partial(place_weight_kernel, split), 5, others),
        out_shape=(
            jax.ShapeDtypeStruct((MEMBERS, rows, split), BF16),
            jax.ShapeDtypeStruct((MEMBERS, rows, columns - split), BF16),
        ),
        in_specs=[pl.BlockSpec(memory_space=pltpu.SMEM)] + in_vmem(4) + unseen(others),
        out_specs=tuple(in_vmem(2)),
        compiler_params=params(),
        name="place_weight",
    )(member, *pairs, *others)


def pick_rows_kernel(member_ref, first_ref, second_ref, even_ref, odd_ref):
    split = first_ref.shape[-1]
    for p in range(MEMBERS):
        out = (even_ref, odd_ref)[p % 2]
        out[p // 2, :, pl.ds(0, split)] = first_ref[member_ref[0] ^ p]
        out[p // 2, :, pl.ds(split, second_ref.shape[-1])] = second_ref[member_ref[0] ^ p]


def pick_rows(first, second, member):
    shape = jax.ShapeDtypeStruct((4, first.shape[1], first.shape[2] + second.shape[2]), BF16)
    return pl.pallas_call(
        pick_rows_kernel,
        out_shape=(shape, shape),
        in_specs=[pl.BlockSpec(memory_space=pltpu.SMEM)] + in_vmem(2),
        out_specs=tuple(in_vmem(2)),
        compiler_params=params(),
        name="pick_rows",
    )(member, first, second)


def place_gradient_kernel(width, member_ref, *refs):
    rest = sizes(width)[1]
    out_ref = refs[4]
    taps, rows, _ = out_ref.shape
    per_tile = LANES // rest
    lane = lane_index((rows, LANES))
    for p in range(MEMBERS):
        source = member_ref[0] ^ p
        block_ref = refs[p // 2]
        column = 0
        for tile in range(2):
            for tap in range(taps):
                for gate in range(3):
                    start = pl.multiple_of(gate * width + (tile * MEMBERS + source) * LANES, LANES)
                    out_ref[tap, :, pl.ds(start, LANES)] = block_ref[p % 2, :, pl.ds(column, LANES)].astype(F32)
                    column += LANES
                if tile == 0:
                    mixed = block_ref[p % 2, :, pl.ds(column, LANES)].astype(F32)
                    column += LANES
                    for gate in range(3):
                        start = pl.multiple_of(gate * width + (2 * MEMBERS + source // per_tile) * LANES, LANES)
                        first = (source % per_tile) * rest
                        part = pltpu.roll(mixed, lax.rem(first - gate * rest + LANES, LANES), 1)
                        inside = (lane >= first) & (lane < first + rest)
                        old = out_ref[tap, :, pl.ds(start, LANES)]
                        out_ref[tap, :, pl.ds(start, LANES)] = jnp.where(inside, part, old)


def place_gradient(pairs, member, shape):
    return pl.pallas_call(
        functools.partial(place_gradient_kernel, shape[2] // 3),
        out_shape=jax.ShapeDtypeStruct(shape, F32),
        in_specs=[pl.BlockSpec(memory_space=pltpu.SMEM)] + in_vmem(4),
        out_specs=pl.BlockSpec(memory_space=pltpu.VMEM),
        compiler_params=params(),
        name="place_gradient",
    )(member, *pairs)


SMALL = 48


def small_rows(width, tokens, biases):
    edge = width // LANES
    keep = edge + tokens // LANES
    bias = keep + -(-biases // LANES)
    return edge, keep, bias, bias + 18


def pack_channels_kernel(width, marks, member_ref, values_ref, small_ref, even_first, odd_first, even_second, odd_second, rows):
    rest = sizes(width)[1]
    per_tile = LANES // rest
    count = values_ref.shape[0]
    tokens = pl.ds(0, count)
    edge, keep, bias, end = marks
    assert end <= SMALL
    for i in range(edge):
        rows[pl.ds(i, 1), :] = small_ref[pl.ds(0, 1), pl.ds(i * LANES, LANES)]
    for i in range(edge, keep):
        rows[pl.ds(i, 1), :] = small_ref[pl.ds(1, 1), pl.ds((i - edge) * LANES, LANES)]
    for i in range(keep, bias):
        rows[pl.ds(i, 1), :] = small_ref[pl.ds(2, 1), pl.ds((i - keep) * LANES, LANES)]
    for i in range(end, SMALL):
        rows[pl.ds(i, 1), :] = jnp.zeros((1, LANES), F32)
    fold = LANES // rest
    folded = pl.ds(count, count // fold)
    lane = lane_index((count // fold, LANES))
    for out in (even_second, odd_second):
        out[:, pl.ds(count, TAIL), :] = jnp.zeros((4, TAIL, LANES), BF16)
    for p in range(MEMBERS):
        first, second = ((even_first, even_second), (odd_first, odd_second))[p % 2]
        to = member_ref[0] ^ p
        for tile, out in enumerate((first, second)):
            start = pl.multiple_of((tile * MEMBERS + to) * LANES, LANES)
            out[p // 2, tokens, pl.ds(0, LANES)] = values_ref[:, pl.ds(start, LANES)]
        start = pl.multiple_of((2 * MEMBERS + to // per_tile) * LANES, LANES)
        part = values_ref[:, pl.ds(start, LANES)].astype(F32)
        total = jnp.zeros((count // fold, LANES), F32)
        for g in range(fold):
            group = pltpu.roll(part[g * (count // fold) : (g + 1) * (count // fold)], lax.rem(LANES + (g - to % per_tile) * rest, LANES), 1)
            total = jnp.where((lane >= g * rest) & (lane < (g + 1) * rest), group, total)
        first[p // 2, folded, :] = total.astype(BF16)
        at = bias
        for vector in (3, 4):
            for tile in range(3):
                start = (tile * MEMBERS + to) * LANES if tile < 2 else (2 * MEMBERS + to // per_tile) * LANES
                value = small_ref[pl.ds(vector, 1), pl.ds(pl.multiple_of(start, LANES), LANES)]
                if tile == 2:
                    value = pltpu.roll(value, lax.rem(LANES - (to % per_tile) * rest, LANES), 1)
                for _ in range(3):
                    piece = value.astype(BF16).astype(F32)
                    rows[pl.ds(at, 1), :] = piece
                    value = value - piece
                    at += 1
        first[p // 2, pl.ds(count + count // fold, SMALL), :] = rows[...].astype(BF16)


def pack_channels(values, small, marks, member, *others):
    rows, width = values.shape
    folded = rows * sizes(width)[1] // LANES
    first = jax.ShapeDtypeStruct((4, rows + folded + SMALL, LANES), BF16)
    second = jax.ShapeDtypeStruct((4, rows + TAIL, LANES), BF16)
    return pl.pallas_call(
        waiting(functools.partial(pack_channels_kernel, width, marks), 3, others),
        out_shape=(first, first, second, second),
        in_specs=[pl.BlockSpec(memory_space=pltpu.SMEM)] + in_vmem(2) + unseen(others),
        out_specs=tuple(in_vmem(4)),
        scratch_shapes=[pltpu.VMEM((SMALL, LANES), F32)],
        compiler_params=params(),
        name="pack_channels",
    )(member, values, small, *others)


def place_channels_kernel(width, member_ref, *refs):
    rest = sizes(width)[1]
    out_ref = refs[8]
    rows, _ = out_ref.shape
    per_tile = LANES // rest
    lane = lane_index((rows, LANES))
    for p in range(MEMBERS):
        source = member_ref[0] ^ p
        for tile in range(2):
            block_ref = refs[4 * tile + p // 2]
            start = pl.multiple_of((tile * MEMBERS + source) * LANES, LANES)
            out_ref[:, pl.ds(start, LANES)] = block_ref[p % 2, :, pl.ds(0, LANES)]
        start = pl.multiple_of((2 * MEMBERS + source // per_tile) * LANES, LANES)
        first = (source % per_tile) * rest
        part = pltpu.roll(refs[p // 2][p % 2, :, pl.ds(LANES, LANES)].astype(F32), first, 1)
        inside = (lane >= first) & (lane < first + rest)
        old = out_ref[:, pl.ds(start, LANES)].astype(F32)
        out_ref[:, pl.ds(start, LANES)] = jnp.where(inside, part, old).astype(BF16)


def place_channels(pairs, member, width):
    return pl.pallas_call(
        functools.partial(place_channels_kernel, width),
        out_shape=jax.ShapeDtypeStruct((pairs[0].shape[1], width), BF16),
        in_specs=[pl.BlockSpec(memory_space=pltpu.SMEM)] + in_vmem(8),
        out_specs=pl.BlockSpec(memory_space=pltpu.VMEM),
        compiler_params=params(),
        name="place_channels",
    )(member, *pairs)


UNROLL = 16


def token_loop(low, high, token, state, reverse):
    def several(i, state):
        for j in range(UNROLL):
            k = high - 1 - (i * UNROLL + j) if reverse else low + i * UNROLL + j
            state = token(k, state)
        return state

    return lax.fori_loop(0, (high - low) // UNROLL, several, state)


def row_block(rows):
    for block in (176, 48, 16):
        if rows % block == 0:
            return block
    return rows


def forward_kernel(tiles, rest, half_steps, *refs):
    gather = half_steps > 0
    x_refs, refs = (refs[:10], refs[10:]) if gather else (refs[:1], refs[1:])
    edge_ref, w_ref, bias_ref, keep_ref, cot_ref, *refs = refs
    if tiles == 2:
        folded_ref, *refs = refs
    act_ref, sum_ref, *refs = refs
    if gather:
        all_ref, *refs = refs
    both, cot_f32, carry, before = refs
    step = pl.program_id(0)
    block = act_ref.shape[0]
    rows = MEMBERS * block
    half = w_ref.shape[1] // 2
    count = half // LANES
    lane = lane_index((MEMBERS, LANES))

    if gather:
        for p in range(6):
            all_ref[p] = x_refs[p][...]

        @pl.when(step < half_steps)
        def _():
            all_ref[6] = x_refs[6][...]
            all_ref[7] = x_refs[7][...]

        @pl.when(step >= half_steps)
        def _():
            all_ref[6] = x_refs[8][...]
            all_ref[7] = x_refs[9][...]

        x = all_ref[...].reshape(rows, all_ref.shape[2])
    else:
        x = x_refs[0][...].reshape(rows, x_refs[0].shape[2])
    result = dot_f32(x, w_ref[...], ((1,), (0,)))
    for i in range(2 * count):
        both[i] = result[:, i * LANES : (i + 1) * LANES]
    cot_f32[0] = cot_ref[...].reshape(rows, LANES).astype(F32)
    if tiles == 2:
        folded = folded_ref[...].reshape(rows, LANES).astype(F32)
        cot_f32[1] = pltpu.roll(folded, lax.rem(LANES - step * rest, LANES), 1)

    @pl.when(step == 0)
    def _():
        for tile in range(tiles):
            carry[3 * tile] = jnp.ones((MEMBERS, LANES), F32)
            carry[3 * tile + 1] = jnp.zeros((MEMBERS, LANES), F32)
            carry[3 * tile + 2] = jnp.zeros((MEMBERS, LANES), F32)
        edges = dot_f32(edge_ref[...], w_ref[:, pl.ds(half, half)], ((1,), (0,)))
        for i in range(count):
            before[i] = edges[:MEMBERS, i * LANES : (i + 1) * LANES]

    def token(k, state):
        sums, earlier = state
        rows_at = pl.ds(k, MEMBERS, stride=block)
        keep = keep_ref[k]
        later = tuple(both[count + i, rows_at, :] for i in range(count))
        gates = [
            both[i, rows_at, :] + keep * earlier[i] + bias_ref[:, pl.ds(i * LANES, LANES)]
            for i in range(count)
        ]
        new = []
        outs = []
        for tile in range(tiles):
            if tile == 0:
                z = jnp.tanh(gates[0])
                u = 1.0 / (1.0 + jnp.exp(gates[1] + FORGET_SHIFT))
                o = 1.0 / (1.0 + jnp.exp(-gates[2]))
                outs += [z, u, o]
            else:
                mixed = gates[3]
                z = jnp.tanh(mixed)
                s = 1.0 / (1.0 + jnp.exp(jnp.where(lane < 2 * rest, mixed + FORGET_SHIFT, -mixed)))
                outs += [jnp.where(lane < rest, z, s)]
                u = pltpu.roll(s, LANES - rest, 1)
                o = pltpu.roll(s, LANES - 2 * rest, 1)
            a = keep * (1.0 - u)
            total, local, back = sums[3 * tile : 3 * tile + 3]
            cot = cot_f32[tile, rows_at, :]
            total = total * a
            new += [total, a * local + u * z, back + total * (cot * o)]
        for i, value in enumerate(outs):
            act_ref[k, :, pl.ds(i * LANES, LANES)] = value
        return tuple(new), later

    start = (tuple(carry[i] for i in range(3 * tiles)), tuple(before[i] for i in range(count)))
    sums, earlier = token_loop(0, block, token, start, False)
    for i in range(3 * tiles):
        carry[i] = sums[i]
        sum_ref[i] = sums[i]
    for i in range(count):
        before[i] = earlier[i]


def forward(pieces, edges, w, bias, keep, cot, tiles, rest, *others):
    gather = len(pieces) > 1
    width = w.shape[0]
    length = keep.shape[0]
    tokens = length - TAIL
    block = tokens // 4
    half = w.shape[1] // 2
    assert LANES // rest == 4
    cot_specs = [pl.BlockSpec((MEMBERS, block, LANES), lambda i: (0, i, 0))]
    if tiles == 2:
        cot_specs += [pl.BlockSpec((MEMBERS, block, LANES), lambda i: (0, 4, 0))]
    if gather:
        x_specs = [pl.BlockSpec((block, width), lambda i: (i, 0))] * 6
        x_specs += [pl.BlockSpec((block, width), lambda i: (jnp.minimum(i, 1), 0))] * 2
        x_specs += [pl.BlockSpec((block, width), lambda i: (jnp.maximum(i - 2, 0), 0))] * 2
    else:
        x_specs = [pl.BlockSpec((MEMBERS, block, width), lambda i: (0, i, 0))]
    whole = [jax.ShapeDtypeStruct((MEMBERS, length, width), BF16)] if gather else []
    return pl.pallas_call(
        waiting(
            functools.partial(forward_kernel, tiles, rest, 2 if gather else 0), len(pieces) + 4 + tiles, others
        ),
        grid=(4,),
        out_shape=(
            jax.ShapeDtypeStruct((length, MEMBERS, half), F32),
            jax.ShapeDtypeStruct((3 * tiles, MEMBERS, LANES), F32),
            *whole,
        ),
        in_specs=[
            *x_specs,
            *in_vmem(3),
            pl.BlockSpec((block, MEMBERS, LANES), lambda i: (i, 0, 0)),
            *cot_specs,
            *unseen(others),
        ],
        out_specs=(
            pl.BlockSpec((block, MEMBERS, half), lambda i: (i, 0, 0)),
            pl.BlockSpec((3 * tiles, MEMBERS, LANES), lambda i: (0, 0, 0)),
            *[pl.BlockSpec((MEMBERS, block, width), lambda i: (0, i, 0)) for _ in whole],
        ),
        scratch_shapes=[
            pltpu.VMEM((2 * half // LANES, MEMBERS * block, LANES), F32),
            pltpu.VMEM((tiles, MEMBERS * block, LANES), F32),
            pltpu.VMEM((3 * tiles, MEMBERS, LANES), F32),
            pltpu.VMEM((half // LANES, MEMBERS, LANES), F32),
        ],
        compiler_params=params(),
        name="forward",
    )(*pieces, edges, w, bias, keep, *[cot] * tiles, *others)


def backward_kernel(
    tiles, rest, blocks, act_ref, keep_ref, enter_ref, arrive_ref, final_ref, cot_ref, folded_ref,
    even_ref, odd_ref, grads_ref, bias_ref, edge_ref, memory, cot_f32, wide, hold, carry, after, unfolded=None,
):
    step = pl.program_id(0)
    block = act_ref.shape[0]
    half = act_ref.shape[2]
    rows = MEMBERS * block
    lane = lane_index((MEMBERS, LANES))
    which = jnp.where(step < blocks, step, 2 * blocks - 1 - step)
    base = which * block
    cot_f32[...] = cot_ref[...].reshape(rows, LANES).astype(F32)
    count = half // LANES
    top = jnp.where(which == blocks - 1, block - TAIL, block)

    def values(k, tile):
        at = lambda i: act_ref[k, :, pl.ds(i * LANES, LANES)]
        if tile == 0:
            return at(0), at(1), at(2)
        mixed = at(3)
        return mixed, pltpu.roll(mixed, LANES - rest, 1), pltpu.roll(mixed, LANES - 2 * rest, 1)

    if tiles == 2:
        long, short = unfolded.shape[0] // MEMBERS, folded_ref.shape[1]

        @pl.when(step == 0)
        def _():
            for p in range(MEMBERS):
                folded = folded_ref[p].astype(F32)
                for g in range(LANES // rest):
                    part = pltpu.roll(folded, LANES - g * rest, 1) if g else folded
                    unfolded[pl.ds(p * long + g * short, short), :] = part

    @pl.when(step == 0)
    def _():
        for tile in range(tiles):
            memory[0, tile] = enter_ref[tile]
            carry[tile] = enter_ref[tile]

    @pl.when(step < blocks)
    def _():
        def token(k, state):
            keep = keep_ref[k]
            new = []
            for tile in range(tiles):
                z, u, o = values(k, tile)
                m = keep * (1.0 - u) * state[tile] + u * z
                memory[base + k + 1, tile] = m
                hold[tile, pl.ds(k, MEMBERS, stride=block), :] = o * m
                new.append(m)
            return tuple(new)

        state = token_loop(0, top, token, tuple(carry[t] for t in range(tiles)), False)
        for tile in range(tiles):
            carry[tile] = state[tile]

        @pl.when(which == blocks - 1)
        def _():
            for tile in range(tiles):
                rest_of = final_ref[tile]
                for row in range(3):
                    part = rest_of.astype(BF16).astype(F32)
                    hold[tile, pl.ds(block - TAIL + row, MEMBERS, stride=block), :] = part
                    rest_of = rest_of - part
                for row in range(3, TAIL):
                    hold[tile, pl.ds(block - TAIL + row, MEMBERS, stride=block), :] = jnp.zeros_like(part)

        for tile in range(tiles):
            for p in range(MEMBERS):
                part = hold[tile, pl.ds(p * block, block), :].astype(BF16)
                (even_ref, odd_ref)[p % 2][p // 2, :, pl.ds(tile * LANES, LANES)] = part

    @pl.when(step == blocks)
    def _():
        for tile in range(tiles):
            carry[tile] = arrive_ref[tile]
        after[...] = jnp.zeros_like(after)
        bias_ref[...] = jnp.zeros_like(bias_ref)

    @pl.when(step >= blocks)
    def _():
        def token(k, state):
            arriving, shifted, totals = state
            rows_at = pl.ds(k, MEMBERS, stride=block)
            keep = keep_ref[k]
            new, parts = [], []
            for tile in range(tiles):
                z, u, o = values(k, tile)
                f = 1.0 - u
                if tile == 0:
                    cot = cot_f32[rows_at, :]
                else:
                    cot = unfolded[pl.ds(base + k, MEMBERS, stride=long), :]
                held = keep * memory[base + k, tile]
                m = memory[base + k + 1, tile]
                grad = cot * o
                adjoint = grad + arriving[tile]
                new.append(keep * f * adjoint)
                scaled = adjoint * u
                one = [scaled * (1.0 - z * z), scaled * (held - z) * f, grad * m * (1.0 - o)]
                if tile == 1:
                    one = [
                        jnp.where(lane < rest, one[0], jnp.where(lane < 2 * rest, pltpu.roll(one[1], rest, 1), jnp.where(lane < 3 * rest, pltpu.roll(one[2], 2 * rest, 1), 0.0)))
                    ]
                parts += one
            for i, part in enumerate(parts):
                wide[i, rows_at, :] = part
                wide[count + i, rows_at, :] = shifted[i]
            return tuple(new), tuple(keep * part for part in parts), tuple(t + p for t, p in zip(totals, parts))

        state = (
            tuple(carry[t] for t in range(tiles)),
            tuple(after[i] for i in range(count)),
            tuple(bias_ref[:, pl.ds(i * LANES, LANES)] for i in range(count)),
        )
        arriving, shifted, totals = token_loop(0, top, token, state, True)
        for tile in range(tiles):
            carry[tile] = arriving[tile]
        for i in range(count):
            after[i] = shifted[i]
            edge_ref[:, pl.ds(i * LANES, LANES)] = shifted[i]
            bias_ref[:, pl.ds(i * LANES, LANES)] = totals[i]

        @pl.when(which == blocks - 1)
        def _():
            for row in range(block - TAIL, block):
                for i in range(2 * count):
                    wide[i, pl.ds(row, MEMBERS, stride=block), :] = jnp.zeros((MEMBERS, LANES), F32)

        for i in range(2 * count):
            grads_ref[:, :, pl.ds(i * LANES, LANES)] = wide[i].astype(BF16).reshape(MEMBERS, block, LANES)


def backward(act, keep, cot, enter, arrive, final, tiles, rest, *others):
    length, members, half = act.shape
    block = row_block(length)
    blocks = length // block
    lanes = tiles * LANES
    turn = lambda i: jnp.where(i < blocks, i, 2 * blocks - 1 - i)
    return pl.pallas_call(
        waiting(functools.partial(backward_kernel, tiles, rest, blocks), 7, others),
        grid=(2 * blocks,),
        out_shape=(
            jax.ShapeDtypeStruct((members // 2, length, lanes), BF16),
            jax.ShapeDtypeStruct((members // 2, length, lanes), BF16),
            jax.ShapeDtypeStruct((members, length, 2 * half), BF16),
            jax.ShapeDtypeStruct((members, half), F32),
            jax.ShapeDtypeStruct((members, half), F32),
        ),
        in_specs=[
            pl.BlockSpec((block, members, half), lambda i: (turn(i), 0, 0)),
            pl.BlockSpec((block, members, LANES), lambda i: (turn(i), 0, 0)),
            *in_vmem(3),
            pl.BlockSpec((members, block, LANES), lambda i: (0, turn(i), 0)),
            pl.BlockSpec((members, (length - TAIL) // 4, LANES), lambda i: (0, 4 if tiles == 2 else 0, 0)),
            *unseen(others),
        ],
        out_specs=(
            pl.BlockSpec((members // 2, block, lanes), lambda i: (0, jnp.minimum(i, blocks - 1), 0)),
            pl.BlockSpec((members // 2, block, lanes), lambda i: (0, jnp.minimum(i, blocks - 1), 0)),
            pl.BlockSpec((members, block, 2 * half), lambda i: (0, jnp.minimum(2 * blocks - 1 - i, blocks - 1), 0)),
            pl.BlockSpec((members, half), lambda i: (0, 0)),
            pl.BlockSpec((members, half), lambda i: (0, 0)),
        ),
        scratch_shapes=[
            pltpu.VMEM((length, tiles, members, LANES), F32),
            pltpu.VMEM((members * block, LANES), F32),
            pltpu.VMEM((2 * half // LANES, members * block, LANES), F32),
            pltpu.VMEM((tiles, members * block, LANES), F32),
            pltpu.VMEM((tiles, members, LANES), F32),
            pltpu.VMEM((half // LANES, members, LANES), F32),
            *[pltpu.VMEM((members * (length - TAIL), LANES), F32) for _ in range(tiles - 1)],
        ],
        compiler_params=params(),
        name="backward",
    )(act, keep, enter, arrive, final, cot, cot, *others)


def input_gradient_kernel(first_ref, second_ref, w_first, w_second, even_ref, odd_ref):
    for p, out in enumerate((even_ref, odd_ref)):
        out[0] = (
            dot_f32(first_ref[p], w_first[...], ((1,), (1,)))
            + dot_f32(second_ref[p], w_second[...], ((1,), (1,)))
        ).astype(BF16)


def input_gradients(first, second, w_first, w_second, start, count, *others):
    _, length, _ = first.shape
    width = w_first.shape[0]
    shape = jax.ShapeDtypeStruct((count, length, width), BF16)
    return pl.pallas_call(
        waiting(input_gradient_kernel, 4, others),
        grid=(count,),
        out_shape=(shape, shape),
        in_specs=[
            pl.BlockSpec((2, length, first.shape[2]), lambda i: (start + i, 0, 0)),
            pl.BlockSpec((2, length, second.shape[2]), lambda i: (start + i, 0, 0)),
            *in_vmem(2),
            *unseen(others),
        ],
        out_specs=(pl.BlockSpec((1, length, width), lambda i: (i, 0, 0)),) * 2,
        compiler_params=params(),
        name="input_gradient",
    )(first, second, w_first, w_second, *others)


def far_sum_kernel(even_ref, odd_ref, low_ref, high_ref):
    total = even_ref[0].astype(F32) + odd_ref[0].astype(F32)
    middle = low_ref.shape[0]
    low_ref[...] = total[:middle].astype(BF16)
    high_ref[...] = total[middle:].astype(BF16)


def far_sum(even, odd, middle):
    _, length, width = even.shape
    block = 384
    sums = [jax.ShapeDtypeStruct((rows, width), BF16) for rows in (middle, length - middle)]
    spec = pl.BlockSpec((1, length, block), lambda i: (0, 0, i))
    return pl.pallas_call(
        far_sum_kernel,
        grid=(width // block,),
        out_shape=sums,
        in_specs=[spec, spec],
        out_specs=[pl.BlockSpec((rows, block), lambda i: (0, i)) for rows in (middle, length - middle)],
        compiler_params=params(),
        name="far_sum",
    )(even, odd)


def near_sums_kernel(even_ref, odd_ref, low_ref, high_ref, to_y, to_x):
    middle = low_ref.shape[0]
    total = even_ref[0].astype(F32) + odd_ref[0].astype(F32)
    to_y[pl.ds(0, middle), :] = (total[:middle] + low_ref[...].astype(F32)).astype(BF16)
    to_y[pl.ds(middle, high_ref.shape[0]), :] = total[middle:].astype(BF16)
    total = even_ref[1].astype(F32) + odd_ref[1].astype(F32)
    to_x[pl.ds(0, middle), :] = total[:middle].astype(BF16)
    to_x[pl.ds(middle, high_ref.shape[0]), :] = (total[middle:] + high_ref[...].astype(F32)).astype(BF16)


def near_sums(even, odd, low, high):
    _, length, width = even.shape
    block = 384
    spec = pl.BlockSpec((2, length, block), lambda i: (0, 0, i))
    out = pl.BlockSpec((length, block), lambda i: (0, i))
    return pl.pallas_call(
        near_sums_kernel,
        grid=(width // block,),
        out_shape=[jax.ShapeDtypeStruct((length, width), BF16)] * 2,
        in_specs=[spec, spec] + [pl.BlockSpec((part.shape[0], block), lambda i: (0, i)) for part in (low, high)],
        out_specs=[out, out],
        compiler_params=params(),
        name="near_sums",
    )(even, odd, low, high)


def adamw(master, gradient, moment_one, moment_two, rate):
    moment_one = BETA_ONE * moment_one + (1.0 - BETA_ONE) * gradient
    moment_two = BETA_TWO * moment_two + (1.0 - BETA_TWO) * gradient * gradient
    step_size = (
        moment_one
        / (1.0 - BETA_ONE**STEP)
        / (jnp.sqrt(moment_two / (1.0 - BETA_TWO**STEP)) + EPSILON)
    )
    return (master - rate * (step_size + DECAY_RATE * master), moment_one, moment_two)


def channel_tiles(vector, member, rest):
    width = vector.shape[-1]
    axis = vector.ndim - 1
    pieces = [
        lax.dynamic_slice_in_dim(vector, member * LANES, LANES, axis),
        lax.dynamic_slice_in_dim(vector, (MEMBERS + member) * LANES, LANES, axis),
        lax.dynamic_slice_in_dim(vector, 2 * MEMBERS * LANES + member * rest, rest, axis),
    ]
    return pieces


def widen(part):
    return jnp.pad(part, [(0, 0)] * (part.ndim - 1) + [(0, LANES - part.shape[-1])])


def on_device(
    inputs,
    boundary,
    start_state,
    weight,
    gate_bias,
    first_weight,
    second_weight,
    first_bias,
    second_bias,
    cotangent,
    final_cotangent,
):
    here = Place()
    tokens, width = inputs.shape[1:]
    rest = sizes(width)[1]
    member = here.member.astype(jnp.int32).reshape(1)
    taps, own_rows, columns = weight.shape
    length = tokens + TAIL
    deep_groups = [[lo + 2 * h for h in range(here.depth)] for lo in range(2)]
    wide_groups = [[jl + 4 * h for h in range(here.wide)] for jl in range(4)]

    weight_pairs = here.pair_up(*pack_weight(weight, member))
    weight_got = here.send_pairs(weight_pairs)

    def all_rows(part):
        cols = part.shape[-1]
        if here.wide > 1:
            part = lax.all_gather(part, "stream", axis=0, axis_index_groups=wide_groups)
            part = part.reshape(here.wide, 2, 4 * own_rows, cols).swapaxes(0, 1)
        part = part.reshape(-1, cols)
        return lax.all_gather(part, "seq", axis=0, tiled=True, axis_index_groups=deep_groups)

    own_bias = gate_bias.shape[0]
    marks = small_rows(width, tokens, own_bias)
    pad_to = lambda row: jnp.pad(row.astype(F32).reshape(1, -1), ((0, 0), (0, width - row.size)))
    small = [inputs[0, -1:].astype(F32), pad_to(1 - boundary[0]), pad_to(gate_bias.astype(BF16))]
    small = jnp.concatenate(small + [start_state, final_cotangent])

    own = inputs[0]
    own_copy = copied(own)
    packed_cot = pack_channels(cotangent[0], small, marks, member, own_copy, weight_pairs[3])
    cot_first, cot_second = here.pair_up(*packed_cot[:2]), here.pair_up(*packed_cot[2:])
    got_first = here.send_pairs(cot_first)
    placed = place_weight(weight_got, member, 8 * LANES, *cot_first[1:])
    weights = [all_rows(part) for part in placed]
    own_sibling = here.flip(own, 1)
    sent = after(own_copy, *placed, *got_first[1:])
    middle = (tokens // 32) * 16
    from_y = here.flip(sent, here.member_mask(2))
    from_x = here.flip(sent, here.member_mask(4))
    low_part, high_part = from_y[:middle], from_x[middle:]
    both_low = here.flip(low_part, here.member_mask(4))
    both_high = here.flip(high_part, here.member_mask(2))
    y_sibling, x_sibling = here.flip(from_y, 1), here.flip(from_x, 1)
    cots = [jnp.concatenate(got_first, axis=0)]
    pieces = [own, own_sibling, from_y, y_sibling, from_x, x_sibling]
    pieces += [both_low, here.flip(both_low, 1), both_high, here.flip(both_high, 1)]

    smalls = cots[0][:, tokens + tokens * rest // LANES :].astype(F32)
    lower = ((jnp.arange(MEMBERS) >> 2) ^ (here.seq % 2)) == 0
    lasts = smalls[:, : marks[0]].reshape(MEMBERS, width).astype(BF16)
    plane = 2 * here.n_stream
    behind = lax.ppermute(lasts, AXES, [(n, n + plane) for n in range(here.count - plane)])
    swap = lambda rows: jnp.concatenate([rows[4:], rows[:4]], axis=0)
    edges = jnp.where(lower[:, None], swap(behind), swap(lasts))
    edges = jnp.pad(edges, ((0, TAIL - MEMBERS), (0, 0)))
    keep = smalls[:, marks[0] : marks[1]].reshape(MEMBERS, tokens).T
    keep = jnp.pad(keep, ((0, TAIL), (0, 0)))
    keep = jnp.broadcast_to(keep[:, :, None], (length, MEMBERS, LANES))
    states = jnp.sum(smalls[:, marks[2] : marks[3]].reshape(MEMBERS, 2, 3, 3, LANES), axis=3)
    starts, finals = ([states[:, i, tile] for tile in range(3)] for i in range(2))
    all_bits = [1 << b for b in range(here.count.bit_length() - 1)]
    bias_all = smalls[:, marks[1] : marks[2]].reshape(1, MEMBERS, -1)[:, :, :own_bias].astype(BF16)
    bias_all = here.gather_flips(bias_all, here.deep_bits + here.wide_bits).astype(F32)
    bias_all = bias_all.reshape(here.wide, here.depth, MEMBERS, own_bias)
    every_member = here.member ^ jnp.arange(MEMBERS)
    bias_all = jnp.take(bias_all, (here.stream // 4) ^ jnp.arange(here.wide), axis=0)
    bias_all = jnp.take(bias_all, here.high ^ jnp.arange(here.depth), axis=1)
    bias_all = jnp.take(bias_all, every_member, axis=2)
    bias_all = bias_all.reshape(here.wide, here.depth, 2, 4, own_bias).transpose(1, 2, 0, 3, 4).reshape(3, width)
    bias_parts = channel_tiles(bias_all, here.member, rest)
    biases = [
        jnp.concatenate([bias_parts[0].reshape(1, 3 * LANES), widen(bias_parts[2].reshape(1, 3 * rest))], axis=1),
        bias_parts[1].reshape(1, 3 * LANES),
    ]

    def both_halves(value):
        other = jnp.concatenate([value[4:], value[:4]], axis=0)
        mask = lower[:, None]
        return jnp.where(mask, value, other), jnp.where(mask, other, value)

    def back_pairs(first, second, start, count, *others):
        even, odd = input_gradients(first, second, weights[0], weights[1], start, count, *others)
        return even, here.flip(odd, 1)

    halfway = (length // 32) * 16
    gradients, outs, hidden_got = [], [], []
    for chunk in range(2):
        tiles = 2 - chunk
        others = (outs[0][4],) if chunk else ()
        source = [x_all] if chunk else pieces
        act, summary, *whole = forward(source, edges, weights[chunk], biases[chunk], keep, cots[chunk], tiles, rest, *others)
        if whole:
            got_second = here.send_pairs([after(pair, summary) for pair in cot_second])
            cots.append(jnp.concatenate(got_second, axis=0))
            behind = jnp.pad(edges[:MEMBERS, None], ((0, 0), (0, TAIL - 1), (0, 0)))
            x_all = lax.dynamic_update_slice(whole[0], behind, (0, tokens, 0))
        every = here.gather_flips(summary[None], here.deep_bits)
        enters, arrives, ends = [], [], []
        for tile in range(tiles):
            where = (0, 2, 1)[2 * chunk + tile]
            state, back = starts[where], finals[where]
            enter, arrive = state, back
            for z in range(here.depth):
                part = jnp.take(every, z ^ here.high, axis=0)
                a_low, a_high = both_halves(part[3 * tile])
                b_low, b_high = both_halves(part[3 * tile + 1])
                between = a_low * state + b_low
                enter = jnp.where(z == here.high, jnp.where(lower[:, None], state, between), enter)
                state = a_high * between + b_high
            for z in reversed(range(here.depth)):
                part = jnp.take(every, z ^ here.high, axis=0)
                a_low, a_high = both_halves(part[3 * tile])
                c_low, c_high = both_halves(part[3 * tile + 2])
                between = a_high * back + c_high
                arrive = jnp.where(z == here.high, jnp.where(lower[:, None], between, back), arrive)
                back = a_low * between + c_low
            enters.append(enter)
            arrives.append(arrive)
            ends.append(state)
        others = () if chunk else (weights[1], cots[1])
        even, odd, grads, bias_grad, edge_grad = backward(
            act, keep, cots[chunk], jnp.stack(enters), jnp.stack(arrives), jnp.stack(ends), tiles, rest, *others
        )
        half = edge_grad.shape[1]
        edge_grad = jnp.pad(edge_grad.astype(BF16)[:, None], ((0, 0), (0, TAIL - 1), (half, 0)))
        grads = lax.dynamic_update_slice(grads, edge_grad, (0, tokens, 0))
        hidden_pairs = here.pair_up(even, odd)
        hidden_got += here.send_pairs(hidden_pairs)
        if chunk == 1:
            far_low, far_high = far_sum(*back_pairs(outs[0][2], grads, 3, 1, *hidden_got[1:4]), halfway)
            grads = after(grads, far_low, gradients[0])
        flat = grads.reshape(MEMBERS * length, -1)
        local = dot_f32(x_all.reshape(MEMBERS * length, width), flat, ((0,), (0,))).astype(BF16)
        cols = local.shape[-1]
        ordered = after(local, gradients[0]) if gradients else local
        summed = lax.psum_scatter(ordered, "seq", scatter_dimension=0, tiled=True, axis_index_groups=deep_groups)
        if here.wide > 1:
            summed = summed.reshape(2, here.wide, 4 * own_rows, cols).swapaxes(0, 1).reshape(-1, cols)
            summed = lax.psum_scatter(summed, "stream", scatter_dimension=0, tiled=True, axis_index_groups=wide_groups)
        gradients.append(summed.reshape(MEMBERS, own_rows, cols))
        outs.append((even, odd, grads, jnp.sum(bias_grad, axis=0), local))

    hidden_own = place_channels(hidden_got, member, width)
    hidden = hidden_own[None, :tokens]
    whole_final = jnp.sum(hidden_own[tokens : tokens + 3].astype(F32), axis=0, keepdims=True)
    own_columns = width // here.n_seq
    final_state = lax.dynamic_slice_in_dim(whole_final, here.seq * own_columns, own_columns, 1)

    low_half = here.flip(far_low, here.member_mask(4))
    high_half = here.flip(far_high, here.member_mask(2))
    grads = outs[0][2], outs[1][2]
    even, odd = back_pairs(*grads, 1, 2, low_half, high_half, outs[1][4], *hidden_got[5:])
    to_y, to_x = near_sums(even, odd, low_half, high_half)
    got_y = here.flip(to_y, here.member_mask(2))
    got_x = here.flip(to_x, here.member_mask(4))
    even, odd = back_pairs(*grads, 0, 1, to_y, to_x)
    gradients = [after(gradient, even, got_y, got_x) for gradient in gradients]
    add_up = lambda rows: sum(part[rows].astype(F32) for part in (even[0], odd[0], got_y, got_x))
    from_next = lax.ppermute(
        add_up(slice(tokens, tokens + 1)), "seq", [(i + 1, i) for i in range(here.n_seq - 1)]
    )
    last = lax.broadcasted_iota(jnp.int32, (tokens, 1), 0) == tokens - 1
    input_gradient = (add_up(slice(0, tokens)) + jnp.where(last, from_next, 0.0)).astype(BF16)[None]

    squares = sum(jnp.sum(jnp.square(g.astype(F32))) for g in gradients)
    vector = jnp.concatenate([outs[0][3], outs[1][3], jnp.broadcast_to(squares, (LANES,))]).reshape(1, -1)
    vector = here.sum_flips(vector, here.deep_bits + here.wide_bits)
    vectors = here.gather_flips(vector, here.group_bits)
    bias_every = jnp.take(vectors[:, :-LANES], every_member, axis=0)
    gradient_norm = jnp.sqrt(jnp.sum(vectors[:, -1]) + jnp.sum(jnp.square(vectors[:, :-LANES])))
    tile_a = bias_every[:, : 3 * LANES].reshape(MEMBERS, 3, LANES)
    tile_b = bias_every[:, 4 * LANES : 7 * LANES].reshape(MEMBERS, 3, LANES)
    tile_c = bias_every[:, 3 * LANES : 3 * LANES + 3 * rest].reshape(MEMBERS, 3, rest)
    natural = jnp.concatenate([t.swapaxes(0, 1).reshape(3, -1) for t in (tile_a, tile_b, tile_c)], axis=1)
    bias_raw = lax.dynamic_slice_in_dim(natural.reshape(-1), here.linear * own_bias, own_bias, 0)

    clip_factor = jnp.minimum(1.0, CLIP_NORM / (gradient_norm + 1e-06))
    received = here.exchange(*pick_rows(*gradients, member))
    raw = place_gradient(received, member, weight.shape)
    weight_gradient = clip_factor * raw
    bias_gradient = clip_factor * bias_raw
    new_weight, new_first_weight, new_second_weight = adamw(
        weight, weight_gradient, first_weight, second_weight, RATE_WEIGHT
    )
    new_bias, new_first_bias, new_second_bias = adamw(
        gate_bias, bias_gradient, first_bias, second_bias, RATE_BIAS
    )
    return (
        hidden,
        final_state,
        input_gradient,
        weight_gradient,
        bias_gradient,
        gradient_norm,
        new_weight,
        new_first_weight,
        new_second_weight,
        new_bias,
        new_first_bias,
        new_second_bias,
    )


def solution(mesh):
    placed = (
        P("stream", "seq", None),
        P("stream", "seq"),
        P("stream", None),
        P(None, ("seq", "stream"), None),
        P(("seq", "stream")),
        P(None, ("seq", "stream"), None),
        P(None, ("seq", "stream"), None),
        P(("seq", "stream")),
        P(("seq", "stream")),
        P("stream", "seq", None),
        P("stream", None),
    )
    return jax.shard_map(
        on_device,
        mesh=mesh,
        in_specs=placed,
        out_specs=(
            P("stream", "seq", None),
            P("stream", "seq"),
            P("stream", "seq", None),
            P(None, ("seq", "stream"), None),
            P(("seq", "stream")),
            P(),
            P(None, ("seq", "stream"), None),
            P(None, ("seq", "stream"), None),
            P(None, ("seq", "stream"), None),
            P(("seq", "stream")),
            P(("seq", "stream")),
            P(("seq", "stream")),
        ),
        check_vma=False,
    )
```

```python
import functools
import jax
import jax.numpy as jnp
from jax import lax
from jax.experimental import pallas as pl
from jax.experimental.pallas import tpu as pltpu
from jax.sharding import PartitionSpec as P

STEP = 10
BETA_ONE = 0.9
BETA_TWO = 0.95
EPSILON = 1e-08
RATE_WEIGHT = 0.01
RATE_BIAS = 1.0
DECAY_RATE = 0.1
CLIP_NORM = 1.0
FORGET_SHIFT = 6.0

AXES = ("seq", "stream")
LANES = 128
MEMBERS = 8
TAIL = 16
BF16 = jnp.bfloat16
F32 = jnp.float32
VMEM_LIMIT = 60 * 1024 * 1024


def params():
    return pltpu.CompilerParams(vmem_limit_bytes=VMEM_LIMIT)


def in_vmem(count):
    return [pl.BlockSpec(memory_space=pltpu.VMEM)] * count


def dot_f32(a, b, dims):
    return lax.dot_general(a, b, (dims, ((), ())), preferred_element_type=F32)


class Place:
    def __init__(self):
        self.n_seq = lax.axis_size("seq")
        self.n_stream = lax.axis_size("stream")
        self.depth = self.n_seq // 2
        self.wide = self.n_stream // 4
        self.count = self.n_seq * self.n_stream
        self.seq = lax.axis_index("seq")
        self.stream = lax.axis_index("stream")
        self.linear = self.seq * self.n_stream + self.stream
        self.member = (self.seq % 2) * 4 + self.stream % 4
        self.high = self.seq // 2
        self.group_bits = [1, 2, self.n_stream]
        self.deep_bits = [self.n_stream * (2 << b) for b in range(self.depth.bit_length() - 1)]
        self.wide_bits = [4 << b for b in range(self.wide.bit_length() - 1)]

    def flip(self, block, mask):
        return lax.ppermute(block, AXES, [(n, n ^ mask) for n in range(self.count)])

    def member_mask(self, p):
        return (p & 3) | ((p >> 2) * self.n_stream)

    def gather_flips(self, block, bits):
        for bit in bits:
            block = jnp.concatenate([block, self.flip(block, bit)], axis=0)
        return block

    def sum_flips(self, value, bits):
        for bit in bits:
            value = value + self.flip(value, bit)
        return value

    def pair_up(self, even, odd):
        sibling = self.flip(odd, 1)
        return [jnp.stack([even[i], sibling[i]]) for i in range(4)]

    def send_pairs(self, pairs):
        return [pairs[0]] + [self.flip(pairs[i], self.member_mask(2 * i)) for i in (1, 2, 3)]

    def exchange(self, even, odd):
        return self.send_pairs(self.pair_up(even, odd))


def after(value, *others):
    return pl.pallas_call(
        lambda *refs: None,
        out_shape=jax.ShapeDtypeStruct(value.shape, value.dtype),
        in_specs=[pl.BlockSpec(memory_space=pl.ANY)] * (1 + len(others)),
        out_specs=pl.BlockSpec(memory_space=pl.ANY),
        input_output_aliases={0: 0},
        name="after",
    )(value, *others)


def copy_kernel(in_ref, out_ref):
    out_ref[...] = in_ref[...]


def copied(value, *others):
    rows, width = value.shape
    spec = pl.BlockSpec((rows // 4, width), lambda i: (i, 0))
    return pl.pallas_call(
        waiting(copy_kernel, 1, others),
        grid=(4,),
        out_shape=jax.ShapeDtypeStruct(value.shape, value.dtype),
        in_specs=[spec, *unseen(others)],
        out_specs=spec,
        name="copied",
    )(value, *others)


def blank(shape, dtype):
    return pl.pallas_call(
        lambda out_ref: None,
        out_shape=jax.ShapeDtypeStruct(shape, dtype),
        out_specs=pl.BlockSpec(memory_space=pl.ANY),
        name="blank",
    )()


def waiting(kernel, operands, others):
    skip = operands + len(others)
    return lambda *refs: kernel(*refs[:operands], *refs[skip:])


def unseen(others):
    return [pl.BlockSpec(memory_space=pl.ANY)] * len(others)


def sizes(width):
    whole = width // (MEMBERS * LANES)
    rest = width // MEMBERS - whole * LANES
    assert whole == 2 and 0 < 3 * rest <= LANES and LANES % rest == 0
    return whole, rest


def lane_index(shape):
    return lax.broadcasted_iota(jnp.int32, shape, len(shape) - 1)


def pack_weight_kernel(width, member_ref, weight_ref, even_ref, odd_ref):
    rest = sizes(width)[1]
    taps, rows, _ = weight_ref.shape
    per_tile = LANES // rest
    lane = lane_index((rows, LANES))
    for p in range(MEMBERS):
        to = member_ref[0] ^ p
        out = (even_ref, odd_ref)[p % 2]
        column = 0
        for tile in range(2):
            for tap in range(taps):
                for gate in range(3):
                    start = pl.multiple_of(gate * width + (tile * MEMBERS + to) * LANES, LANES)
                    out[p // 2, :, pl.ds(column, LANES)] = weight_ref[tap, :, pl.ds(start, LANES)].astype(BF16)
                    column += LANES
                if tile == 0:
                    mixed = jnp.zeros((rows, LANES), F32)
                    for gate in range(3):
                        start = pl.multiple_of(gate * width + (2 * MEMBERS + to // per_tile) * LANES, LANES)
                        part = weight_ref[tap, :, pl.ds(start, LANES)]
                        part = pltpu.roll(part, lax.rem((gate - to % per_tile) * rest + LANES, LANES), 1)
                        inside = (lane >= gate * rest) & (lane < (gate + 1) * rest)
                        mixed = jnp.where(inside, part, mixed)
                    out[p // 2, :, pl.ds(column, LANES)] = mixed.astype(BF16)
                    column += LANES


def pack_weight(weight, member):
    taps, rows, columns = weight.shape
    shape = jax.ShapeDtypeStruct((4, rows, 14 * LANES), BF16)
    return pl.pallas_call(
        functools.partial(pack_weight_kernel, columns // 3),
        out_shape=(shape, shape),
        in_specs=[pl.BlockSpec(memory_space=pltpu.SMEM)] + in_vmem(1),
        out_specs=tuple(in_vmem(2)),
        compiler_params=params(),
        name="pack_weight",
    )(member, weight)


def place_weight_kernel(split, member_ref, own_ref, y_ref, x_ref, both_ref, first_ref, second_ref):
    for p in range(MEMBERS):
        block = (own_ref, y_ref, x_ref, both_ref)[p // 2][p % 2]
        first_ref[member_ref[0] ^ p] = block[:, :split]
        second_ref[member_ref[0] ^ p] = block[:, split:]


def place_weight(pairs, member, split, *others):
    _, rows, columns = pairs[0].shape
    return pl.pallas_call(
        waiting(functools.partial(place_weight_kernel, split), 5, others),
        out_shape=(
            jax.ShapeDtypeStruct((MEMBERS, rows, split), BF16),
            jax.ShapeDtypeStruct((MEMBERS, rows, columns - split), BF16),
        ),
        in_specs=[pl.BlockSpec(memory_space=pltpu.SMEM)] + in_vmem(4) + unseen(others),
        out_specs=tuple(in_vmem(2)),
        compiler_params=params(),
        name="place_weight",
    )(member, *pairs, *others)


def pick_rows_kernel(member_ref, first_ref, second_ref, even_ref, odd_ref, squares_ref):
    split = first_ref.shape[-1]
    squares = jnp.zeros((first_ref.shape[1], LANES), F32)
    for p in range(MEMBERS):
        for ref in (first_ref, second_ref):
            for i in range(ref.shape[-1] // LANES):
                squares += jnp.square(ref[p, :, pl.ds(i * LANES, LANES)].astype(F32))
    squares_ref[...] = jnp.sum(squares, axis=0, keepdims=True)
    for p in range(MEMBERS):
        out = (even_ref, odd_ref)[p % 2]
        out[p // 2, :, pl.ds(0, split)] = first_ref[member_ref[0] ^ p]
        out[p // 2, :, pl.ds(split, second_ref.shape[-1])] = second_ref[member_ref[0] ^ p]


def pick_rows(first, second, member):
    shape = jax.ShapeDtypeStruct((4, first.shape[1], first.shape[2] + second.shape[2]), BF16)
    return pl.pallas_call(
        pick_rows_kernel,
        out_shape=(shape, shape, jax.ShapeDtypeStruct((1, LANES), F32)),
        in_specs=[pl.BlockSpec(memory_space=pltpu.SMEM)] + in_vmem(2),
        out_specs=tuple(in_vmem(3)),
        compiler_params=params(),
        name="pick_rows",
    )(member, first, second)


def place_gradient_kernel(width, member_ref, *refs):
    rest = sizes(width)[1]
    out_ref = refs[4]
    taps, rows, _ = out_ref.shape
    per_tile = LANES // rest
    lane = lane_index((rows, LANES))
    for p in range(MEMBERS):
        source = member_ref[0] ^ p
        block_ref = refs[p // 2]
        column = 0
        for tile in range(2):
            for tap in range(taps):
                for gate in range(3):
                    start = pl.multiple_of(gate * width + (tile * MEMBERS + source) * LANES, LANES)
                    out_ref[tap, :, pl.ds(start, LANES)] = block_ref[p % 2, :, pl.ds(column, LANES)]
                    column += LANES
                if tile == 0:
                    mixed = block_ref[p % 2, :, pl.ds(column, LANES)].astype(F32)
                    column += LANES
                    for gate in range(3):
                        start = pl.multiple_of(gate * width + (2 * MEMBERS + source // per_tile) * LANES, LANES)
                        first = (source % per_tile) * rest
                        part = pltpu.roll(mixed, lax.rem(first - gate * rest + LANES, LANES), 1)
                        inside = (lane >= first) & (lane < first + rest)
                        old = out_ref[tap, :, pl.ds(start, LANES)].astype(F32)
                        out_ref[tap, :, pl.ds(start, LANES)] = jnp.where(inside, part, old).astype(BF16)


def place_gradient(pairs, member, shape):
    return pl.pallas_call(
        functools.partial(place_gradient_kernel, shape[2] // 3),
        out_shape=jax.ShapeDtypeStruct(shape, BF16),
        in_specs=[pl.BlockSpec(memory_space=pltpu.SMEM)] + in_vmem(4),
        out_specs=pl.BlockSpec(memory_space=pltpu.VMEM),
        compiler_params=params(),
        name="place_gradient",
    )(member, *pairs)


SMALL = 48


def small_rows(width, tokens, biases):
    edge = width // LANES
    keep = edge + tokens // LANES
    bias = keep + -(-biases // LANES)
    return edge, keep, bias, bias + 18


def pack_channels_kernel(width, marks, member_ref, values_ref, small_ref, even_first, odd_first, even_second, odd_second, rows):
    rest = sizes(width)[1]
    per_tile = LANES // rest
    count = values_ref.shape[0]
    tokens = pl.ds(0, count)
    edge, keep, bias, end = marks
    assert end <= SMALL
    for i in range(edge):
        rows[pl.ds(i, 1), :] = small_ref[pl.ds(0, 1), pl.ds(i * LANES, LANES)]
    for i in range(edge, keep):
        rows[pl.ds(i, 1), :] = small_ref[pl.ds(1, 1), pl.ds((i - edge) * LANES, LANES)]
    for i in range(keep, bias):
        rows[pl.ds(i, 1), :] = small_ref[pl.ds(2, 1), pl.ds((i - keep) * LANES, LANES)]
    for i in range(end, SMALL):
        rows[pl.ds(i, 1), :] = jnp.zeros((1, LANES), F32)
    fold = LANES // rest
    folded = pl.ds(count, count // fold)
    lane = lane_index((count // fold, LANES))
    for out in (even_second, odd_second):
        out[:, pl.ds(count, TAIL), :] = jnp.zeros((4, TAIL, LANES), BF16)
    for p in range(MEMBERS):
        first, second = ((even_first, even_second), (odd_first, odd_second))[p % 2]
        to = member_ref[0] ^ p
        for tile, out in enumerate((first, second)):
            start = pl.multiple_of((tile * MEMBERS + to) * LANES, LANES)
            out[p // 2, tokens, pl.ds(0, LANES)] = values_ref[:, pl.ds(start, LANES)]
        start = pl.multiple_of((2 * MEMBERS + to // per_tile) * LANES, LANES)
        part = values_ref[:, pl.ds(start, LANES)].astype(F32)
        total = jnp.zeros((count // fold, LANES), F32)
        for g in range(fold):
            group = pltpu.roll(part[g * (count // fold) : (g + 1) * (count // fold)], lax.rem(LANES + (g - to % per_tile) * rest, LANES), 1)
            total = jnp.where((lane >= g * rest) & (lane < (g + 1) * rest), group, total)
        first[p // 2, folded, :] = total.astype(BF16)
        at = bias
        for vector in (3, 4):
            for tile in range(3):
                start = (tile * MEMBERS + to) * LANES if tile < 2 else (2 * MEMBERS + to // per_tile) * LANES
                value = small_ref[pl.ds(vector, 1), pl.ds(pl.multiple_of(start, LANES), LANES)]
                if tile == 2:
                    value = pltpu.roll(value, lax.rem(LANES - (to % per_tile) * rest, LANES), 1)
                for _ in range(3):
                    piece = value.astype(BF16).astype(F32)
                    rows[pl.ds(at, 1), :] = piece
                    value = value - piece
                    at += 1
        first[p // 2, pl.ds(count + count // fold, SMALL), :] = rows[...].astype(BF16)


def pack_channels(values, small, marks, member, *others):
    rows, width = values.shape
    folded = rows * sizes(width)[1] // LANES
    first = jax.ShapeDtypeStruct((4, rows + folded + SMALL, LANES), BF16)
    second = jax.ShapeDtypeStruct((4, rows + TAIL, LANES), BF16)
    return pl.pallas_call(
        waiting(functools.partial(pack_channels_kernel, width, marks), 3, others),
        out_shape=(first, first, second, second),
        in_specs=[pl.BlockSpec(memory_space=pltpu.SMEM)] + in_vmem(2) + unseen(others),
        out_specs=tuple(in_vmem(4)),
        scratch_shapes=[pltpu.VMEM((SMALL, LANES), F32)],
        compiler_params=params(),
        name="pack_channels",
    )(member, values, small, *others)


def place_channels_kernel(width, member_ref, *refs):
    rest = sizes(width)[1]
    out_ref, tail_ref, all_ref = refs[8:]
    rows, _ = all_ref.shape
    per_tile = LANES // rest
    lane = lane_index((rows, LANES))
    for p in range(MEMBERS):
        source = member_ref[0] ^ p
        for tile in range(2):
            block_ref = refs[4 * tile + p // 2]
            start = pl.multiple_of((tile * MEMBERS + source) * LANES, LANES)
            all_ref[:, pl.ds(start, LANES)] = block_ref[p % 2, :, pl.ds(0, LANES)]
        start = pl.multiple_of((2 * MEMBERS + source // per_tile) * LANES, LANES)
        first = (source % per_tile) * rest
        part = pltpu.roll(refs[p // 2][p % 2, :, pl.ds(LANES, LANES)].astype(F32), first, 1)
        inside = (lane >= first) & (lane < first + rest)
        old = all_ref[:, pl.ds(start, LANES)].astype(F32)
        all_ref[:, pl.ds(start, LANES)] = jnp.where(inside, part, old).astype(BF16)
    out_ref[...] = all_ref[pl.ds(0, rows - TAIL), :]
    tail_ref[...] = all_ref[pl.ds(rows - TAIL, TAIL), :]


def place_channels(pairs, member, width):
    return pl.pallas_call(
        functools.partial(place_channels_kernel, width),
        out_shape=[jax.ShapeDtypeStruct((n, width), BF16) for n in (pairs[0].shape[1] - TAIL, TAIL)],
        in_specs=[pl.BlockSpec(memory_space=pltpu.SMEM)] + in_vmem(8),
        out_specs=in_vmem(2),
        scratch_shapes=[pltpu.VMEM((pairs[0].shape[1], width), BF16)],
        compiler_params=params(),
        name="place_channels",
    )(member, *pairs)


def bias_columns_kernel(width, place_ref, vectors_ref, out_ref, natural):
    rest = sizes(width)[1]
    per_tile = LANES // rest
    tiles = width // LANES
    lane = lane_index((1, LANES))
    for p in range(MEMBERS):
        source = place_ref[0] ^ p
        mixed = vectors_ref[pl.ds(p, 1), pl.ds(3 * LANES, LANES)]
        first = (source % per_tile) * rest
        for gate in range(3):
            natural[pl.ds(gate * tiles + source, 1), :] = vectors_ref[pl.ds(p, 1), pl.ds(gate * LANES, LANES)]
            part = vectors_ref[pl.ds(p, 1), pl.ds((4 + gate) * LANES, LANES)]
            natural[pl.ds(gate * tiles + MEMBERS + source, 1), :] = part
            row = pl.ds(gate * tiles + 2 * MEMBERS + source // per_tile, 1)
            part = pltpu.roll(mixed, lax.rem(first - gate * rest + LANES, LANES), 1)
            inside = (lane >= first) & (lane < first + rest)
            natural[row, :] = jnp.where(inside, part, natural[row, :])
    shift = place_ref[2]
    for i in range(out_ref.shape[0]):
        here = pltpu.roll(natural[pl.ds(place_ref[1] + i, 1), :], lax.rem(LANES - shift, LANES), 1)
        later = pltpu.roll(natural[pl.ds(place_ref[1] + i + 1, 1), :], lax.rem(LANES - shift, LANES), 1)
        out_ref[pl.ds(i, 1), :] = jnp.where(lane < LANES - shift, here, later)


def bias_columns(vectors, here, width, count):
    rows = -(-count // LANES)
    start = here.linear * count
    place = jnp.stack([here.member, start // LANES, start % LANES]).astype(jnp.int32)
    found = pl.pallas_call(
        functools.partial(bias_columns_kernel, width),
        out_shape=jax.ShapeDtypeStruct((rows, LANES), F32),
        in_specs=[pl.BlockSpec(memory_space=pltpu.SMEM)] + in_vmem(1),
        out_specs=pl.BlockSpec(memory_space=pltpu.VMEM),
        scratch_shapes=[pltpu.VMEM((3 * width // LANES + rows + 8, LANES), F32)],
        compiler_params=params(),
        name="bias_columns",
    )(place, vectors)
    return found.reshape(-1)[:count]


UNROLL = 16
GAP = 8


def token_loop(low, high, token, state, reverse):
    def several(i, state):
        for j in range(UNROLL):
            k = high - 1 - (i * UNROLL + j) if reverse else low + i * UNROLL + j
            state = token(k, state)
        return state

    return lax.fori_loop(0, (high - low) // UNROLL, several, state)


def row_block(rows):
    for block in (176, 48, 16):
        if rows % block == 0:
            return block
    return rows


def forward_kernel(tiles, rest, half_steps, *refs):
    gather = half_steps > 0
    x_refs, refs = (refs[:10], refs[10:]) if gather else (refs[:1], refs[1:])
    edge_ref, w_ref, bias_ref, keep_ref, cot_ref, *refs = refs
    if tiles == 2:
        folded_ref, *refs = refs
    act_ref, sum_ref, *refs = refs
    if gather:
        all_ref, *refs = refs
    both, cot_f32, carry, before = refs
    step = pl.program_id(0)
    block = act_ref.shape[0]
    rows = MEMBERS * block
    half = w_ref.shape[1] // 2
    count = half // LANES
    lane = lane_index((MEMBERS, LANES))

    if gather:
        for p in range(6):
            all_ref[p] = x_refs[p][...]

        @pl.when(step < half_steps)
        def _():
            all_ref[6] = x_refs[6][...]
            all_ref[7] = x_refs[7][...]

        @pl.when(step >= half_steps)
        def _():
            all_ref[6] = x_refs[8][...]
            all_ref[7] = x_refs[9][...]

        x = all_ref[...].reshape(rows, all_ref.shape[2])
    else:
        x = x_refs[0][...].reshape(rows, x_refs[0].shape[2])
    result = dot_f32(x, w_ref[...], ((1,), (0,)))
    for p in range(MEMBERS):
        at = pl.ds(p * (block + GAP), block)
        for i in range(2 * count):
            both[i, at, :] = result[p * block : (p + 1) * block, i * LANES : (i + 1) * LANES]
        cot_f32[0, at, :] = cot_ref[p].astype(F32)
        if tiles == 2:
            cot_f32[1, at, :] = pltpu.roll(folded_ref[p].astype(F32), lax.rem(LANES - step * rest, LANES), 1)

    @pl.when(step == 0)
    def _():
        for tile in range(tiles):
            carry[3 * tile] = jnp.ones((MEMBERS, LANES), F32)
            carry[3 * tile + 1] = jnp.zeros((MEMBERS, LANES), F32)
            carry[3 * tile + 2] = jnp.zeros((MEMBERS, LANES), F32)
        edges = dot_f32(edge_ref[...], w_ref[:, pl.ds(half, half)], ((1,), (0,)))
        for i in range(count):
            before[i] = edges[:MEMBERS, i * LANES : (i + 1) * LANES]

    def token(k, state):
        sums, earlier = state
        rows_at = pl.ds(k, MEMBERS, stride=block + GAP)
        keep = keep_ref[k]
        later = tuple(both[count + i, rows_at, :] for i in range(count))
        gates = [
            both[i, rows_at, :] + keep * earlier[i] + bias_ref[:, pl.ds(i * LANES, LANES)]
            for i in range(count)
        ]
        new = []
        outs = []
        for tile in range(tiles):
            if tile == 0:
                z = jnp.tanh(gates[0])
                u = 1.0 / (1.0 + jnp.exp(gates[1] + FORGET_SHIFT))
                o = 1.0 / (1.0 + jnp.exp(-gates[2]))
                outs += [z, u, o]
            else:
                mixed = gates[3]
                z = jnp.tanh(mixed)
                s = 1.0 / (1.0 + jnp.exp(jnp.where(lane < 2 * rest, mixed + FORGET_SHIFT, -mixed)))
                outs += [jnp.where(lane < rest, z, s)]
                u = pltpu.roll(s, LANES - rest, 1)
                o = pltpu.roll(s, LANES - 2 * rest, 1)
            a = keep * (1.0 - u)
            total, local, back = sums[3 * tile : 3 * tile + 3]
            cot = cot_f32[tile, rows_at, :]
            total = total * a
            new += [total, a * local + u * z, back + total * (cot * o)]
        for i, value in enumerate(outs):
            act_ref[k, :, pl.ds(i * LANES, LANES)] = value
        return tuple(new), later

    start = (tuple(carry[i] for i in range(3 * tiles)), tuple(before[i] for i in range(count)))
    sums, earlier = token_loop(0, block, token, start, False)
    for i in range(3 * tiles):
        carry[i] = sums[i]
        sum_ref[i] = sums[i]
    for i in range(count):
        before[i] = earlier[i]


def forward(pieces, edges, w, bias, keep, cot, tiles, rest, *others):
    gather = len(pieces) > 1
    width = w.shape[0]
    length = keep.shape[0]
    tokens = length - TAIL
    block = tokens // 4
    half = w.shape[1] // 2
    assert LANES // rest == 4
    cot_specs = [pl.BlockSpec((MEMBERS, block, LANES), lambda i: (0, i, 0))]
    if tiles == 2:
        cot_specs += [pl.BlockSpec((MEMBERS, block, LANES), lambda i: (0, 4, 0))]
    if gather:
        x_specs = [pl.BlockSpec((block, width), lambda i: (i, 0))] * 6
        x_specs += [pl.BlockSpec((block, width), lambda i: (jnp.minimum(i, 1), 0))] * 2
        x_specs += [pl.BlockSpec((block, width), lambda i: (jnp.maximum(i - 2, 0), 0))] * 2
    else:
        x_specs = [pl.BlockSpec((MEMBERS, block, width), lambda i: (0, i, 0))]
    whole = [jax.ShapeDtypeStruct((MEMBERS, length, width), BF16)] if gather else []
    return pl.pallas_call(
        waiting(
            functools.partial(forward_kernel, tiles, rest, 2 if gather else 0), len(pieces) + 4 + tiles, others
        ),
        grid=(4,),
        out_shape=(
            jax.ShapeDtypeStruct((length, MEMBERS, half), F32),
            jax.ShapeDtypeStruct((3 * tiles, MEMBERS, LANES), F32),
            *whole,
        ),
        in_specs=[
            *x_specs,
            *in_vmem(3),
            pl.BlockSpec((block, MEMBERS, LANES), lambda i: (i, 0, 0)),
            *cot_specs,
            *unseen(others),
        ],
        out_specs=(
            pl.BlockSpec((block, MEMBERS, half), lambda i: (i, 0, 0)),
            pl.BlockSpec((3 * tiles, MEMBERS, LANES), lambda i: (0, 0, 0)),
            *[pl.BlockSpec((MEMBERS, block, width), lambda i: (0, i, 0)) for _ in whole],
        ),
        scratch_shapes=[
            pltpu.VMEM((2 * half // LANES, MEMBERS * (block + GAP), LANES), F32),
            pltpu.VMEM((tiles, MEMBERS * (block + GAP), LANES), F32),
            pltpu.VMEM((3 * tiles, MEMBERS, LANES), F32),
            pltpu.VMEM((half // LANES, MEMBERS, LANES), F32),
        ],
        compiler_params=params(),
        name="forward",
    )(*pieces, edges, w, bias, keep, *[cot] * tiles, *others)


def backward_kernel(
    tiles, rest, blocks, act_ref, keep_ref, enter_ref, arrive_ref, final_ref, cot_ref, folded_ref,
    even_ref, odd_ref, grads_ref, bias_ref, edge_ref, memory, cot_f32, wide, hold, carry, after, unfolded=None,
):
    step = pl.program_id(0)
    block = act_ref.shape[0]
    half = act_ref.shape[2]
    lane = lane_index((MEMBERS, LANES))
    which = jnp.where(step < blocks, step, 2 * blocks - 1 - step)
    base = which * block
    for p in range(MEMBERS):
        cot_f32[pl.ds(p * (block + GAP), block), :] = cot_ref[p].astype(F32)
    count = half // LANES
    top = jnp.where(which == blocks - 1, block - TAIL, block)

    def values(k, tile):
        at = lambda i: act_ref[k, :, pl.ds(i * LANES, LANES)]
        if tile == 0:
            return at(0), at(1), at(2)
        mixed = at(3)
        return mixed, pltpu.roll(mixed, LANES - rest, 1), pltpu.roll(mixed, LANES - 2 * rest, 1)

    if tiles == 2:
        long, short = unfolded.shape[0] // MEMBERS, folded_ref.shape[1]

        @pl.when(step == 0)
        def _():
            for p in range(MEMBERS):
                folded = folded_ref[p].astype(F32)
                for g in range(LANES // rest):
                    part = pltpu.roll(folded, LANES - g * rest, 1) if g else folded
                    unfolded[pl.ds(p * long + g * short, short), :] = part

    @pl.when(step == 0)
    def _():
        for tile in range(tiles):
            memory[0, tile] = enter_ref[tile]
            carry[tile] = enter_ref[tile]

    @pl.when(step < blocks)
    def _():
        def token(k, state):
            keep = keep_ref[k]
            new = []
            for tile in range(tiles):
                z, u, o = values(k, tile)
                m = keep * (1.0 - u) * state[tile] + u * z
                memory[base + k + 1, tile] = m
                hold[tile, pl.ds(k, MEMBERS, stride=block + GAP), :] = o * m
                new.append(m)
            return tuple(new)

        state = token_loop(0, top, token, tuple(carry[t] for t in range(tiles)), False)
        for tile in range(tiles):
            carry[tile] = state[tile]

        @pl.when(which == blocks - 1)
        def _():
            for tile in range(tiles):
                rest_of = final_ref[tile]
                for row in range(3):
                    part = rest_of.astype(BF16).astype(F32)
                    hold[tile, pl.ds(block - TAIL + row, MEMBERS, stride=block + GAP), :] = part
                    rest_of = rest_of - part
                for row in range(3, TAIL):
                    hold[tile, pl.ds(block - TAIL + row, MEMBERS, stride=block + GAP), :] = jnp.zeros_like(part)

        for tile in range(tiles):
            for p in range(MEMBERS):
                part = hold[tile, pl.ds(p * (block + GAP), block), :].astype(BF16)
                (even_ref, odd_ref)[p % 2][p // 2, :, pl.ds(tile * LANES, LANES)] = part

    @pl.when(step == blocks)
    def _():
        for tile in range(tiles):
            carry[tile] = arrive_ref[tile]
        after[...] = jnp.zeros_like(after)
        bias_ref[...] = jnp.zeros_like(bias_ref)

    @pl.when(step >= blocks)
    def _():
        def token(k, state):
            arriving, shifted, totals = state
            rows_at = pl.ds(k, MEMBERS, stride=block + GAP)
            keep = keep_ref[k]
            new, parts = [], []
            for tile in range(tiles):
                z, u, o = values(k, tile)
                f = 1.0 - u
                if tile == 0:
                    cot = cot_f32[rows_at, :]
                else:
                    cot = unfolded[pl.ds(base + k, MEMBERS, stride=long), :]
                held = keep * memory[base + k, tile]
                m = memory[base + k + 1, tile]
                grad = cot * o
                adjoint = grad + arriving[tile]
                new.append(keep * f * adjoint)
                scaled = adjoint * u
                one = [scaled * (1.0 - z * z), scaled * (held - z) * f, grad * m * (1.0 - o)]
                if tile == 1:
                    one = [
                        jnp.where(lane < rest, one[0], jnp.where(lane < 2 * rest, pltpu.roll(one[1], rest, 1), jnp.where(lane < 3 * rest, pltpu.roll(one[2], 2 * rest, 1), 0.0)))
                    ]
                parts += one
            for i, part in enumerate(parts):
                wide[i, rows_at, :] = part
                wide[count + i, rows_at, :] = shifted[i]
            return tuple(new), tuple(keep * part for part in parts), tuple(t + p for t, p in zip(totals, parts))

        state = (
            tuple(carry[t] for t in range(tiles)),
            tuple(after[i] for i in range(count)),
            tuple(bias_ref[:, pl.ds(i * LANES, LANES)] for i in range(count)),
        )
        arriving, shifted, totals = token_loop(0, top, token, state, True)
        for tile in range(tiles):
            carry[tile] = arriving[tile]
        for i in range(count):
            after[i] = shifted[i]
            edge_ref[:, pl.ds(i * LANES, LANES)] = shifted[i]
            bias_ref[:, pl.ds(i * LANES, LANES)] = totals[i]

        @pl.when(which == blocks - 1)
        def _():
            for row in range(block - TAIL, block):
                for i in range(2 * count):
                    wide[i, pl.ds(row, MEMBERS, stride=block + GAP), :] = jnp.zeros((MEMBERS, LANES), F32)

        for i in range(2 * count):
            for p in range(MEMBERS):
                part = wide[i, pl.ds(p * (block + GAP), block), :].astype(BF16)
                grads_ref[p, :, pl.ds(i * LANES, LANES)] = part


def backward(act, keep, cot, enter, arrive, final, tiles, rest, *others):
    length, members, half = act.shape
    block = row_block(length)
    blocks = length // block
    lanes = tiles * LANES
    turn = lambda i: jnp.where(i < blocks, i, 2 * blocks - 1 - i)
    return pl.pallas_call(
        waiting(functools.partial(backward_kernel, tiles, rest, blocks), 7, others),
        grid=(2 * blocks,),
        out_shape=(
            jax.ShapeDtypeStruct((members // 2, length, lanes), BF16),
            jax.ShapeDtypeStruct((members // 2, length, lanes), BF16),
            jax.ShapeDtypeStruct((members, length, 2 * half), BF16),
            jax.ShapeDtypeStruct((members, half), F32),
            jax.ShapeDtypeStruct((members, half), F32),
        ),
        in_specs=[
            pl.BlockSpec((block, members, half), lambda i: (turn(i), 0, 0)),
            pl.BlockSpec((block, members, LANES), lambda i: (turn(i), 0, 0)),
            *in_vmem(3),
            pl.BlockSpec((members, block, LANES), lambda i: (0, turn(i), 0)),
            pl.BlockSpec((members, (length - TAIL) // 4, LANES), lambda i: (0, 4 if tiles == 2 else 0, 0)),
            *unseen(others),
        ],
        out_specs=(
            pl.BlockSpec((members // 2, block, lanes), lambda i: (0, jnp.minimum(i, blocks - 1), 0)),
            pl.BlockSpec((members // 2, block, lanes), lambda i: (0, jnp.minimum(i, blocks - 1), 0)),
            pl.BlockSpec((members, block, 2 * half), lambda i: (0, jnp.minimum(2 * blocks - 1 - i, blocks - 1), 0)),
            pl.BlockSpec((members, half), lambda i: (0, 0)),
            pl.BlockSpec((members, half), lambda i: (0, 0)),
        ),
        scratch_shapes=[
            pltpu.VMEM((length, tiles, members, LANES), F32),
            pltpu.VMEM((members * (block + GAP), LANES), F32),
            pltpu.VMEM((2 * half // LANES, members * (block + GAP), LANES), F32),
            pltpu.VMEM((tiles, members * (block + GAP), LANES), F32),
            pltpu.VMEM((tiles, members, LANES), F32),
            pltpu.VMEM((half // LANES, members, LANES), F32),
            *[pltpu.VMEM((members * (length - TAIL + GAP), LANES), F32) for _ in range(tiles - 1)],
        ],
        compiler_params=params(),
        name="backward",
    )(act, keep, enter, arrive, final, cot, cot, *others)


def input_gradient_kernel(first_ref, second_ref, w_first, w_second, even_ref, odd_ref):
    for p, out in enumerate((even_ref, odd_ref)):
        out[0] = (
            dot_f32(first_ref[p], w_first[...], ((1,), (1,)))
            + dot_f32(second_ref[p], w_second[...], ((1,), (1,)))
        ).astype(BF16)


def input_gradients(first, second, w_first, w_second, start, count, *others):
    _, length, _ = first.shape
    width = w_first.shape[0]
    shape = jax.ShapeDtypeStruct((count, length, width), BF16)
    return pl.pallas_call(
        waiting(input_gradient_kernel, 4, others),
        grid=(count,),
        out_shape=(shape, shape),
        in_specs=[
            pl.BlockSpec((2, length, first.shape[2]), lambda i: (start + i, 0, 0)),
            pl.BlockSpec((2, length, second.shape[2]), lambda i: (start + i, 0, 0)),
            *in_vmem(2),
            *unseen(others),
        ],
        out_specs=(pl.BlockSpec((1, length, width), lambda i: (i, 0, 0)),) * 2,
        compiler_params=params(),
        name="input_gradient",
    )(first, second, w_first, w_second, *others)


def far_sum_kernel(even_ref, odd_ref, low_ref, high_ref):
    total = even_ref[0].astype(F32) + odd_ref[0].astype(F32)
    middle = low_ref.shape[0]
    low_ref[...] = total[:middle].astype(BF16)
    high_ref[...] = total[middle:].astype(BF16)


def far_sum(even, odd, middle):
    _, length, width = even.shape
    block = 384
    sums = [jax.ShapeDtypeStruct((rows, width), BF16) for rows in (middle, length - middle)]
    spec = pl.BlockSpec((1, length, block), lambda i: (0, 0, i))
    return pl.pallas_call(
        far_sum_kernel,
        grid=(width // block,),
        out_shape=sums,
        in_specs=[spec, spec],
        out_specs=[pl.BlockSpec((rows, block), lambda i: (0, i)) for rows in (middle, length - middle)],
        compiler_params=params(),
        name="far_sum",
    )(even, odd)


def near_sums_kernel(even_ref, odd_ref, low_ref, high_ref, y_low, y_high, x_low, x_high):
    middle = low_ref.shape[0]
    total = even_ref[0].astype(F32) + odd_ref[0].astype(F32)
    y_low[...] = (total[:middle] + low_ref[...].astype(F32)).astype(BF16)
    y_high[...] = total[middle:].astype(BF16)
    total = even_ref[1].astype(F32) + odd_ref[1].astype(F32)
    x_low[...] = total[:middle].astype(BF16)
    x_high[...] = (total[middle:] + high_ref[...].astype(F32)).astype(BF16)


def near_sums(even, odd, low, high):
    _, length, width = even.shape
    block = 384
    spec = pl.BlockSpec((2, length, block), lambda i: (0, 0, i))
    halves = [pl.BlockSpec((part.shape[0], block), lambda i: (0, i)) for part in (low, high)]
    return pl.pallas_call(
        near_sums_kernel,
        grid=(width // block,),
        out_shape=[jax.ShapeDtypeStruct(part.shape, BF16) for part in (low, high, low, high)],
        in_specs=[spec, spec] + halves,
        out_specs=halves * 2,
        compiler_params=params(),
        name="near_sums",
    )(even, odd, low, high)


def last_sum_kernel(even_ref, odd_ref, y_low, x_low, y_high, x_high, next_ref, out_ref):
    middle = y_low.shape[0]
    rows = out_ref.shape[0] - middle
    total = even_ref[0].astype(F32) + odd_ref[0].astype(F32)
    out_ref[pl.ds(0, middle), :] = (total[:middle] + y_low[...].astype(F32) + x_low[...].astype(F32)).astype(BF16)
    high = total[middle : middle + rows] + y_high[pl.ds(0, rows), :].astype(F32) + x_high[pl.ds(0, rows), :].astype(F32)
    row = lax.broadcasted_iota(jnp.int32, high.shape, 0)
    out_ref[pl.ds(middle, rows), :] = jnp.where(row == rows - 1, high + next_ref[...], high).astype(BF16)


def last_sum(even, odd, lows, highs, from_next, tokens):
    _, length, width = even.shape
    block = 384
    spec = pl.BlockSpec((1, length, block), lambda i: (0, 0, i))
    parts = [*lows, *highs, from_next]
    return pl.pallas_call(
        last_sum_kernel,
        grid=(width // block,),
        out_shape=jax.ShapeDtypeStruct((tokens, width), BF16),
        in_specs=[spec, spec] + [pl.BlockSpec((part.shape[0], block), lambda i: (0, i)) for part in parts],
        out_specs=pl.BlockSpec((tokens, block), lambda i: (0, i)),
        compiler_params=params(),
        name="last_sum",
    )(even, odd, *parts)


def adamw(master, gradient, moment_one, moment_two, rate):
    moment_one = BETA_ONE * moment_one + (1.0 - BETA_ONE) * gradient
    moment_two = BETA_TWO * moment_two + (1.0 - BETA_TWO) * gradient * gradient
    step_size = (
        moment_one
        / (1.0 - BETA_ONE**STEP)
        / (jnp.sqrt(moment_two / (1.0 - BETA_TWO**STEP)) + EPSILON)
    )
    return (master - rate * (step_size + DECAY_RATE * master), moment_one, moment_two)


def channel_tiles(vector, member, rest):
    width = vector.shape[-1]
    axis = vector.ndim - 1
    pieces = [
        lax.dynamic_slice_in_dim(vector, member * LANES, LANES, axis),
        lax.dynamic_slice_in_dim(vector, (MEMBERS + member) * LANES, LANES, axis),
        lax.dynamic_slice_in_dim(vector, 2 * MEMBERS * LANES + member * rest, rest, axis),
    ]
    return pieces


def widen(part):
    return jnp.pad(part, [(0, 0)] * (part.ndim - 1) + [(0, LANES - part.shape[-1])])


def on_device(
    inputs,
    boundary,
    start_state,
    weight,
    gate_bias,
    first_weight,
    second_weight,
    first_bias,
    second_bias,
    cotangent,
    final_cotangent,
):
    here = Place()
    tokens, width = inputs.shape[1:]
    rest = sizes(width)[1]
    member = here.member.astype(jnp.int32).reshape(1)
    taps, own_rows, columns = weight.shape
    length = tokens + TAIL
    deep_groups = [[lo + 2 * h for h in range(here.depth)] for lo in range(2)]
    wide_groups = [[jl + 4 * h for h in range(here.wide)] for jl in range(4)]

    weight_pairs = here.pair_up(*pack_weight(weight, member))
    weight_got = here.send_pairs(weight_pairs)

    def all_rows(part):
        cols = part.shape[-1]
        if here.wide > 1:
            part = lax.all_gather(part, "stream", axis=0, axis_index_groups=wide_groups)
            part = part.reshape(here.wide, 2, 4 * own_rows, cols).swapaxes(0, 1)
        part = part.reshape(-1, cols)
        return lax.all_gather(part, "seq", axis=0, tiled=True, axis_index_groups=deep_groups)

    own_bias = gate_bias.shape[0]
    marks = small_rows(width, tokens, own_bias)
    pad_to = lambda row: jnp.pad(row.astype(F32).reshape(1, -1), ((0, 0), (0, width - row.size)))
    small = [inputs[0, -1:].astype(F32), pad_to(1 - boundary[0]), pad_to(gate_bias.astype(BF16))]
    small = jnp.concatenate(small + [start_state, final_cotangent])

    own = inputs[0]
    own_copy = copied(own, weight_pairs[3])
    packed_cot = pack_channels(cotangent[0], small, marks, member, own_copy, weight_pairs[3])
    cot_first = here.pair_up(*packed_cot[:2])
    got_first = here.send_pairs(cot_first)
    placed = place_weight(weight_got, member, 8 * LANES, got_first[1])
    weights = [all_rows(part) for part in placed]
    own_sibling = here.flip(own, 1)
    sent = after(own_copy, *got_first[1:])
    middle = (tokens // 32) * 16
    from_y = here.flip(sent, here.member_mask(2))
    from_x = here.flip(sent, here.member_mask(4))
    low_part, high_part = from_y[:middle], from_x[middle:]
    both_low = here.flip(low_part, here.member_mask(4))
    both_high = here.flip(high_part, here.member_mask(2))
    y_sibling, x_sibling = here.flip(from_y, 1), here.flip(from_x, 1)
    cots = [jnp.concatenate(got_first, axis=0)]
    pieces = [own, own_sibling, from_y, y_sibling, from_x, x_sibling]
    pieces += [both_low, here.flip(both_low, 1), both_high, here.flip(both_high, 1)]

    smalls = cots[0][:, tokens + tokens * rest // LANES :].astype(F32)
    lower = ((jnp.arange(MEMBERS) >> 2) ^ (here.seq % 2)) == 0
    lasts = smalls[:, : marks[0]].reshape(MEMBERS, width).astype(BF16)
    plane = 2 * here.n_stream
    behind = lax.ppermute(lasts, AXES, [(n, n + plane) for n in range(here.count - plane)])
    swap = lambda rows: jnp.concatenate([rows[4:], rows[:4]], axis=0)
    edges = jnp.where(lower[:, None], swap(behind), swap(lasts))
    edges = jnp.pad(edges, ((0, TAIL - MEMBERS), (0, 0)))
    keep = smalls[:, marks[0] : marks[1]].reshape(MEMBERS, tokens).T
    keep = jnp.pad(keep, ((0, TAIL), (0, 0)))
    keep = jnp.broadcast_to(keep[:, :, None], (length, MEMBERS, LANES))
    states = jnp.sum(smalls[:, marks[2] : marks[3]].reshape(MEMBERS, 2, 3, 3, LANES), axis=3)
    starts, finals = ([states[:, i, tile] for tile in range(3)] for i in range(2))
    all_bits = [1 << b for b in range(here.count.bit_length() - 1)]
    bias_all = smalls[:, marks[1] : marks[2]].reshape(1, MEMBERS, -1)[:, :, :own_bias].astype(BF16)
    bias_all = here.gather_flips(bias_all, here.deep_bits + here.wide_bits).astype(F32)
    bias_all = bias_all.reshape(here.wide, here.depth, MEMBERS, own_bias)
    every_member = here.member ^ jnp.arange(MEMBERS)
    bias_all = jnp.take(bias_all, (here.stream // 4) ^ jnp.arange(here.wide), axis=0)
    bias_all = jnp.take(bias_all, here.high ^ jnp.arange(here.depth), axis=1)
    bias_all = jnp.take(bias_all, every_member, axis=2)
    bias_all = bias_all.reshape(here.wide, here.depth, 2, 4, own_bias).transpose(1, 2, 0, 3, 4).reshape(3, width)
    cot_second = here.pair_up(packed_cot[2], after(packed_cot[3], behind))
    got_second = here.send_pairs([after(pair, pieces[7], pieces[9]) for pair in cot_second])
    bias_parts = channel_tiles(bias_all, here.member, rest)
    biases = [
        jnp.concatenate([bias_parts[0].reshape(1, 3 * LANES), widen(bias_parts[2].reshape(1, 3 * rest))], axis=1),
        bias_parts[1].reshape(1, 3 * LANES),
    ]

    def both_halves(value):
        other = jnp.concatenate([value[4:], value[:4]], axis=0)
        mask = lower[:, None]
        return jnp.where(mask, value, other), jnp.where(mask, other, value)

    def back_pairs(first, second, start, count, *others):
        even, odd = input_gradients(first, second, weights[0], weights[1], start, count, *others)
        return even, here.flip(odd, 1)

    halfway = (length // 32) * 16
    gradients, outs, hidden_got = [], [], []
    acts, summaries = [], []
    for chunk in range(2):
        source = [x_all] if chunk else pieces
        act, summary, *whole = forward(source, edges, weights[chunk], biases[chunk], keep, cots[chunk], 2 - chunk, rest)
        acts.append(act)
        summaries.append(summary)
        if whole:
            got_second = [after(got, summary) for got in got_second]
            cots.append(jnp.concatenate(got_second, axis=0))
            behind = jnp.pad(edges[:MEMBERS, None], ((0, 0), (0, TAIL - 1), (0, 0)))
            x_all = lax.dynamic_update_slice(whole[0], behind, (0, tokens, 0))
    both_every = here.gather_flips(jnp.concatenate(summaries)[None], here.deep_bits)

    for chunk in range(2):
        tiles = 2 - chunk
        act = acts[chunk]
        every = both_every[:, :6] if chunk == 0 else both_every[:, 6:]
        enters, arrives, ends = [], [], []
        for tile in range(tiles):
            where = (0, 2, 1)[2 * chunk + tile]
            state, back = starts[where], finals[where]
            enter, arrive = state, back
            for z in range(here.depth):
                part = jnp.take(every, z ^ here.high, axis=0)
                a_low, a_high = both_halves(part[3 * tile])
                b_low, b_high = both_halves(part[3 * tile + 1])
                between = a_low * state + b_low
                enter = jnp.where(z == here.high, jnp.where(lower[:, None], state, between), enter)
                state = a_high * between + b_high
            for z in reversed(range(here.depth)):
                part = jnp.take(every, z ^ here.high, axis=0)
                a_low, a_high = both_halves(part[3 * tile])
                c_low, c_high = both_halves(part[3 * tile + 2])
                between = a_high * back + c_high
                arrive = jnp.where(z == here.high, jnp.where(lower[:, None], between, back), arrive)
                back = a_low * between + c_low
            enters.append(enter)
            arrives.append(arrive)
            ends.append(state)
        others = (outs[0][4],) if chunk else ()
        even, odd, grads, bias_grad, edge_grad = backward(
            act, keep, cots[chunk], jnp.stack(enters), jnp.stack(arrives), jnp.stack(ends), tiles, rest, *others
        )
        half = edge_grad.shape[1]
        edge_grad = jnp.pad(edge_grad.astype(BF16)[:, None], ((0, 0), (0, TAIL - 1), (half, 0)))
        grads = lax.dynamic_update_slice(grads, edge_grad, (0, tokens, 0))
        hidden_got += here.send_pairs(here.pair_up(even, odd))
        if chunk == 1:
            far_low, far_high = far_sum(*back_pairs(outs[0][2], grads, 3, 1, *hidden_got[1:4]), halfway)
            grads = after(grads, far_low, *hidden_got[5:])
        flat = grads.reshape(MEMBERS * length, -1)
        local = dot_f32(x_all.reshape(MEMBERS * length, width), flat, ((0,), (0,))).astype(BF16)
        cols = local.shape[-1]
        local = after(local, gradients[0]) if gradients else local
        summed = lax.psum_scatter(local, "seq", scatter_dimension=0, tiled=True, axis_index_groups=deep_groups)
        if here.wide > 1:
            summed = summed.reshape(2, here.wide, 4 * own_rows, cols).swapaxes(0, 1).reshape(-1, cols)
            summed = lax.psum_scatter(summed, "stream", scatter_dimension=0, tiled=True, axis_index_groups=wide_groups)
        gradients.append(summed.reshape(MEMBERS, own_rows, cols))
        outs.append((even, odd, grads, jnp.sum(bias_grad, axis=0), local))

    low_half = here.flip(far_low, here.member_mask(4))
    high_half = here.flip(far_high, here.member_mask(2))
    grads = outs[0][2], outs[1][2]
    even, odd = back_pairs(*grads, 1, 2, low_half, high_half, outs[1][4], gradients[0])
    y_low, y_high, x_low, x_high = near_sums(even, odd, low_half, high_half)
    lows = here.flip(y_low, here.member_mask(2)), here.flip(x_low, here.member_mask(4))
    highs = here.flip(y_high, here.member_mask(2)), here.flip(x_high, here.member_mask(4))
    hidden_own, final_rows = place_channels(hidden_got, member, width)
    hidden = hidden_own[None]
    whole_final = jnp.sum(final_rows[:3].astype(F32), axis=0, keepdims=True)
    own_columns = width // here.n_seq
    final_state = lax.dynamic_slice_in_dim(whole_final, here.seq * own_columns, own_columns, 1)
    even, odd = back_pairs(*grads, 0, 1, y_high, hidden_own)
    gradients = [after(gradient, even, *highs) for gradient in gradients]
    *picked, squares = pick_rows(*gradients, member)
    post_pairs = here.pair_up(*picked)
    edge_sum = sum(part[tokens - halfway : tokens - halfway + 1].astype(F32) for part in (even[0, halfway:], odd[0, halfway:], *highs))
    from_next = lax.ppermute(edge_sum, "seq", [(i + 1, i) for i in range(here.n_seq - 1)])
    received = here.send_pairs(post_pairs)

    vector = jnp.concatenate([outs[0][3], outs[1][3], squares[0]]).reshape(1, -1)
    vector = here.sum_flips(after(vector, *post_pairs[1:]), here.deep_bits + here.wide_bits)
    vector = here.gather_flips(vector, here.group_bits[:1])
    vector = after(vector, *received[1:])
    from_next = after(from_next, vector)
    input_gradient = last_sum(even, odd, lows, highs, from_next, tokens)[None]
    vectors = [vector] + [here.flip(vector, here.member_mask(2 * i)) for i in (1, 2, 3)]
    vectors = jnp.concatenate(vectors, axis=0)
    gradient_norm = jnp.sqrt(jnp.sum(vectors[:, -LANES:]) + jnp.sum(jnp.square(vectors[:, :-LANES])))
    bias_raw = bias_columns(vectors, here, width, own_bias)

    clip_factor = jnp.minimum(1.0, CLIP_NORM / (gradient_norm + 1e-06))
    raw = place_gradient(received, member, weight.shape)
    weight_gradient = clip_factor * raw.astype(F32)
    bias_gradient = clip_factor * bias_raw
    new_weight, new_first_weight, new_second_weight = adamw(
        weight, weight_gradient, first_weight, second_weight, RATE_WEIGHT
    )
    new_bias, new_first_bias, new_second_bias = adamw(
        gate_bias, bias_gradient, first_bias, second_bias, RATE_BIAS
    )
    return (
        hidden,
        final_state,
        input_gradient,
        weight_gradient,
        bias_gradient,
        gradient_norm,
        new_weight,
        new_first_weight,
        new_second_weight,
        new_bias,
        new_first_bias,
        new_second_bias,
    )


def solution(mesh):
    placed = (
        P("stream", "seq", None),
        P("stream", "seq"),
        P("stream", None),
        P(None, ("seq", "stream"), None),
        P(("seq", "stream")),
        P(None, ("seq", "stream"), None),
        P(None, ("seq", "stream"), None),
        P(("seq", "stream")),
        P(("seq", "stream")),
        P("stream", "seq", None),
        P("stream", None),
    )
    return jax.shard_map(
        on_device,
        mesh=mesh,
        in_specs=placed,
        out_specs=(
            P("stream", "seq", None),
            P("stream", "seq"),
            P("stream", "seq", None),
            P(None, ("seq", "stream"), None),
            P(("seq", "stream")),
            P(),
            P(None, ("seq", "stream"), None),
            P(None, ("seq", "stream"), None),
            P(None, ("seq", "stream"), None),
            P(("seq", "stream")),
            P(("seq", "stream")),
            P(("seq", "stream")),
        ),
        check_vma=False,
    )
```

```python
import functools
import jax
import jax.numpy as jnp
from jax import lax
from jax.experimental import pallas as pl
from jax.experimental.pallas import tpu as pltpu
from jax.sharding import PartitionSpec as P

STEP = 10
BETA_ONE = 0.9
BETA_TWO = 0.95
EPSILON = 1e-08
RATE_WEIGHT = 0.01
RATE_BIAS = 1.0
DECAY_RATE = 0.1
CLIP_NORM = 1.0
FORGET_SHIFT = 6.0

AXES = ("seq", "stream")
LANES = 128
MEMBERS = 8
TAIL = 16
BF16 = jnp.bfloat16
F32 = jnp.float32
VMEM_LIMIT = 60 * 1024 * 1024


def params():
    return pltpu.CompilerParams(vmem_limit_bytes=VMEM_LIMIT)


def in_vmem(count):
    return [pl.BlockSpec(memory_space=pltpu.VMEM)] * count


def dot_f32(a, b, dims):
    return lax.dot_general(a, b, (dims, ((), ())), preferred_element_type=F32)


class Place:
    def __init__(self):
        self.n_seq = lax.axis_size("seq")
        self.n_stream = lax.axis_size("stream")
        self.depth = self.n_seq // 2
        self.wide = self.n_stream // 4
        self.count = self.n_seq * self.n_stream
        self.seq = lax.axis_index("seq")
        self.stream = lax.axis_index("stream")
        self.linear = self.seq * self.n_stream + self.stream
        self.member = (self.seq % 2) * 4 + self.stream % 4
        self.high = self.seq // 2
        self.group_bits = [1, 2, self.n_stream]
        self.deep_bits = [self.n_stream * (2 << b) for b in range(self.depth.bit_length() - 1)]
        self.wide_bits = [4 << b for b in range(self.wide.bit_length() - 1)]

    def flip(self, block, mask):
        return lax.ppermute(block, AXES, [(n, n ^ mask) for n in range(self.count)])

    def member_mask(self, p):
        return (p & 3) | ((p >> 2) * self.n_stream)

    def gather_flips(self, block, bits):
        if len(bits) == 2:
            parts = [self.flip(block, mask) for mask in (bits[0], bits[1], bits[0] | bits[1])]
            return jnp.concatenate([block, *parts], axis=0)
        for bit in bits:
            block = jnp.concatenate([block, self.flip(block, bit)], axis=0)
        return block

    def sum_flips(self, value, bits):
        if len(bits) == 2:
            parts = [self.flip(value, mask) for mask in (bits[0], bits[1], bits[0] | bits[1])]
            return (value + parts[0]) + (parts[1] + parts[2])
        for bit in bits:
            value = value + self.flip(value, bit)
        return value

    def pair_up(self, even, odd):
        sibling = self.flip(odd, 1)
        return [jnp.stack([even[i], sibling[i]]) for i in range(4)]

    def send_pairs(self, pairs):
        return [pairs[0]] + [self.flip(pairs[i], self.member_mask(2 * i)) for i in (1, 2, 3)]

    def exchange(self, even, odd):
        return self.send_pairs(self.pair_up(even, odd))


def after(value, *others):
    return pl.pallas_call(
        lambda *refs: None,
        out_shape=jax.ShapeDtypeStruct(value.shape, value.dtype),
        in_specs=[pl.BlockSpec(memory_space=pl.ANY)] * (1 + len(others)),
        out_specs=pl.BlockSpec(memory_space=pl.ANY),
        input_output_aliases={0: 0},
        name="after",
    )(value, *others)


def copy_kernel(in_ref, out_ref):
    out_ref[...] = in_ref[...]


def copied(value, *others):
    rows, width = value.shape
    spec = pl.BlockSpec((rows // 4, width), lambda i: (i, 0))
    return pl.pallas_call(
        waiting(copy_kernel, 1, others),
        grid=(4,),
        out_shape=jax.ShapeDtypeStruct(value.shape, value.dtype),
        in_specs=[spec, *unseen(others)],
        out_specs=spec,
        name="copied",
    )(value, *others)


def blank(shape, dtype):
    return pl.pallas_call(
        lambda out_ref: None,
        out_shape=jax.ShapeDtypeStruct(shape, dtype),
        out_specs=pl.BlockSpec(memory_space=pl.ANY),
        name="blank",
    )()


def waiting(kernel, operands, others):
    skip = operands + len(others)
    return lambda *refs: kernel(*refs[:operands], *refs[skip:])


def unseen(others):
    return [pl.BlockSpec(memory_space=pl.ANY)] * len(others)


def sizes(width):
    whole = width // (MEMBERS * LANES)
    rest = width // MEMBERS - whole * LANES
    assert whole == 2 and 0 < 3 * rest <= LANES and LANES % rest == 0
    return whole, rest


def lane_index(shape):
    return lax.broadcasted_iota(jnp.int32, shape, len(shape) - 1)


def pack_weight_kernel(width, member_ref, weight_ref, even_ref, odd_ref):
    rest = sizes(width)[1]
    taps, rows, _ = weight_ref.shape
    per_tile = LANES // rest
    lane = lane_index((rows, LANES))
    for p in range(MEMBERS):
        to = member_ref[0] ^ p
        out = (even_ref, odd_ref)[p % 2]
        column = 0
        for tile in range(2):
            for tap in range(taps):
                for gate in range(3):
                    start = pl.multiple_of(gate * width + (tile * MEMBERS + to) * LANES, LANES)
                    out[p // 2, :, pl.ds(column, LANES)] = weight_ref[tap, :, pl.ds(start, LANES)].astype(BF16)
                    column += LANES
                if tile == 0:
                    mixed = jnp.zeros((rows, LANES), F32)
                    for gate in range(3):
                        start = pl.multiple_of(gate * width + (2 * MEMBERS + to // per_tile) * LANES, LANES)
                        part = weight_ref[tap, :, pl.ds(start, LANES)]
                        part = pltpu.roll(part, lax.rem((gate - to % per_tile) * rest + LANES, LANES), 1)
                        inside = (lane >= gate * rest) & (lane < (gate + 1) * rest)
                        mixed = jnp.where(inside, part, mixed)
                    out[p // 2, :, pl.ds(column, LANES)] = mixed.astype(BF16)
                    column += LANES


def pack_weight(weight, member):
    taps, rows, columns = weight.shape
    shape = jax.ShapeDtypeStruct((4, rows, 14 * LANES), BF16)
    return pl.pallas_call(
        functools.partial(pack_weight_kernel, columns // 3),
        out_shape=(shape, shape),
        in_specs=[pl.BlockSpec(memory_space=pltpu.SMEM)] + in_vmem(1),
        out_specs=tuple(in_vmem(2)),
        compiler_params=params(),
        name="pack_weight",
    )(member, weight)


def place_weight_kernel(split, member_ref, own_ref, y_ref, x_ref, both_ref, first_ref, second_ref):
    for p in range(MEMBERS):
        block = (own_ref, y_ref, x_ref, both_ref)[p // 2][p % 2]
        first_ref[member_ref[0] ^ p] = block[:, :split]
        second_ref[member_ref[0] ^ p] = block[:, split:]


def place_weight(pairs, member, split, *others):
    _, rows, columns = pairs[0].shape
    return pl.pallas_call(
        waiting(functools.partial(place_weight_kernel, split), 5, others),
        out_shape=(
            jax.ShapeDtypeStruct((MEMBERS, rows, split), BF16),
            jax.ShapeDtypeStruct((MEMBERS, rows, columns - split), BF16),
        ),
        in_specs=[pl.BlockSpec(memory_space=pltpu.SMEM)] + in_vmem(4) + unseen(others),
        out_specs=tuple(in_vmem(2)),
        compiler_params=params(),
        name="place_weight",
    )(member, *pairs, *others)


def pick_rows_kernel(member_ref, first_ref, second_ref, even_ref, odd_ref, squares_ref):
    split = first_ref.shape[-1]
    squares = jnp.zeros((first_ref.shape[1], LANES), F32)
    for p in range(MEMBERS):
        for ref in (first_ref, second_ref):
            for i in range(ref.shape[-1] // LANES):
                squares += jnp.square(ref[p, :, pl.ds(i * LANES, LANES)].astype(F32))
    squares_ref[...] = jnp.sum(squares, axis=0, keepdims=True)
    for p in range(MEMBERS):
        out = (even_ref, odd_ref)[p % 2]
        out[p // 2, :, pl.ds(0, split)] = first_ref[member_ref[0] ^ p]
        out[p // 2, :, pl.ds(split, second_ref.shape[-1])] = second_ref[member_ref[0] ^ p]


def pick_rows(first, second, member):
    shape = jax.ShapeDtypeStruct((4, first.shape[1], first.shape[2] + second.shape[2]), BF16)
    return pl.pallas_call(
        pick_rows_kernel,
        out_shape=(shape, shape, jax.ShapeDtypeStruct((1, LANES), F32)),
        in_specs=[pl.BlockSpec(memory_space=pltpu.SMEM)] + in_vmem(2),
        out_specs=tuple(in_vmem(3)),
        compiler_params=params(),
        name="pick_rows",
    )(member, first, second)


def place_gradient_kernel(width, member_ref, *refs):
    rest = sizes(width)[1]
    out_ref = refs[4]
    taps, rows, _ = out_ref.shape
    per_tile = LANES // rest
    lane = lane_index((rows, LANES))
    for p in range(MEMBERS):
        source = member_ref[0] ^ p
        block_ref = refs[p // 2]
        column = 0
        for tile in range(2):
            for tap in range(taps):
                for gate in range(3):
                    start = pl.multiple_of(gate * width + (tile * MEMBERS + source) * LANES, LANES)
                    out_ref[tap, :, pl.ds(start, LANES)] = block_ref[p % 2, :, pl.ds(column, LANES)]
                    column += LANES
                if tile == 0:
                    mixed = block_ref[p % 2, :, pl.ds(column, LANES)].astype(F32)
                    column += LANES
                    for gate in range(3):
                        start = pl.multiple_of(gate * width + (2 * MEMBERS + source // per_tile) * LANES, LANES)
                        first = (source % per_tile) * rest
                        part = pltpu.roll(mixed, lax.rem(first - gate * rest + LANES, LANES), 1)
                        inside = (lane >= first) & (lane < first + rest)
                        old = out_ref[tap, :, pl.ds(start, LANES)].astype(F32)
                        out_ref[tap, :, pl.ds(start, LANES)] = jnp.where(inside, part, old).astype(BF16)


def place_gradient(pairs, member, shape):
    return pl.pallas_call(
        functools.partial(place_gradient_kernel, shape[2] // 3),
        out_shape=jax.ShapeDtypeStruct(shape, BF16),
        in_specs=[pl.BlockSpec(memory_space=pltpu.SMEM)] + in_vmem(4),
        out_specs=pl.BlockSpec(memory_space=pltpu.VMEM),
        compiler_params=params(),
        name="place_gradient",
    )(member, *pairs)


SMALL = 48


def small_rows(width, tokens, biases):
    edge = width // LANES
    keep = edge + tokens // LANES
    bias = keep + -(-biases // LANES)
    return edge, keep, bias, bias + 18


def pack_channels_kernel(width, marks, member_ref, values_ref, small_ref, even_first, odd_first, even_second, odd_second, rows):
    rest = sizes(width)[1]
    per_tile = LANES // rest
    count = values_ref.shape[0]
    tokens = pl.ds(0, count)
    edge, keep, bias, end = marks
    assert end <= SMALL
    for i in range(edge):
        rows[pl.ds(i, 1), :] = small_ref[pl.ds(0, 1), pl.ds(i * LANES, LANES)]
    for i in range(edge, keep):
        rows[pl.ds(i, 1), :] = small_ref[pl.ds(1, 1), pl.ds((i - edge) * LANES, LANES)]
    for i in range(keep, bias):
        rows[pl.ds(i, 1), :] = small_ref[pl.ds(2, 1), pl.ds((i - keep) * LANES, LANES)]
    for i in range(end, SMALL):
        rows[pl.ds(i, 1), :] = jnp.zeros((1, LANES), F32)
    fold = LANES // rest
    folded = pl.ds(count, count // fold)
    lane = lane_index((count // fold, LANES))
    for out in (even_second, odd_second):
        out[:, pl.ds(count, TAIL), :] = jnp.zeros((4, TAIL, LANES), BF16)
    for p in range(MEMBERS):
        first, second = ((even_first, even_second), (odd_first, odd_second))[p % 2]
        to = member_ref[0] ^ p
        for tile, out in enumerate((first, second)):
            start = pl.multiple_of((tile * MEMBERS + to) * LANES, LANES)
            out[p // 2, tokens, pl.ds(0, LANES)] = values_ref[:, pl.ds(start, LANES)]
        start = pl.multiple_of((2 * MEMBERS + to // per_tile) * LANES, LANES)
        part = values_ref[:, pl.ds(start, LANES)].astype(F32)
        total = jnp.zeros((count // fold, LANES), F32)
        for g in range(fold):
            group = pltpu.roll(part[g * (count // fold) : (g + 1) * (count // fold)], lax.rem(LANES + (g - to % per_tile) * rest, LANES), 1)
            total = jnp.where((lane >= g * rest) & (lane < (g + 1) * rest), group, total)
        first[p // 2, folded, :] = total.astype(BF16)
        at = bias
        for vector in (3, 4):
            for tile in range(3):
                start = (tile * MEMBERS + to) * LANES if tile < 2 else (2 * MEMBERS + to // per_tile) * LANES
                value = small_ref[pl.ds(vector, 1), pl.ds(pl.multiple_of(start, LANES), LANES)]
                if tile == 2:
                    value = pltpu.roll(value, lax.rem(LANES - (to % per_tile) * rest, LANES), 1)
                for _ in range(3):
                    piece = value.astype(BF16).astype(F32)
                    rows[pl.ds(at, 1), :] = piece
                    value = value - piece
                    at += 1
        first[p // 2, pl.ds(count + count // fold, SMALL), :] = rows[...].astype(BF16)


def pack_channels(values, small, marks, member, *others):
    rows, width = values.shape
    folded = rows * sizes(width)[1] // LANES
    first = jax.ShapeDtypeStruct((4, rows + folded + SMALL, LANES), BF16)
    second = jax.ShapeDtypeStruct((4, rows + TAIL, LANES), BF16)
    return pl.pallas_call(
        waiting(functools.partial(pack_channels_kernel, width, marks), 3, others),
        out_shape=(first, first, second, second),
        in_specs=[pl.BlockSpec(memory_space=pltpu.SMEM)] + in_vmem(2) + unseen(others),
        out_specs=tuple(in_vmem(4)),
        scratch_shapes=[pltpu.VMEM((SMALL, LANES), F32)],
        compiler_params=params(),
        name="pack_channels",
    )(member, values, small, *others)


def place_channels_kernel(width, member_ref, *refs):
    rest = sizes(width)[1]
    out_ref, tail_ref, all_ref = refs[8:]
    rows, _ = all_ref.shape
    per_tile = LANES // rest
    lane = lane_index((rows, LANES))
    for p in range(MEMBERS):
        source = member_ref[0] ^ p
        for tile in range(2):
            block_ref = refs[4 * tile + p // 2]
            start = pl.multiple_of((tile * MEMBERS + source) * LANES, LANES)
            all_ref[:, pl.ds(start, LANES)] = block_ref[p % 2, :, pl.ds(0, LANES)]
        start = pl.multiple_of((2 * MEMBERS + source // per_tile) * LANES, LANES)
        first = (source % per_tile) * rest
        part = pltpu.roll(refs[p // 2][p % 2, :, pl.ds(LANES, LANES)].astype(F32), first, 1)
        inside = (lane >= first) & (lane < first + rest)
        old = all_ref[:, pl.ds(start, LANES)].astype(F32)
        all_ref[:, pl.ds(start, LANES)] = jnp.where(inside, part, old).astype(BF16)
    out_ref[...] = all_ref[pl.ds(0, rows - TAIL), :]
    tail_ref[...] = all_ref[pl.ds(rows - TAIL, TAIL), :]


def place_channels(pairs, member, width):
    return pl.pallas_call(
        functools.partial(place_channels_kernel, width),
        out_shape=[jax.ShapeDtypeStruct((n, width), BF16) for n in (pairs[0].shape[1] - TAIL, TAIL)],
        in_specs=[pl.BlockSpec(memory_space=pltpu.SMEM)] + in_vmem(8),
        out_specs=in_vmem(2),
        scratch_shapes=[pltpu.VMEM((pairs[0].shape[1], width), BF16)],
        compiler_params=params(),
        name="place_channels",
    )(member, *pairs)


def bias_columns_kernel(width, place_ref, vectors_ref, out_ref, natural):
    rest = sizes(width)[1]
    per_tile = LANES // rest
    tiles = width // LANES
    lane = lane_index((1, LANES))
    for p in range(MEMBERS):
        source = place_ref[0] ^ p
        mixed = vectors_ref[pl.ds(p, 1), pl.ds(3 * LANES, LANES)]
        first = (source % per_tile) * rest
        for gate in range(3):
            natural[pl.ds(gate * tiles + source, 1), :] = vectors_ref[pl.ds(p, 1), pl.ds(gate * LANES, LANES)]
            part = vectors_ref[pl.ds(p, 1), pl.ds((4 + gate) * LANES, LANES)]
            natural[pl.ds(gate * tiles + MEMBERS + source, 1), :] = part
            row = pl.ds(gate * tiles + 2 * MEMBERS + source // per_tile, 1)
            part = pltpu.roll(mixed, lax.rem(first - gate * rest + LANES, LANES), 1)
            inside = (lane >= first) & (lane < first + rest)
            natural[row, :] = jnp.where(inside, part, natural[row, :])
    shift = place_ref[2]
    for i in range(out_ref.shape[0]):
        here = pltpu.roll(natural[pl.ds(place_ref[1] + i, 1), :], lax.rem(LANES - shift, LANES), 1)
        later = pltpu.roll(natural[pl.ds(place_ref[1] + i + 1, 1), :], lax.rem(LANES - shift, LANES), 1)
        out_ref[pl.ds(i, 1), :] = jnp.where(lane < LANES - shift, here, later)


def bias_columns(vectors, here, width, count):
    rows = -(-count // LANES)
    start = here.linear * count
    place = jnp.stack([here.member, start // LANES, start % LANES]).astype(jnp.int32)
    found = pl.pallas_call(
        functools.partial(bias_columns_kernel, width),
        out_shape=jax.ShapeDtypeStruct((rows, LANES), F32),
        in_specs=[pl.BlockSpec(memory_space=pltpu.SMEM)] + in_vmem(1),
        out_specs=pl.BlockSpec(memory_space=pltpu.VMEM),
        scratch_shapes=[pltpu.VMEM((3 * width // LANES + rows + 8, LANES), F32)],
        compiler_params=params(),
        name="bias_columns",
    )(place, vectors)
    return found.reshape(-1)[:count]


UNROLL = 16
GAP = 8


def token_loop(low, high, token, state, reverse):
    def several(i, state):
        for j in range(UNROLL):
            k = high - 1 - (i * UNROLL + j) if reverse else low + i * UNROLL + j
            state = token(k, state)
        return state

    return lax.fori_loop(0, (high - low) // UNROLL, several, state)


def row_block(rows):
    for block in (176, 48, 16):
        if rows % block == 0:
            return block
    return rows


def forward_kernel(tiles, rest, half_steps, *refs):
    gather = half_steps > 0
    x_refs, refs = (refs[:10], refs[10:]) if gather else (refs[:1], refs[1:])
    edge_ref, w_ref, bias_ref, keep_ref, cot_ref, *refs = refs
    if tiles == 2:
        folded_ref, *refs = refs
    act_ref, sum_ref, *refs = refs
    if gather:
        all_ref, *refs = refs
    both, cot_f32, carry, before = refs
    step = pl.program_id(0)
    block = act_ref.shape[0]
    rows = MEMBERS * block
    half = w_ref.shape[1] // 2
    count = half // LANES
    lane = lane_index((MEMBERS, LANES))

    if gather:
        for p in range(6):
            all_ref[p] = x_refs[p][...]

        @pl.when(step < half_steps)
        def _():
            all_ref[6] = x_refs[6][...]
            all_ref[7] = x_refs[7][...]

        @pl.when(step >= half_steps)
        def _():
            all_ref[6] = x_refs[8][...]
            all_ref[7] = x_refs[9][...]

        x = all_ref[...].reshape(rows, all_ref.shape[2])
    else:
        x = x_refs[0][...].reshape(rows, x_refs[0].shape[2])
    result = dot_f32(x, w_ref[...], ((1,), (0,)))
    for p in range(MEMBERS):
        at = pl.ds(p * (block + GAP), block)
        for i in range(2 * count):
            both[i, at, :] = result[p * block : (p + 1) * block, i * LANES : (i + 1) * LANES]
        cot_f32[0, at, :] = cot_ref[p].astype(F32)
        if tiles == 2:
            cot_f32[1, at, :] = pltpu.roll(folded_ref[p].astype(F32), lax.rem(LANES - step * rest, LANES), 1)

    @pl.when(step == 0)
    def _():
        for tile in range(tiles):
            carry[3 * tile] = jnp.ones((MEMBERS, LANES), F32)
            carry[3 * tile + 1] = jnp.zeros((MEMBERS, LANES), F32)
            carry[3 * tile + 2] = jnp.zeros((MEMBERS, LANES), F32)
        edges = dot_f32(edge_ref[...], w_ref[:, pl.ds(half, half)], ((1,), (0,)))
        for i in range(count):
            before[i] = edges[:MEMBERS, i * LANES : (i + 1) * LANES]

    def token(k, state):
        sums, earlier = state
        rows_at = pl.ds(k, MEMBERS, stride=block + GAP)
        keep = keep_ref[k]
        later = tuple(both[count + i, rows_at, :] for i in range(count))
        gates = [
            both[i, rows_at, :] + keep * earlier[i] + bias_ref[:, pl.ds(i * LANES, LANES)]
            for i in range(count)
        ]
        new = []
        outs = []
        for tile in range(tiles):
            if tile == 0:
                z = jnp.tanh(gates[0])
                u = 1.0 / (1.0 + jnp.exp(gates[1] + FORGET_SHIFT))
                o = 1.0 / (1.0 + jnp.exp(-gates[2]))
                outs += [z, u, o]
            else:
                mixed = gates[3]
                z = jnp.tanh(mixed)
                s = 1.0 / (1.0 + jnp.exp(jnp.where(lane < 2 * rest, mixed + FORGET_SHIFT, -mixed)))
                outs += [jnp.where(lane < rest, z, s)]
                u = pltpu.roll(s, LANES - rest, 1)
                o = pltpu.roll(s, LANES - 2 * rest, 1)
            a = keep * (1.0 - u)
            total, local, back = sums[3 * tile : 3 * tile + 3]
            cot = cot_f32[tile, rows_at, :]
            total = total * a
            new += [total, a * local + u * z, back + total * (cot * o)]
        for i, value in enumerate(outs):
            act_ref[k, :, pl.ds(i * LANES, LANES)] = value
        return tuple(new), later

    start = (tuple(carry[i] for i in range(3 * tiles)), tuple(before[i] for i in range(count)))
    sums, earlier = token_loop(0, block, token, start, False)
    for i in range(3 * tiles):
        carry[i] = sums[i]
        sum_ref[i] = sums[i]
    for i in range(count):
        before[i] = earlier[i]


def forward(pieces, edges, w, bias, keep, cot, tiles, rest, *others):
    gather = len(pieces) > 1
    width = w.shape[0]
    length = keep.shape[0]
    tokens = length - TAIL
    block = tokens // 4
    half = w.shape[1] // 2
    assert LANES // rest == 4
    cot_specs = [pl.BlockSpec((MEMBERS, block, LANES), lambda i: (0, i, 0))]
    if tiles == 2:
        cot_specs += [pl.BlockSpec((MEMBERS, block, LANES), lambda i: (0, 4, 0))]
    if gather:
        x_specs = [pl.BlockSpec((block, width), lambda i: (i, 0))] * 6
        x_specs += [pl.BlockSpec((block, width), lambda i: (jnp.minimum(i, 1), 0))] * 2
        x_specs += [pl.BlockSpec((block, width), lambda i: (jnp.maximum(i - 2, 0), 0))] * 2
    else:
        x_specs = [pl.BlockSpec((MEMBERS, block, width), lambda i: (0, i, 0))]
    whole = [jax.ShapeDtypeStruct((MEMBERS, length, width), BF16)] if gather else []
    return pl.pallas_call(
        waiting(
            functools.partial(forward_kernel, tiles, rest, 2 if gather else 0), len(pieces) + 4 + tiles, others
        ),
        grid=(4,),
        out_shape=(
            jax.ShapeDtypeStruct((length, MEMBERS, half), F32),
            jax.ShapeDtypeStruct((3 * tiles, MEMBERS, LANES), F32),
            *whole,
        ),
        in_specs=[
            *x_specs,
            *in_vmem(3),
            pl.BlockSpec((block, MEMBERS, LANES), lambda i: (i, 0, 0)),
            *cot_specs,
            *unseen(others),
        ],
        out_specs=(
            pl.BlockSpec((block, MEMBERS, half), lambda i: (i, 0, 0)),
            pl.BlockSpec((3 * tiles, MEMBERS, LANES), lambda i: (0, 0, 0)),
            *[pl.BlockSpec((MEMBERS, block, width), lambda i: (0, i, 0)) for _ in whole],
        ),
        scratch_shapes=[
            pltpu.VMEM((2 * half // LANES, MEMBERS * (block + GAP), LANES), F32),
            pltpu.VMEM((tiles, MEMBERS * (block + GAP), LANES), F32),
            pltpu.VMEM((3 * tiles, MEMBERS, LANES), F32),
            pltpu.VMEM((half // LANES, MEMBERS, LANES), F32),
        ],
        compiler_params=params(),
        name="forward",
    )(*pieces, edges, w, bias, keep, *[cot] * tiles, *others)


def backward_kernel(
    tiles, rest, blocks, act_ref, keep_ref, enter_ref, arrive_ref, final_ref, cot_ref, folded_ref,
    even_ref, odd_ref, grads_ref, bias_ref, edge_ref, memory, cot_f32, wide, hold, carry, after, unfolded=None,
):
    step = pl.program_id(0)
    block = act_ref.shape[0]
    half = act_ref.shape[2]
    lane = lane_index((MEMBERS, LANES))
    which = jnp.where(step < blocks, step, 2 * blocks - 1 - step)
    base = which * block
    for p in range(MEMBERS):
        cot_f32[pl.ds(p * (block + GAP), block), :] = cot_ref[p].astype(F32)
    count = half // LANES
    top = jnp.where(which == blocks - 1, block - TAIL, block)

    def values(k, tile):
        at = lambda i: act_ref[k, :, pl.ds(i * LANES, LANES)]
        if tile == 0:
            return at(0), at(1), at(2)
        mixed = at(3)
        return mixed, pltpu.roll(mixed, LANES - rest, 1), pltpu.roll(mixed, LANES - 2 * rest, 1)

    if tiles == 2:
        long, short = unfolded.shape[0] // MEMBERS, folded_ref.shape[1]

        @pl.when(step == 0)
        def _():
            for p in range(MEMBERS):
                folded = folded_ref[p].astype(F32)
                for g in range(LANES // rest):
                    part = pltpu.roll(folded, LANES - g * rest, 1) if g else folded
                    unfolded[pl.ds(p * long + g * short, short), :] = part

    @pl.when(step == 0)
    def _():
        for tile in range(tiles):
            memory[0, tile] = enter_ref[tile]
            carry[tile] = enter_ref[tile]

    @pl.when(step < blocks)
    def _():
        def token(k, state):
            keep = keep_ref[k]
            new = []
            for tile in range(tiles):
                z, u, o = values(k, tile)
                m = keep * (1.0 - u) * state[tile] + u * z
                memory[base + k + 1, tile] = m
                hold[tile, pl.ds(k, MEMBERS, stride=block + GAP), :] = o * m
                new.append(m)
            return tuple(new)

        state = token_loop(0, top, token, tuple(carry[t] for t in range(tiles)), False)
        for tile in range(tiles):
            carry[tile] = state[tile]

        @pl.when(which == blocks - 1)
        def _():
            for tile in range(tiles):
                rest_of = final_ref[tile]
                for row in range(3):
                    part = rest_of.astype(BF16).astype(F32)
                    hold[tile, pl.ds(block - TAIL + row, MEMBERS, stride=block + GAP), :] = part
                    rest_of = rest_of - part
                for row in range(3, TAIL):
                    hold[tile, pl.ds(block - TAIL + row, MEMBERS, stride=block + GAP), :] = jnp.zeros_like(part)

        for tile in range(tiles):
            for p in range(MEMBERS):
                part = hold[tile, pl.ds(p * (block + GAP), block), :].astype(BF16)
                (even_ref, odd_ref)[p % 2][p // 2, :, pl.ds(tile * LANES, LANES)] = part

    @pl.when(step == blocks)
    def _():
        for tile in range(tiles):
            carry[tile] = arrive_ref[tile]
        after[...] = jnp.zeros_like(after)
        bias_ref[...] = jnp.zeros_like(bias_ref)

    @pl.when(step >= blocks)
    def _():
        def token(k, state):
            arriving, shifted, totals = state
            rows_at = pl.ds(k, MEMBERS, stride=block + GAP)
            keep = keep_ref[k]
            new, parts = [], []
            for tile in range(tiles):
                z, u, o = values(k, tile)
                f = 1.0 - u
                if tile == 0:
                    cot = cot_f32[rows_at, :]
                else:
                    cot = unfolded[pl.ds(base + k, MEMBERS, stride=long), :]
                held = keep * memory[base + k, tile]
                m = memory[base + k + 1, tile]
                grad = cot * o
                adjoint = grad + arriving[tile]
                new.append(keep * f * adjoint)
                scaled = adjoint * u
                one = [scaled * (1.0 - z * z), scaled * (held - z) * f, grad * m * (1.0 - o)]
                if tile == 1:
                    one = [
                        jnp.where(lane < rest, one[0], jnp.where(lane < 2 * rest, pltpu.roll(one[1], rest, 1), jnp.where(lane < 3 * rest, pltpu.roll(one[2], 2 * rest, 1), 0.0)))
                    ]
                parts += one
            for i, part in enumerate(parts):
                wide[i, rows_at, :] = part
                wide[count + i, rows_at, :] = shifted[i]
            return tuple(new), tuple(keep * part for part in parts), tuple(t + p for t, p in zip(totals, parts))

        state = (
            tuple(carry[t] for t in range(tiles)),
            tuple(after[i] for i in range(count)),
            tuple(bias_ref[:, pl.ds(i * LANES, LANES)] for i in range(count)),
        )
        arriving, shifted, totals = token_loop(0, top, token, state, True)
        for tile in range(tiles):
            carry[tile] = arriving[tile]
        for i in range(count):
            after[i] = shifted[i]
            edge_ref[:, pl.ds(i * LANES, LANES)] = shifted[i]
            bias_ref[:, pl.ds(i * LANES, LANES)] = totals[i]

        @pl.when(which == blocks - 1)
        def _():
            for row in range(block - TAIL, block):
                for i in range(2 * count):
                    wide[i, pl.ds(row, MEMBERS, stride=block + GAP), :] = jnp.zeros((MEMBERS, LANES), F32)

        for i in range(2 * count):
            for p in range(MEMBERS):
                part = wide[i, pl.ds(p * (block + GAP), block), :].astype(BF16)
                grads_ref[p, :, pl.ds(i * LANES, LANES)] = part


def backward(act, keep, cot, enter, arrive, final, tiles, rest, *others):
    length, members, half = act.shape
    block = row_block(length)
    blocks = length // block
    lanes = tiles * LANES
    turn = lambda i: jnp.where(i < blocks, i, 2 * blocks - 1 - i)
    return pl.pallas_call(
        waiting(functools.partial(backward_kernel, tiles, rest, blocks), 7, others),
        grid=(2 * blocks,),
        out_shape=(
            jax.ShapeDtypeStruct((members // 2, length, lanes), BF16),
            jax.ShapeDtypeStruct((members // 2, length, lanes), BF16),
            jax.ShapeDtypeStruct((members, length, 2 * half), BF16),
            jax.ShapeDtypeStruct((members, half), F32),
            jax.ShapeDtypeStruct((members, half), F32),
        ),
        in_specs=[
            pl.BlockSpec((block, members, half), lambda i: (turn(i), 0, 0)),
            pl.BlockSpec((block, members, LANES), lambda i: (turn(i), 0, 0)),
            *in_vmem(3),
            pl.BlockSpec((members, block, LANES), lambda i: (0, turn(i), 0)),
            pl.BlockSpec((members, (length - TAIL) // 4, LANES), lambda i: (0, 4 if tiles == 2 else 0, 0)),
            *unseen(others),
        ],
        out_specs=(
            pl.BlockSpec((members // 2, block, lanes), lambda i: (0, jnp.minimum(i, blocks - 1), 0)),
            pl.BlockSpec((members // 2, block, lanes), lambda i: (0, jnp.minimum(i, blocks - 1), 0)),
            pl.BlockSpec((members, block, 2 * half), lambda i: (0, jnp.minimum(2 * blocks - 1 - i, blocks - 1), 0)),
            pl.BlockSpec((members, half), lambda i: (0, 0)),
            pl.BlockSpec((members, half), lambda i: (0, 0)),
        ),
        scratch_shapes=[
            pltpu.VMEM((length, tiles, members, LANES), F32),
            pltpu.VMEM((members * (block + GAP), LANES), F32),
            pltpu.VMEM((2 * half // LANES, members * (block + GAP), LANES), F32),
            pltpu.VMEM((tiles, members * (block + GAP), LANES), F32),
            pltpu.VMEM((tiles, members, LANES), F32),
            pltpu.VMEM((half // LANES, members, LANES), F32),
            *[pltpu.VMEM((members * (length - TAIL + GAP), LANES), F32) for _ in range(tiles - 1)],
        ],
        compiler_params=params(),
        name="backward",
    )(act, keep, enter, arrive, final, cot, cot, *others)


def input_gradient_kernel(first_ref, second_ref, w_first, w_second, even_ref, odd_ref):
    for p, out in enumerate((even_ref, odd_ref)):
        out[0] = (
            dot_f32(first_ref[p], w_first[...], ((1,), (1,)))
            + dot_f32(second_ref[p], w_second[...], ((1,), (1,)))
        ).astype(BF16)


def input_gradients(first, second, w_first, w_second, start, count, *others):
    _, length, _ = first.shape
    width = w_first.shape[0]
    shape = jax.ShapeDtypeStruct((count, length, width), BF16)
    return pl.pallas_call(
        waiting(input_gradient_kernel, 4, others),
        grid=(3, count),
        out_shape=(shape, shape),
        in_specs=[
            pl.BlockSpec((2, length, first.shape[2]), lambda n, i: (start + i, 0, 0)),
            pl.BlockSpec((2, length, second.shape[2]), lambda n, i: (start + i, 0, 0)),
            pl.BlockSpec((width // 3, first.shape[2]), lambda n, i: (n, 0)),
            pl.BlockSpec((width // 3, second.shape[2]), lambda n, i: (n, 0)),
            *unseen(others),
        ],
        out_specs=(pl.BlockSpec((1, length, width // 3), lambda n, i: (i, 0, n)),) * 2,
        compiler_params=params(),
        name="input_gradient",
    )(first, second, w_first, w_second, *others)


def far_sum_kernel(even_ref, odd_ref, low_ref, high_ref):
    total = even_ref[0].astype(F32) + odd_ref[0].astype(F32)
    middle = low_ref.shape[0]
    low_ref[...] = total[:middle].astype(BF16)
    high_ref[...] = total[middle:].astype(BF16)


def far_sum(even, odd, middle):
    _, length, width = even.shape
    block = 384
    sums = [jax.ShapeDtypeStruct((rows, width), BF16) for rows in (middle, length - middle)]
    spec = pl.BlockSpec((1, length, block), lambda i: (0, 0, i))
    return pl.pallas_call(
        far_sum_kernel,
        grid=(width // block,),
        out_shape=sums,
        in_specs=[spec, spec],
        out_specs=[pl.BlockSpec((rows, block), lambda i: (0, i)) for rows in (middle, length - middle)],
        compiler_params=params(),
        name="far_sum",
    )(even, odd)


def near_sums_kernel(even_ref, odd_ref, low_ref, high_ref, y_low, y_high, x_low, x_high):
    middle, cut = low_ref.shape[0], y_low.shape[0]
    assert cut == middle
    total = even_ref[0].astype(F32) + odd_ref[0].astype(F32)
    first = total[:middle] + low_ref[...].astype(F32)
    y_low[...] = first[:cut].astype(BF16)
    y_high[...] = total[middle:].astype(BF16)
    total = even_ref[1].astype(F32) + odd_ref[1].astype(F32)
    x_low[...] = total[:cut].astype(BF16)
    x_high[...] = (total[middle:] + high_ref[...].astype(F32)).astype(BF16)


def near_sums(even, odd, low, high, cut):
    _, length, width = even.shape
    block = 384
    spec = pl.BlockSpec((2, length, block), lambda i: (0, 0, i))
    halves = [pl.BlockSpec((rows, block), lambda i: (0, i)) for rows in (low.shape[0], high.shape[0])]
    parts = [cut, length - cut]
    return pl.pallas_call(
        near_sums_kernel,
        grid=(width // block,),
        out_shape=[jax.ShapeDtypeStruct((rows, width), BF16) for rows in parts * 2],
        in_specs=[spec, spec] + halves,
        out_specs=[pl.BlockSpec((rows, block), lambda i: (0, i)) for rows in parts * 2],
        compiler_params=params(),
        name="near_sums",
    )(even, odd, low, high)


def last_sum_kernel(even_ref, odd_ref, y_low, x_low, y_high, x_high, next_ref, out_ref):
    middle = y_low.shape[0]
    rows = out_ref.shape[0] - middle
    total = even_ref[0].astype(F32) + odd_ref[0].astype(F32)
    out_ref[pl.ds(0, middle), :] = (total[:middle] + y_low[...].astype(F32) + x_low[...].astype(F32)).astype(BF16)
    high = total[middle : middle + rows] + y_high[pl.ds(0, rows), :].astype(F32) + x_high[pl.ds(0, rows), :].astype(F32)
    row = lax.broadcasted_iota(jnp.int32, high.shape, 0)
    out_ref[pl.ds(middle, rows), :] = jnp.where(row == rows - 1, high + next_ref[...], high).astype(BF16)


def last_sum(even, odd, lows, highs, from_next, tokens):
    _, length, width = even.shape
    block = 384
    spec = pl.BlockSpec((1, length, block), lambda i: (0, 0, i))
    parts = [*lows, *highs, from_next]
    return pl.pallas_call(
        last_sum_kernel,
        grid=(width // block,),
        out_shape=jax.ShapeDtypeStruct((tokens, width), BF16),
        in_specs=[spec, spec] + [pl.BlockSpec((part.shape[0], block), lambda i: (0, i)) for part in parts],
        out_specs=pl.BlockSpec((tokens, block), lambda i: (0, i)),
        compiler_params=params(),
        name="last_sum",
    )(even, odd, *parts)


def adamw(master, gradient, moment_one, moment_two, rate):
    moment_one = BETA_ONE * moment_one + (1.0 - BETA_ONE) * gradient
    moment_two = BETA_TWO * moment_two + (1.0 - BETA_TWO) * gradient * gradient
    step_size = (
        moment_one
        / (1.0 - BETA_ONE**STEP)
        / (jnp.sqrt(moment_two / (1.0 - BETA_TWO**STEP)) + EPSILON)
    )
    return (master - rate * (step_size + DECAY_RATE * master), moment_one, moment_two)


def channel_tiles(vector, member, rest):
    width = vector.shape[-1]
    axis = vector.ndim - 1
    pieces = [
        lax.dynamic_slice_in_dim(vector, member * LANES, LANES, axis),
        lax.dynamic_slice_in_dim(vector, (MEMBERS + member) * LANES, LANES, axis),
        lax.dynamic_slice_in_dim(vector, 2 * MEMBERS * LANES + member * rest, rest, axis),
    ]
    return pieces


def widen(part):
    return jnp.pad(part, [(0, 0)] * (part.ndim - 1) + [(0, LANES - part.shape[-1])])


def on_device(
    inputs,
    boundary,
    start_state,
    weight,
    gate_bias,
    first_weight,
    second_weight,
    first_bias,
    second_bias,
    cotangent,
    final_cotangent,
):
    here = Place()
    tokens, width = inputs.shape[1:]
    rest = sizes(width)[1]
    member = here.member.astype(jnp.int32).reshape(1)
    taps, own_rows, columns = weight.shape
    length = tokens + TAIL
    deep_groups = [[lo + 2 * h for h in range(here.depth)] for lo in range(2)]
    wide_groups = [[jl + 4 * h for h in range(here.wide)] for jl in range(4)]

    weight_pairs = here.pair_up(*pack_weight(weight, member))
    weight_got = here.send_pairs(weight_pairs)

    def all_rows(part):
        cols = part.shape[-1]
        if here.wide > 1:
            part = lax.all_gather(part, "stream", axis=0, axis_index_groups=wide_groups)
            part = part.reshape(here.wide, 2, 4 * own_rows, cols).swapaxes(0, 1)
        part = part.reshape(-1, cols)
        return lax.all_gather(part, "seq", axis=0, tiled=True, axis_index_groups=deep_groups)

    own_bias = gate_bias.shape[0]
    marks = small_rows(width, tokens, own_bias)
    pad_to = lambda row: jnp.pad(row.astype(F32).reshape(1, -1), ((0, 0), (0, width - row.size)))
    small = [inputs[0, -1:].astype(F32), pad_to(1 - boundary[0]), pad_to(gate_bias.astype(BF16))]
    small = jnp.concatenate(small + [start_state, final_cotangent])

    own = inputs[0]
    own_copy = copied(own, weight_pairs[3])
    packed_cot = pack_channels(cotangent[0], small, marks, member, own_copy, weight_pairs[3])
    cot_first = here.pair_up(*packed_cot[:2])
    got_first = here.send_pairs(cot_first)
    placed = place_weight(weight_got, member, 8 * LANES, *cot_first[1:])
    weights = [all_rows(part) for part in placed]
    own_sibling = here.flip(own, 1)
    sent = after(own_copy, *got_first[1:])
    middle = (tokens // 32) * 16
    from_y = here.flip(sent, here.member_mask(2))
    from_x = here.flip(sent, here.member_mask(4))
    low_part, high_part = from_y[:middle], from_x[middle:]
    both_low = here.flip(low_part, here.member_mask(4))
    both_high = here.flip(high_part, here.member_mask(2))
    y_sibling, x_sibling = here.flip(from_y, 1), here.flip(from_x, 1)
    cots = [jnp.concatenate(got_first, axis=0)]
    pieces = [own, own_sibling, from_y, y_sibling, from_x, x_sibling]
    pieces += [both_low, here.flip(both_low, 1), both_high, here.flip(both_high, 1)]

    smalls = cots[0][:, tokens + tokens * rest // LANES :].astype(F32)
    lower = ((jnp.arange(MEMBERS) >> 2) ^ (here.seq % 2)) == 0
    lasts = smalls[:, : marks[0]].reshape(MEMBERS, width).astype(BF16)
    plane = 2 * here.n_stream
    behind = lax.ppermute(lasts, AXES, [(n, n + plane) for n in range(here.count - plane)])
    swap = lambda rows: jnp.concatenate([rows[4:], rows[:4]], axis=0)
    edges = jnp.where(lower[:, None], swap(behind), swap(lasts))
    edges = jnp.pad(edges, ((0, TAIL - MEMBERS), (0, 0)))
    keep = smalls[:, marks[0] : marks[1]].reshape(MEMBERS, tokens).T
    keep = jnp.pad(keep, ((0, TAIL), (0, 0)))
    keep = jnp.broadcast_to(keep[:, :, None], (length, MEMBERS, LANES))
    states = jnp.sum(smalls[:, marks[2] : marks[3]].reshape(MEMBERS, 2, 3, 3, LANES), axis=3)
    starts, finals = ([states[:, i, tile] for tile in range(3)] for i in range(2))
    all_bits = [1 << b for b in range(here.count.bit_length() - 1)]
    bias_all = smalls[:, marks[1] : marks[2]].reshape(1, MEMBERS, -1)[:, :, :own_bias].astype(BF16)
    bias_all = here.gather_flips(bias_all, here.deep_bits + here.wide_bits).astype(F32)
    bias_all = bias_all.reshape(here.wide, here.depth, MEMBERS, own_bias)
    every_member = here.member ^ jnp.arange(MEMBERS)
    bias_all = jnp.take(bias_all, (here.stream // 4) ^ jnp.arange(here.wide), axis=0)
    bias_all = jnp.take(bias_all, here.high ^ jnp.arange(here.depth), axis=1)
    bias_all = jnp.take(bias_all, every_member, axis=2)
    bias_all = bias_all.reshape(here.wide, here.depth, 2, 4, own_bias).transpose(1, 2, 0, 3, 4).reshape(3, width)
    cot_second = here.pair_up(packed_cot[2], after(packed_cot[3], behind))
    got_second = here.send_pairs([after(pair, pieces[7], pieces[9]) for pair in cot_second])
    bias_parts = channel_tiles(bias_all, here.member, rest)
    biases = [
        jnp.concatenate([bias_parts[0].reshape(1, 3 * LANES), widen(bias_parts[2].reshape(1, 3 * rest))], axis=1),
        bias_parts[1].reshape(1, 3 * LANES),
    ]

    def both_halves(value):
        other = jnp.concatenate([value[4:], value[:4]], axis=0)
        mask = lower[:, None]
        return jnp.where(mask, value, other), jnp.where(mask, other, value)

    def back_pairs(first, second, start, count, *others):
        even, odd = input_gradients(first, second, weights[0], weights[1], start, count, *others)
        return even, here.flip(odd, 1)

    halfway = (length // 32) * 16
    gradients, outs, hidden_got = [], [], []
    acts, summaries = [], []
    for chunk in range(2):
        source = [x_all] if chunk else pieces
        act, summary, *whole = forward(source, edges, weights[chunk], biases[chunk], keep, cots[chunk], 2 - chunk, rest)
        acts.append(act)
        summaries.append(summary)
        if whole:
            got_second = [after(got, summary) for got in got_second]
            cots.append(jnp.concatenate(got_second, axis=0))
            behind = jnp.pad(edges[:MEMBERS, None], ((0, 0), (0, TAIL - 1), (0, 0)))
            x_all = lax.dynamic_update_slice(whole[0], behind, (0, tokens, 0))
    both_every = here.gather_flips(jnp.concatenate(summaries)[None], here.deep_bits)

    for chunk in range(2):
        tiles = 2 - chunk
        act = acts[chunk]
        every = both_every[:, :6] if chunk == 0 else both_every[:, 6:]
        enters, arrives, ends = [], [], []
        for tile in range(tiles):
            where = (0, 2, 1)[2 * chunk + tile]
            state, back = starts[where], finals[where]
            enter, arrive = state, back
            for z in range(here.depth):
                part = jnp.take(every, z ^ here.high, axis=0)
                a_low, a_high = both_halves(part[3 * tile])
                b_low, b_high = both_halves(part[3 * tile + 1])
                between = a_low * state + b_low
                enter = jnp.where(z == here.high, jnp.where(lower[:, None], state, between), enter)
                state = a_high * between + b_high
            for z in reversed(range(here.depth)):
                part = jnp.take(every, z ^ here.high, axis=0)
                a_low, a_high = both_halves(part[3 * tile])
                c_low, c_high = both_halves(part[3 * tile + 2])
                between = a_high * back + c_high
                arrive = jnp.where(z == here.high, jnp.where(lower[:, None], between, back), arrive)
                back = a_low * between + c_low
            enters.append(enter)
            arrives.append(arrive)
            ends.append(state)
        others = (outs[0][4],) if chunk else ()
        even, odd, grads, bias_grad, edge_grad = backward(
            act, keep, cots[chunk], jnp.stack(enters), jnp.stack(arrives), jnp.stack(ends), tiles, rest, *others
        )
        half = edge_grad.shape[1]
        edge_grad = jnp.pad(edge_grad.astype(BF16)[:, None], ((0, 0), (0, TAIL - 1), (half, 0)))
        grads = lax.dynamic_update_slice(grads, edge_grad, (0, tokens, 0))
        hidden_got += here.send_pairs(here.pair_up(even, odd))
        if chunk == 1:
            far_low, far_high = far_sum(*back_pairs(outs[0][2], grads, 3, 1, *hidden_got[1:4]), halfway)
            grads = after(grads, far_low, *hidden_got[5:])
        flat = grads.reshape(MEMBERS * length, -1)
        local = dot_f32(x_all.reshape(MEMBERS * length, width), flat, ((0,), (0,))).astype(BF16)
        cols = local.shape[-1]
        local = after(local, gradients[0]) if gradients else local
        summed = lax.psum_scatter(local, "seq", scatter_dimension=0, tiled=True, axis_index_groups=deep_groups)
        if here.wide > 1:
            summed = summed.reshape(2, here.wide, 4 * own_rows, cols).swapaxes(0, 1).reshape(-1, cols)
            summed = lax.psum_scatter(summed, "stream", scatter_dimension=0, tiled=True, axis_index_groups=wide_groups)
        gradients.append(summed.reshape(MEMBERS, own_rows, cols))
        outs.append((even, odd, grads, jnp.sum(bias_grad, axis=0), local))

    low_half = here.flip(far_low, here.member_mask(4))
    high_half = here.flip(far_high, here.member_mask(2))
    grads = outs[0][2], outs[1][2]
    even, odd = back_pairs(*grads, 1, 2, low_half, high_half, outs[1][4], gradients[0])
    y_low, y_high, x_low, x_high = near_sums(even, odd, low_half, high_half, halfway)
    highs = here.flip(y_high, here.member_mask(2)), here.flip(x_high, here.member_mask(4))
    hidden_own, final_rows = place_channels(hidden_got, member, width)
    hidden = hidden_own[None]
    whole_final = jnp.sum(final_rows[:3].astype(F32), axis=0, keepdims=True)
    own_columns = width // here.n_seq
    final_state = lax.dynamic_slice_in_dim(whole_final, here.seq * own_columns, own_columns, 1)
    even, odd = back_pairs(*grads, 0, 1, y_high, hidden_own)
    gradients = [after(gradient, even, *highs) for gradient in gradients]
    *picked, squares = pick_rows(*gradients, member)
    post_pairs = here.pair_up(*picked)
    edge_parts = even[0, tokens : tokens + 1], odd[0, tokens : tokens + 1], *(part[-TAIL : 1 - TAIL] for part in highs)
    edge_sum = sum(part.astype(F32) for part in edge_parts)
    from_next = lax.ppermute(edge_sum, "seq", [(i + 1, i) for i in range(here.n_seq - 1)])
    received = here.send_pairs(post_pairs)

    vector = jnp.concatenate([outs[0][3], outs[1][3], squares[0]]).reshape(1, -1)
    vector = here.sum_flips(after(vector, *post_pairs[1:]), here.deep_bits + here.wide_bits)
    vector = here.gather_flips(vector, here.group_bits[:1])
    vector = after(vector, *received[1:])
    y_low, x_low = after(y_low, *received[1:]), after(x_low, *received[1:])
    lows = here.flip(y_low, here.member_mask(2)), here.flip(x_low, here.member_mask(4))
    from_next = after(from_next, vector)
    input_gradient = last_sum(even, odd, lows, highs, from_next, tokens)[None]
    vectors = [vector] + [here.flip(vector, here.member_mask(2 * i)) for i in (1, 2, 3)]
    vectors = jnp.concatenate(vectors, axis=0)
    gradient_norm = jnp.sqrt(jnp.sum(vectors[:, -LANES:]) + jnp.sum(jnp.square(vectors[:, :-LANES])))
    bias_raw = bias_columns(vectors, here, width, own_bias)

    clip_factor = jnp.minimum(1.0, CLIP_NORM / (gradient_norm + 1e-06))
    raw = place_gradient(received, member, weight.shape)
    weight_gradient = clip_factor * raw.astype(F32)
    bias_gradient = clip_factor * bias_raw
    new_weight, new_first_weight, new_second_weight = adamw(
        weight, weight_gradient, first_weight, second_weight, RATE_WEIGHT
    )
    new_bias, new_first_bias, new_second_bias = adamw(
        gate_bias, bias_gradient, first_bias, second_bias, RATE_BIAS
    )
    return (
        hidden,
        final_state,
        input_gradient,
        weight_gradient,
        bias_gradient,
        gradient_norm,
        new_weight,
        new_first_weight,
        new_second_weight,
        new_bias,
        new_first_bias,
        new_second_bias,
    )


def solution(mesh):
    placed = (
        P("stream", "seq", None),
        P("stream", "seq"),
        P("stream", None),
        P(None, ("seq", "stream"), None),
        P(("seq", "stream")),
        P(None, ("seq", "stream"), None),
        P(None, ("seq", "stream"), None),
        P(("seq", "stream")),
        P(("seq", "stream")),
        P("stream", "seq", None),
        P("stream", None),
    )
    return jax.shard_map(
        on_device,
        mesh=mesh,
        in_specs=placed,
        out_specs=(
            P("stream", "seq", None),
            P("stream", "seq"),
            P("stream", "seq", None),
            P(None, ("seq", "stream"), None),
            P(("seq", "stream")),
            P(),
            P(None, ("seq", "stream"), None),
            P(None, ("seq", "stream"), None),
            P(None, ("seq", "stream"), None),
            P(("seq", "stream")),
            P(("seq", "stream")),
            P(("seq", "stream")),
        ),
        check_vma=False,
    )
```

```python
import functools
import jax
import jax.numpy as jnp
from jax import lax
from jax.experimental import pallas as pl
from jax.experimental.pallas import tpu as pltpu
from jax.sharding import PartitionSpec as P

STEP = 10
BETA_ONE = 0.9
BETA_TWO = 0.95
EPSILON = 1e-08
RATE_WEIGHT = 0.01
RATE_BIAS = 1.0
DECAY_RATE = 0.1
CLIP_NORM = 1.0
FORGET_SHIFT = 6.0

AXES = ("seq", "stream")
LANES = 128
MEMBERS = 8
TAIL = 16
BF16 = jnp.bfloat16
F32 = jnp.float32
VMEM_LIMIT = 60 * 1024 * 1024


def params():
    return pltpu.CompilerParams(vmem_limit_bytes=VMEM_LIMIT)


def in_vmem(count):
    return [pl.BlockSpec(memory_space=pltpu.VMEM)] * count


def dot_f32(a, b, dims):
    return lax.dot_general(a, b, (dims, ((), ())), preferred_element_type=F32)


class Place:
    def __init__(self):
        self.n_seq = lax.axis_size("seq")
        self.n_stream = lax.axis_size("stream")
        self.depth = self.n_seq // 2
        self.wide = self.n_stream // 4
        self.count = self.n_seq * self.n_stream
        self.seq = lax.axis_index("seq")
        self.stream = lax.axis_index("stream")
        self.linear = self.seq * self.n_stream + self.stream
        self.member = (self.seq % 2) * 4 + self.stream % 4
        self.high = self.seq // 2
        self.group_bits = [1, 2, self.n_stream]
        self.deep_bits = [self.n_stream * (2 << b) for b in range(self.depth.bit_length() - 1)]
        self.wide_bits = [4 << b for b in range(self.wide.bit_length() - 1)]

    def flip(self, block, mask):
        return lax.ppermute(block, AXES, [(n, n ^ mask) for n in range(self.count)])

    def member_mask(self, p):
        return (p & 3) | ((p >> 2) * self.n_stream)

    def gather_flips(self, block, bits):
        if len(bits) == 2:
            parts = [self.flip(block, mask) for mask in (bits[0], bits[1], bits[0] | bits[1])]
            return jnp.concatenate([block, *parts], axis=0)
        for bit in bits:
            block = jnp.concatenate([block, self.flip(block, bit)], axis=0)
        return block

    def sum_flips(self, value, bits):
        if len(bits) == 2:
            parts = [self.flip(value, mask) for mask in (bits[0], bits[1], bits[0] | bits[1])]
            return (value + parts[0]) + (parts[1] + parts[2])
        for bit in bits:
            value = value + self.flip(value, bit)
        return value

    def pair_up(self, even, odd):
        sibling = self.flip(odd, 1)
        return [jnp.stack([even[i], sibling[i]]) for i in range(4)]

    def send_pairs(self, pairs):
        return [pairs[0]] + [self.flip(pairs[i], self.member_mask(2 * i)) for i in (1, 2, 3)]

    def exchange(self, even, odd):
        return self.send_pairs(self.pair_up(even, odd))


def after(value, *others):
    return pl.pallas_call(
        lambda *refs: None,
        out_shape=jax.ShapeDtypeStruct(value.shape, value.dtype),
        in_specs=[pl.BlockSpec(memory_space=pl.ANY)] * (1 + len(others)),
        out_specs=pl.BlockSpec(memory_space=pl.ANY),
        input_output_aliases={0: 0},
        name="after",
    )(value, *others)


def copy_kernel(in_ref, out_ref):
    out_ref[...] = in_ref[...]


def copied(value, *others):
    rows, width = value.shape
    spec = pl.BlockSpec((rows // 4, width), lambda i: (i, 0))
    return pl.pallas_call(
        waiting(copy_kernel, 1, others),
        grid=(4,),
        out_shape=jax.ShapeDtypeStruct(value.shape, value.dtype),
        in_specs=[spec, *unseen(others)],
        out_specs=spec,
        name="copied",
    )(value, *others)


def blank(shape, dtype):
    return pl.pallas_call(
        lambda out_ref: None,
        out_shape=jax.ShapeDtypeStruct(shape, dtype),
        out_specs=pl.BlockSpec(memory_space=pl.ANY),
        name="blank",
    )()


def waiting(kernel, operands, others):
    skip = operands + len(others)
    return lambda *refs: kernel(*refs[:operands], *refs[skip:])


def unseen(others):
    return [pl.BlockSpec(memory_space=pl.ANY)] * len(others)


def sizes(width):
    whole = width // (MEMBERS * LANES)
    rest = width // MEMBERS - whole * LANES
    assert whole == 2 and 0 < 3 * rest <= LANES and LANES % rest == 0
    return whole, rest


def lane_index(shape):
    return lax.broadcasted_iota(jnp.int32, shape, len(shape) - 1)


def pack_weight_kernel(width, member_ref, weight_ref, even_ref, odd_ref):
    rest = sizes(width)[1]
    taps, rows, _ = weight_ref.shape
    per_tile = LANES // rest
    lane = lane_index((rows, LANES))
    for p in range(MEMBERS):
        to = member_ref[0] ^ p
        out = (even_ref, odd_ref)[p % 2]
        column = 0
        for tile in range(2):
            for tap in range(taps):
                for gate in range(3):
                    start = pl.multiple_of(gate * width + (tile * MEMBERS + to) * LANES, LANES)
                    out[p // 2, :, pl.ds(column, LANES)] = weight_ref[tap, :, pl.ds(start, LANES)].astype(BF16)
                    column += LANES
                if tile == 0:
                    mixed = jnp.zeros((rows, LANES), F32)
                    for gate in range(3):
                        start = pl.multiple_of(gate * width + (2 * MEMBERS + to // per_tile) * LANES, LANES)
                        part = weight_ref[tap, :, pl.ds(start, LANES)]
                        part = pltpu.roll(part, lax.rem((gate - to % per_tile) * rest + LANES, LANES), 1)
                        inside = (lane >= gate * rest) & (lane < (gate + 1) * rest)
                        mixed = jnp.where(inside, part, mixed)
                    out[p // 2, :, pl.ds(column, LANES)] = mixed.astype(BF16)
                    column += LANES


def pack_weight(weight, member):
    taps, rows, columns = weight.shape
    shape = jax.ShapeDtypeStruct((4, rows, 14 * LANES), BF16)
    return pl.pallas_call(
        functools.partial(pack_weight_kernel, columns // 3),
        out_shape=(shape, shape),
        in_specs=[pl.BlockSpec(memory_space=pltpu.SMEM)] + in_vmem(1),
        out_specs=tuple(in_vmem(2)),
        compiler_params=params(),
        name="pack_weight",
    )(member, weight)


def place_weight_kernel(split, member_ref, own_ref, y_ref, x_ref, both_ref, first_ref, second_ref):
    for p in range(MEMBERS):
        block = (own_ref, y_ref, x_ref, both_ref)[p // 2][p % 2]
        first_ref[member_ref[0] ^ p] = block[:, :split]
        second_ref[member_ref[0] ^ p] = block[:, split:]


def place_weight(pairs, member, split, *others):
    _, rows, columns = pairs[0].shape
    return pl.pallas_call(
        waiting(functools.partial(place_weight_kernel, split), 5, others),
        out_shape=(
            jax.ShapeDtypeStruct((MEMBERS, rows, split), BF16),
            jax.ShapeDtypeStruct((MEMBERS, rows, columns - split), BF16),
        ),
        in_specs=[pl.BlockSpec(memory_space=pltpu.SMEM)] + in_vmem(4) + unseen(others),
        out_specs=tuple(in_vmem(2)),
        compiler_params=params(),
        name="place_weight",
    )(member, *pairs, *others)


def pick_rows_kernel(member_ref, first_ref, second_ref, even_ref, odd_ref, squares_ref):
    split = first_ref.shape[-1]
    squares = jnp.zeros((first_ref.shape[1], LANES), F32)
    for p in range(MEMBERS):
        for ref in (first_ref, second_ref):
            for i in range(ref.shape[-1] // LANES):
                squares += jnp.square(ref[p, :, pl.ds(i * LANES, LANES)].astype(F32))
    squares_ref[...] = jnp.sum(squares, axis=0, keepdims=True)
    for p in range(MEMBERS):
        out = (even_ref, odd_ref)[p % 2]
        out[p // 2, :, pl.ds(0, split)] = first_ref[member_ref[0] ^ p]
        out[p // 2, :, pl.ds(split, second_ref.shape[-1])] = second_ref[member_ref[0] ^ p]


def pick_rows(first, second, member):
    shape = jax.ShapeDtypeStruct((4, first.shape[1], first.shape[2] + second.shape[2]), BF16)
    return pl.pallas_call(
        pick_rows_kernel,
        out_shape=(shape, shape, jax.ShapeDtypeStruct((1, LANES), F32)),
        in_specs=[pl.BlockSpec(memory_space=pltpu.SMEM)] + in_vmem(2),
        out_specs=tuple(in_vmem(3)),
        compiler_params=params(),
        name="pick_rows",
    )(member, first, second)


def place_gradient_kernel(width, member_ref, *refs):
    rest = sizes(width)[1]
    out_ref = refs[4]
    taps, rows, _ = out_ref.shape
    per_tile = LANES // rest
    lane = lane_index((rows, LANES))
    for p in range(MEMBERS):
        source = member_ref[0] ^ p
        block_ref = refs[p // 2]
        column = 0
        for tile in range(2):
            for tap in range(taps):
                for gate in range(3):
                    start = pl.multiple_of(gate * width + (tile * MEMBERS + source) * LANES, LANES)
                    out_ref[tap, :, pl.ds(start, LANES)] = block_ref[p % 2, :, pl.ds(column, LANES)]
                    column += LANES
                if tile == 0:
                    mixed = block_ref[p % 2, :, pl.ds(column, LANES)].astype(F32)
                    column += LANES
                    for gate in range(3):
                        start = pl.multiple_of(gate * width + (2 * MEMBERS + source // per_tile) * LANES, LANES)
                        first = (source % per_tile) * rest
                        part = pltpu.roll(mixed, lax.rem(first - gate * rest + LANES, LANES), 1)
                        inside = (lane >= first) & (lane < first + rest)
                        old = out_ref[tap, :, pl.ds(start, LANES)].astype(F32)
                        out_ref[tap, :, pl.ds(start, LANES)] = jnp.where(inside, part, old).astype(BF16)


def place_gradient(pairs, member, shape):
    return pl.pallas_call(
        functools.partial(place_gradient_kernel, shape[2] // 3),
        out_shape=jax.ShapeDtypeStruct(shape, BF16),
        in_specs=[pl.BlockSpec(memory_space=pltpu.SMEM)] + in_vmem(4),
        out_specs=pl.BlockSpec(memory_space=pltpu.VMEM),
        compiler_params=params(),
        name="place_gradient",
    )(member, *pairs)


SMALL = 48


def small_rows(width, tokens, biases):
    edge = width // LANES
    keep = edge + tokens // LANES
    bias = keep + -(-biases // LANES)
    return edge, keep, bias, bias + 18


def pack_channels_kernel(width, marks, member_ref, values_ref, small_ref, even_first, odd_first, even_second, odd_second, rows):
    rest = sizes(width)[1]
    per_tile = LANES // rest
    count = values_ref.shape[0]
    tokens = pl.ds(0, count)
    edge, keep, bias, end = marks
    assert end <= SMALL
    for i in range(edge):
        rows[pl.ds(i, 1), :] = small_ref[pl.ds(0, 1), pl.ds(i * LANES, LANES)]
    for i in range(edge, keep):
        rows[pl.ds(i, 1), :] = small_ref[pl.ds(1, 1), pl.ds((i - edge) * LANES, LANES)]
    for i in range(keep, bias):
        rows[pl.ds(i, 1), :] = small_ref[pl.ds(2, 1), pl.ds((i - keep) * LANES, LANES)]
    for i in range(end, SMALL):
        rows[pl.ds(i, 1), :] = jnp.zeros((1, LANES), F32)
    fold = LANES // rest
    folded = pl.ds(count, count // fold)
    lane = lane_index((count // fold, LANES))
    for out in (even_second, odd_second):
        out[:, pl.ds(count, TAIL), :] = jnp.zeros((4, TAIL, LANES), BF16)
    for p in range(MEMBERS):
        first, second = ((even_first, even_second), (odd_first, odd_second))[p % 2]
        to = member_ref[0] ^ p
        for tile, out in enumerate((first, second)):
            start = pl.multiple_of((tile * MEMBERS + to) * LANES, LANES)
            out[p // 2, tokens, pl.ds(0, LANES)] = values_ref[:, pl.ds(start, LANES)]
        start = pl.multiple_of((2 * MEMBERS + to // per_tile) * LANES, LANES)
        part = values_ref[:, pl.ds(start, LANES)].astype(F32)
        total = jnp.zeros((count // fold, LANES), F32)
        for g in range(fold):
            group = pltpu.roll(part[g * (count // fold) : (g + 1) * (count // fold)], lax.rem(LANES + (g - to % per_tile) * rest, LANES), 1)
            total = jnp.where((lane >= g * rest) & (lane < (g + 1) * rest), group, total)
        first[p // 2, folded, :] = total.astype(BF16)
        at = bias
        for vector in (3, 4):
            for tile in range(3):
                start = (tile * MEMBERS + to) * LANES if tile < 2 else (2 * MEMBERS + to // per_tile) * LANES
                value = small_ref[pl.ds(vector, 1), pl.ds(pl.multiple_of(start, LANES), LANES)]
                if tile == 2:
                    value = pltpu.roll(value, lax.rem(LANES - (to % per_tile) * rest, LANES), 1)
                for _ in range(3):
                    piece = value.astype(BF16).astype(F32)
                    rows[pl.ds(at, 1), :] = piece
                    value = value - piece
                    at += 1
        first[p // 2, pl.ds(count + count // fold, SMALL), :] = rows[...].astype(BF16)


def pack_channels(values, small, marks, member, *others):
    rows, width = values.shape
    folded = rows * sizes(width)[1] // LANES
    first = jax.ShapeDtypeStruct((4, rows + folded + SMALL, LANES), BF16)
    second = jax.ShapeDtypeStruct((4, rows + TAIL, LANES), BF16)
    return pl.pallas_call(
        waiting(functools.partial(pack_channels_kernel, width, marks), 3, others),
        out_shape=(first, first, second, second),
        in_specs=[pl.BlockSpec(memory_space=pltpu.SMEM)] + in_vmem(2) + unseen(others),
        out_specs=tuple(in_vmem(4)),
        scratch_shapes=[pltpu.VMEM((SMALL, LANES), F32)],
        compiler_params=params(),
        name="pack_channels",
    )(member, values, small, *others)


def place_channels_kernel(width, member_ref, *refs):
    rest = sizes(width)[1]
    out_ref, tail_ref, all_ref = refs[8:]
    rows, _ = all_ref.shape
    per_tile = LANES // rest
    lane = lane_index((rows, LANES))
    for p in range(MEMBERS):
        source = member_ref[0] ^ p
        for tile in range(2):
            block_ref = refs[4 * tile + p // 2]
            start = pl.multiple_of((tile * MEMBERS + source) * LANES, LANES)
            all_ref[:, pl.ds(start, LANES)] = block_ref[p % 2, :, pl.ds(0, LANES)]
        start = pl.multiple_of((2 * MEMBERS + source // per_tile) * LANES, LANES)
        first = (source % per_tile) * rest
        part = pltpu.roll(refs[p // 2][p % 2, :, pl.ds(LANES, LANES)].astype(F32), first, 1)
        inside = (lane >= first) & (lane < first + rest)
        old = all_ref[:, pl.ds(start, LANES)].astype(F32)
        all_ref[:, pl.ds(start, LANES)] = jnp.where(inside, part, old).astype(BF16)
    out_ref[...] = all_ref[pl.ds(0, rows - TAIL), :]
    tail_ref[...] = all_ref[pl.ds(rows - TAIL, TAIL), :]


def place_channels(pairs, member, width):
    return pl.pallas_call(
        functools.partial(place_channels_kernel, width),
        out_shape=[jax.ShapeDtypeStruct((n, width), BF16) for n in (pairs[0].shape[1] - TAIL, TAIL)],
        in_specs=[pl.BlockSpec(memory_space=pltpu.SMEM)] + in_vmem(8),
        out_specs=in_vmem(2),
        scratch_shapes=[pltpu.VMEM((pairs[0].shape[1], width), BF16)],
        compiler_params=params(),
        name="place_channels",
    )(member, *pairs)


def bias_columns_kernel(width, place_ref, vectors_ref, out_ref, natural):
    rest = sizes(width)[1]
    per_tile = LANES // rest
    tiles = width // LANES
    lane = lane_index((1, LANES))
    for p in range(MEMBERS):
        source = place_ref[0] ^ p
        mixed = vectors_ref[pl.ds(p, 1), pl.ds(3 * LANES, LANES)]
        first = (source % per_tile) * rest
        for gate in range(3):
            natural[pl.ds(gate * tiles + source, 1), :] = vectors_ref[pl.ds(p, 1), pl.ds(gate * LANES, LANES)]
            part = vectors_ref[pl.ds(p, 1), pl.ds((4 + gate) * LANES, LANES)]
            natural[pl.ds(gate * tiles + MEMBERS + source, 1), :] = part
            row = pl.ds(gate * tiles + 2 * MEMBERS + source // per_tile, 1)
            part = pltpu.roll(mixed, lax.rem(first - gate * rest + LANES, LANES), 1)
            inside = (lane >= first) & (lane < first + rest)
            natural[row, :] = jnp.where(inside, part, natural[row, :])
    shift = place_ref[2]
    for i in range(out_ref.shape[0]):
        here = pltpu.roll(natural[pl.ds(place_ref[1] + i, 1), :], lax.rem(LANES - shift, LANES), 1)
        later = pltpu.roll(natural[pl.ds(place_ref[1] + i + 1, 1), :], lax.rem(LANES - shift, LANES), 1)
        out_ref[pl.ds(i, 1), :] = jnp.where(lane < LANES - shift, here, later)


def bias_columns(vectors, here, width, count):
    rows = -(-count // LANES)
    start = here.linear * count
    place = jnp.stack([here.member, start // LANES, start % LANES]).astype(jnp.int32)
    found = pl.pallas_call(
        functools.partial(bias_columns_kernel, width),
        out_shape=jax.ShapeDtypeStruct((rows, LANES), F32),
        in_specs=[pl.BlockSpec(memory_space=pltpu.SMEM)] + in_vmem(1),
        out_specs=pl.BlockSpec(memory_space=pltpu.VMEM),
        scratch_shapes=[pltpu.VMEM((3 * width // LANES + rows + 8, LANES), F32)],
        compiler_params=params(),
        name="bias_columns",
    )(place, vectors)
    return found.reshape(-1)[:count]


UNROLL = 16
GAP = 8


def token_loop(low, high, token, state, reverse):
    def several(i, state):
        for j in range(UNROLL):
            k = high - 1 - (i * UNROLL + j) if reverse else low + i * UNROLL + j
            state = token(k, state)
        return state

    return lax.fori_loop(0, (high - low) // UNROLL, several, state)


def row_block(rows):
    for block in (176, 48, 16):
        if rows % block == 0:
            return block
    return rows


def forward_kernel(tiles, rest, half_steps, *refs):
    gather = half_steps > 0
    x_refs, refs = (refs[:10], refs[10:]) if gather else (refs[:1], refs[1:])
    edge_ref, w_ref, bias_ref, keep_ref, cot_ref, *refs = refs
    if tiles == 2:
        folded_ref, *refs = refs
    act_ref, sum_ref, *refs = refs
    if gather:
        all_ref, *refs = refs
    both, cot_f32, carry, before = refs
    step = pl.program_id(0)
    block = act_ref.shape[0]
    rows = MEMBERS * block
    half = w_ref.shape[1] // 2
    count = half // LANES
    lane = lane_index((MEMBERS, LANES))

    if gather:
        for p in range(6):
            all_ref[p] = x_refs[p][...]

        @pl.when(step < half_steps)
        def _():
            all_ref[6] = x_refs[6][...]
            all_ref[7] = x_refs[7][...]

        @pl.when(step >= half_steps)
        def _():
            all_ref[6] = x_refs[8][...]
            all_ref[7] = x_refs[9][...]

        x = all_ref[...].reshape(rows, all_ref.shape[2])
    else:
        x = x_refs[0][...].reshape(rows, x_refs[0].shape[2])
    result = dot_f32(x, w_ref[...], ((1,), (0,)))
    for p in range(MEMBERS):
        at = pl.ds(p * (block + GAP), block)
        for i in range(2 * count):
            both[i, at, :] = result[p * block : (p + 1) * block, i * LANES : (i + 1) * LANES]
        cot_f32[0, at, :] = cot_ref[p].astype(F32)
        if tiles == 2:
            cot_f32[1, at, :] = pltpu.roll(folded_ref[p].astype(F32), lax.rem(LANES - step * rest, LANES), 1)

    @pl.when(step == 0)
    def _():
        for tile in range(tiles):
            carry[3 * tile] = jnp.ones((MEMBERS, LANES), F32)
            carry[3 * tile + 1] = jnp.zeros((MEMBERS, LANES), F32)
            carry[3 * tile + 2] = jnp.zeros((MEMBERS, LANES), F32)
        edges = dot_f32(edge_ref[...], w_ref[:, pl.ds(half, half)], ((1,), (0,)))
        for i in range(count):
            before[i] = edges[:MEMBERS, i * LANES : (i + 1) * LANES]

    def token(k, state):
        sums, earlier = state
        rows_at = pl.ds(k, MEMBERS, stride=block + GAP)
        keep = keep_ref[k]
        later = tuple(both[count + i, rows_at, :] for i in range(count))
        gates = [
            both[i, rows_at, :] + keep * earlier[i] + bias_ref[:, pl.ds(i * LANES, LANES)]
            for i in range(count)
        ]
        new = []
        outs = []
        for tile in range(tiles):
            if tile == 0:
                z = jnp.tanh(gates[0])
                u = 1.0 / (1.0 + jnp.exp(gates[1] + FORGET_SHIFT))
                o = 1.0 / (1.0 + jnp.exp(-gates[2]))
                outs += [z, u, o]
            else:
                mixed = gates[3]
                z = jnp.tanh(mixed)
                s = 1.0 / (1.0 + jnp.exp(jnp.where(lane < 2 * rest, mixed + FORGET_SHIFT, -mixed)))
                outs += [jnp.where(lane < rest, z, s)]
                u = pltpu.roll(s, LANES - rest, 1)
                o = pltpu.roll(s, LANES - 2 * rest, 1)
            a = keep * (1.0 - u)
            total, local, back = sums[3 * tile : 3 * tile + 3]
            cot = cot_f32[tile, rows_at, :]
            total = total * a
            new += [total, a * local + u * z, back + total * (cot * o)]
        for i, value in enumerate(outs):
            act_ref[k, :, pl.ds(i * LANES, LANES)] = value
        return tuple(new), later

    start = (tuple(carry[i] for i in range(3 * tiles)), tuple(before[i] for i in range(count)))
    sums, earlier = token_loop(0, block, token, start, False)
    for i in range(3 * tiles):
        carry[i] = sums[i]
        sum_ref[i] = sums[i]
    for i in range(count):
        before[i] = earlier[i]


def forward(pieces, edges, w, bias, keep, cot, tiles, rest, *others):
    gather = len(pieces) > 1
    width = w.shape[0]
    length = keep.shape[0]
    tokens = length - TAIL
    block = tokens // 4
    half = w.shape[1] // 2
    assert LANES // rest == 4
    cot_specs = [pl.BlockSpec((MEMBERS, block, LANES), lambda i: (0, i, 0))]
    if tiles == 2:
        cot_specs += [pl.BlockSpec((MEMBERS, block, LANES), lambda i: (0, 4, 0))]
    if gather:
        x_specs = [pl.BlockSpec((block, width), lambda i: (i, 0))] * 6
        x_specs += [pl.BlockSpec((block, width), lambda i: (jnp.minimum(i, 1), 0))] * 2
        x_specs += [pl.BlockSpec((block, width), lambda i: (jnp.maximum(i - 2, 0), 0))] * 2
    else:
        x_specs = [pl.BlockSpec((MEMBERS, block, width), lambda i: (0, i, 0))]
    whole = [jax.ShapeDtypeStruct((MEMBERS, length, width), BF16)] if gather else []
    return pl.pallas_call(
        waiting(
            functools.partial(forward_kernel, tiles, rest, 2 if gather else 0), len(pieces) + 4 + tiles, others
        ),
        grid=(4,),
        out_shape=(
            jax.ShapeDtypeStruct((length, MEMBERS, half), F32),
            jax.ShapeDtypeStruct((3 * tiles, MEMBERS, LANES), F32),
            *whole,
        ),
        in_specs=[
            *x_specs,
            *in_vmem(3),
            pl.BlockSpec((block, MEMBERS, LANES), lambda i: (i, 0, 0)),
            *cot_specs,
            *unseen(others),
        ],
        out_specs=(
            pl.BlockSpec((block, MEMBERS, half), lambda i: (i, 0, 0)),
            pl.BlockSpec((3 * tiles, MEMBERS, LANES), lambda i: (0, 0, 0)),
            *[pl.BlockSpec((MEMBERS, block, width), lambda i: (0, i, 0)) for _ in whole],
        ),
        scratch_shapes=[
            pltpu.VMEM((2 * half // LANES, MEMBERS * (block + GAP), LANES), F32),
            pltpu.VMEM((tiles, MEMBERS * (block + GAP), LANES), F32),
            pltpu.VMEM((3 * tiles, MEMBERS, LANES), F32),
            pltpu.VMEM((half // LANES, MEMBERS, LANES), F32),
        ],
        compiler_params=params(),
        name="forward",
    )(*pieces, edges, w, bias, keep, *[cot] * tiles, *others)


def backward_kernel(
    tiles, rest, blocks, act_ref, keep_ref, enter_ref, arrive_ref, final_ref, cot_ref, folded_ref,
    even_ref, odd_ref, grads_ref, bias_ref, edge_ref, memory, cot_f32, wide, hold, carry, after, unfolded=None,
):
    step = pl.program_id(0)
    block = act_ref.shape[0]
    half = act_ref.shape[2]
    lane = lane_index((MEMBERS, LANES))
    which = jnp.where(step < blocks, step, 2 * blocks - 1 - step)
    base = which * block
    for p in range(MEMBERS):
        cot_f32[pl.ds(p * (block + GAP), block), :] = cot_ref[p].astype(F32)
    count = half // LANES
    top = jnp.where(which == blocks - 1, block - TAIL, block)

    def values(k, tile):
        at = lambda i: act_ref[k, :, pl.ds(i * LANES, LANES)]
        if tile == 0:
            return at(0), at(1), at(2)
        mixed = at(3)
        return mixed, pltpu.roll(mixed, LANES - rest, 1), pltpu.roll(mixed, LANES - 2 * rest, 1)

    if tiles == 2:
        long, short = unfolded.shape[0] // MEMBERS, folded_ref.shape[1]

        @pl.when(step == 0)
        def _():
            for p in range(MEMBERS):
                folded = folded_ref[p].astype(F32)
                for g in range(LANES // rest):
                    part = pltpu.roll(folded, LANES - g * rest, 1) if g else folded
                    unfolded[pl.ds(p * long + g * short, short), :] = part

    @pl.when(step == 0)
    def _():
        for tile in range(tiles):
            memory[0, tile] = enter_ref[tile]
            carry[tile] = enter_ref[tile]

    @pl.when(step < blocks)
    def _():
        def token(k, state):
            keep = keep_ref[k]
            new = []
            for tile in range(tiles):
                z, u, o = values(k, tile)
                m = keep * (1.0 - u) * state[tile] + u * z
                memory[base + k + 1, tile] = m
                hold[tile, pl.ds(k, MEMBERS, stride=block + GAP), :] = o * m
                new.append(m)
            return tuple(new)

        state = token_loop(0, top, token, tuple(carry[t] for t in range(tiles)), False)
        for tile in range(tiles):
            carry[tile] = state[tile]

        @pl.when(which == blocks - 1)
        def _():
            for tile in range(tiles):
                rest_of = final_ref[tile]
                for row in range(3):
                    part = rest_of.astype(BF16).astype(F32)
                    hold[tile, pl.ds(block - TAIL + row, MEMBERS, stride=block + GAP), :] = part
                    rest_of = rest_of - part
                for row in range(3, TAIL):
                    hold[tile, pl.ds(block - TAIL + row, MEMBERS, stride=block + GAP), :] = jnp.zeros_like(part)

        for tile in range(tiles):
            for p in range(MEMBERS):
                part = hold[tile, pl.ds(p * (block + GAP), block), :].astype(BF16)
                (even_ref, odd_ref)[p % 2][p // 2, :, pl.ds(tile * LANES, LANES)] = part

    @pl.when(step == blocks)
    def _():
        for tile in range(tiles):
            carry[tile] = arrive_ref[tile]
        after[...] = jnp.zeros_like(after)
        bias_ref[...] = jnp.zeros_like(bias_ref)

    @pl.when(step >= blocks)
    def _():
        def token(k, state):
            arriving, shifted, totals = state
            rows_at = pl.ds(k, MEMBERS, stride=block + GAP)
            keep = keep_ref[k]
            new, parts = [], []
            for tile in range(tiles):
                z, u, o = values(k, tile)
                f = 1.0 - u
                if tile == 0:
                    cot = cot_f32[rows_at, :]
                else:
                    cot = unfolded[pl.ds(base + k, MEMBERS, stride=long), :]
                held = keep * memory[base + k, tile]
                m = memory[base + k + 1, tile]
                grad = cot * o
                adjoint = grad + arriving[tile]
                new.append(keep * f * adjoint)
                scaled = adjoint * u
                one = [scaled * (1.0 - z * z), scaled * (held - z) * f, grad * m * (1.0 - o)]
                if tile == 1:
                    one = [
                        jnp.where(lane < rest, one[0], jnp.where(lane < 2 * rest, pltpu.roll(one[1], rest, 1), jnp.where(lane < 3 * rest, pltpu.roll(one[2], 2 * rest, 1), 0.0)))
                    ]
                parts += one
            for i, part in enumerate(parts):
                wide[i, rows_at, :] = part
                wide[count + i, rows_at, :] = shifted[i]
            return tuple(new), tuple(keep * part for part in parts), tuple(t + p for t, p in zip(totals, parts))

        state = (
            tuple(carry[t] for t in range(tiles)),
            tuple(after[i] for i in range(count)),
            tuple(bias_ref[:, pl.ds(i * LANES, LANES)] for i in range(count)),
        )
        arriving, shifted, totals = token_loop(0, top, token, state, True)
        for tile in range(tiles):
            carry[tile] = arriving[tile]
        for i in range(count):
            after[i] = shifted[i]
            edge_ref[:, pl.ds(i * LANES, LANES)] = shifted[i]
            bias_ref[:, pl.ds(i * LANES, LANES)] = totals[i]

        @pl.when(which == blocks - 1)
        def _():
            for row in range(block - TAIL, block):
                for i in range(2 * count):
                    wide[i, pl.ds(row, MEMBERS, stride=block + GAP), :] = jnp.zeros((MEMBERS, LANES), F32)

        for i in range(2 * count):
            for p in range(MEMBERS):
                part = wide[i, pl.ds(p * (block + GAP), block), :].astype(BF16)
                grads_ref[p, :, pl.ds(i * LANES, LANES)] = part


def backward(act, keep, cot, enter, arrive, final, tiles, rest, *others):
    length, members, half = act.shape
    block = row_block(length)
    blocks = length // block
    lanes = tiles * LANES
    turn = lambda i: jnp.where(i < blocks, i, 2 * blocks - 1 - i)
    return pl.pallas_call(
        waiting(functools.partial(backward_kernel, tiles, rest, blocks), 7, others),
        grid=(2 * blocks,),
        out_shape=(
            jax.ShapeDtypeStruct((members // 2, length, lanes), BF16),
            jax.ShapeDtypeStruct((members // 2, length, lanes), BF16),
            jax.ShapeDtypeStruct((members, length, 2 * half), BF16),
            jax.ShapeDtypeStruct((members, half), F32),
            jax.ShapeDtypeStruct((members, half), F32),
        ),
        in_specs=[
            pl.BlockSpec((block, members, half), lambda i: (turn(i), 0, 0)),
            pl.BlockSpec((block, members, LANES), lambda i: (turn(i), 0, 0)),
            *in_vmem(3),
            pl.BlockSpec((members, block, LANES), lambda i: (0, turn(i), 0)),
            pl.BlockSpec((members, (length - TAIL) // 4, LANES), lambda i: (0, 4 if tiles == 2 else 0, 0)),
            *unseen(others),
        ],
        out_specs=(
            pl.BlockSpec((members // 2, block, lanes), lambda i: (0, jnp.minimum(i, blocks - 1), 0)),
            pl.BlockSpec((members // 2, block, lanes), lambda i: (0, jnp.minimum(i, blocks - 1), 0)),
            pl.BlockSpec((members, block, 2 * half), lambda i: (0, jnp.minimum(2 * blocks - 1 - i, blocks - 1), 0)),
            pl.BlockSpec((members, half), lambda i: (0, 0)),
            pl.BlockSpec((members, half), lambda i: (0, 0)),
        ),
        scratch_shapes=[
            pltpu.VMEM((length, tiles, members, LANES), F32),
            pltpu.VMEM((members * (block + GAP), LANES), F32),
            pltpu.VMEM((2 * half // LANES, members * (block + GAP), LANES), F32),
            pltpu.VMEM((tiles, members * (block + GAP), LANES), F32),
            pltpu.VMEM((tiles, members, LANES), F32),
            pltpu.VMEM((half // LANES, members, LANES), F32),
            *[pltpu.VMEM((members * (length - TAIL + GAP), LANES), F32) for _ in range(tiles - 1)],
        ],
        compiler_params=params(),
        name="backward",
    )(act, keep, enter, arrive, final, cot, cot, *others)


def input_gradient_kernel(first_ref, second_ref, w_first, w_second, even_ref, odd_ref):
    for p, out in enumerate((even_ref, odd_ref)):
        out[0] = (
            dot_f32(first_ref[p], w_first[...], ((1,), (1,)))
            + dot_f32(second_ref[p], w_second[...], ((1,), (1,)))
        ).astype(BF16)


def input_gradients(first, second, w_first, w_second, start, count, *others):
    _, length, _ = first.shape
    width = w_first.shape[0]
    shape = jax.ShapeDtypeStruct((count, length, width), BF16)
    return pl.pallas_call(
        waiting(input_gradient_kernel, 4, others),
        grid=(3, count),
        out_shape=(shape, shape),
        in_specs=[
            pl.BlockSpec((2, length, first.shape[2]), lambda n, i: (start + i, 0, 0)),
            pl.BlockSpec((2, length, second.shape[2]), lambda n, i: (start + i, 0, 0)),
            pl.BlockSpec((width // 3, first.shape[2]), lambda n, i: (n, 0)),
            pl.BlockSpec((width // 3, second.shape[2]), lambda n, i: (n, 0)),
            *unseen(others),
        ],
        out_specs=(pl.BlockSpec((1, length, width // 3), lambda n, i: (i, 0, n)),) * 2,
        compiler_params=params(),
        name="input_gradient",
    )(first, second, w_first, w_second, *others)


def far_sum_kernel(even_ref, odd_ref, low_ref, high_ref):
    total = even_ref[0].astype(F32) + odd_ref[0].astype(F32)
    middle = low_ref.shape[0]
    low_ref[...] = total[:middle].astype(BF16)
    high_ref[...] = total[middle:].astype(BF16)


def far_sum(even, odd, middle):
    _, length, width = even.shape
    block = 384
    sums = [jax.ShapeDtypeStruct((rows, width), BF16) for rows in (middle, length - middle)]
    spec = pl.BlockSpec((1, length, block), lambda i: (0, 0, i))
    return pl.pallas_call(
        far_sum_kernel,
        grid=(width // block,),
        out_shape=sums,
        in_specs=[spec, spec],
        out_specs=[pl.BlockSpec((rows, block), lambda i: (0, i)) for rows in (middle, length - middle)],
        compiler_params=params(),
        name="far_sum",
    )(even, odd)


def near_sums_kernel(even_ref, odd_ref, low_ref, high_ref, y_low, y_high, x_low, x_high):
    middle, cut = low_ref.shape[0], y_low.shape[0]
    assert cut == middle
    total = even_ref[0].astype(F32) + odd_ref[0].astype(F32)
    first = total[:middle] + low_ref[...].astype(F32)
    y_low[...] = first[:cut].astype(BF16)
    y_high[...] = total[middle:].astype(BF16)
    total = even_ref[1].astype(F32) + odd_ref[1].astype(F32)
    x_low[...] = total[:cut].astype(BF16)
    x_high[...] = (total[middle:] + high_ref[...].astype(F32)).astype(BF16)


def near_sums(even, odd, low, high, cut):
    _, length, width = even.shape
    block = 384
    spec = pl.BlockSpec((2, length, block), lambda i: (0, 0, i))
    halves = [pl.BlockSpec((rows, block), lambda i: (0, i)) for rows in (low.shape[0], high.shape[0])]
    parts = [cut, length - cut]
    return pl.pallas_call(
        near_sums_kernel,
        grid=(width // block,),
        out_shape=[jax.ShapeDtypeStruct((rows, width), BF16) for rows in parts * 2],
        in_specs=[spec, spec] + halves,
        out_specs=[pl.BlockSpec((rows, block), lambda i: (0, i)) for rows in parts * 2],
        compiler_params=params(),
        name="near_sums",
    )(even, odd, low, high)


def high_sum_kernel(even_ref, odd_ref, y_high, x_high, next_ref, out_ref):
    rows = out_ref.shape[0]
    here = pl.ds(rows, rows)
    total = even_ref[0, here, :].astype(F32) + odd_ref[0, here, :].astype(F32)
    total = total + y_high[pl.ds(0, rows), :].astype(F32) + x_high[pl.ds(0, rows), :].astype(F32)
    row = lax.broadcasted_iota(jnp.int32, total.shape, 0)
    out_ref[...] = jnp.where(row == rows - 1, total + next_ref[...], total).astype(BF16)


def low_sum_kernel(even_ref, odd_ref, y_low, x_low, _, out_ref):
    total = even_ref[0].astype(F32) + odd_ref[0].astype(F32)
    out_ref[...] = (total + y_low[...].astype(F32) + x_low[...].astype(F32)).astype(BF16)


def last_sum(even, odd, lows, highs, from_next, tokens):
    _, length, width = even.shape
    block, rows = 384, tokens // 2
    assert lows[0].shape[0] == rows
    shape = jax.ShapeDtypeStruct((tokens, width), BF16)
    columns = lambda part: pl.BlockSpec((part.shape[0], block), lambda i: (0, i))
    whole = pl.BlockSpec((1, length, block), lambda i: (0, 0, i))
    half = pl.BlockSpec((1, rows, block), lambda i: (0, 0, i))
    done = pl.pallas_call(
        high_sum_kernel,
        grid=(width // block,),
        out_shape=shape,
        in_specs=[whole, whole, *map(columns, (*highs, from_next))],
        out_specs=pl.BlockSpec((rows, block), lambda i: (1, i)),
        compiler_params=params(),
        name="high_sum",
    )(even, odd, *highs, from_next)
    return pl.pallas_call(
        low_sum_kernel,
        grid=(width // block,),
        out_shape=shape,
        in_specs=[half, half, *map(columns, lows), pl.BlockSpec(memory_space=pl.ANY)],
        out_specs=pl.BlockSpec((rows, block), lambda i: (0, i)),
        input_output_aliases={4: 0},
        compiler_params=params(),
        name="low_sum",
    )(even, odd, *lows, done)


def adamw(master, gradient, moment_one, moment_two, rate):
    moment_one = BETA_ONE * moment_one + (1.0 - BETA_ONE) * gradient
    moment_two = BETA_TWO * moment_two + (1.0 - BETA_TWO) * gradient * gradient
    step_size = (
        moment_one
        / (1.0 - BETA_ONE**STEP)
        / (jnp.sqrt(moment_two / (1.0 - BETA_TWO**STEP)) + EPSILON)
    )
    return (master - rate * (step_size + DECAY_RATE * master), moment_one, moment_two)


def channel_tiles(vector, member, rest):
    width = vector.shape[-1]
    axis = vector.ndim - 1
    pieces = [
        lax.dynamic_slice_in_dim(vector, member * LANES, LANES, axis),
        lax.dynamic_slice_in_dim(vector, (MEMBERS + member) * LANES, LANES, axis),
        lax.dynamic_slice_in_dim(vector, 2 * MEMBERS * LANES + member * rest, rest, axis),
    ]
    return pieces


def widen(part):
    return jnp.pad(part, [(0, 0)] * (part.ndim - 1) + [(0, LANES - part.shape[-1])])


def on_device(
    inputs,
    boundary,
    start_state,
    weight,
    gate_bias,
    first_weight,
    second_weight,
    first_bias,
    second_bias,
    cotangent,
    final_cotangent,
):
    here = Place()
    tokens, width = inputs.shape[1:]
    rest = sizes(width)[1]
    member = here.member.astype(jnp.int32).reshape(1)
    taps, own_rows, columns = weight.shape
    length = tokens + TAIL
    deep_groups = [[lo + 2 * h for h in range(here.depth)] for lo in range(2)]
    wide_groups = [[jl + 4 * h for h in range(here.wide)] for jl in range(4)]

    weight_pairs = here.pair_up(*pack_weight(weight, member))
    weight_got = here.send_pairs(weight_pairs)

    def all_rows(part):
        cols = part.shape[-1]
        if here.wide > 1:
            part = lax.all_gather(part, "stream", axis=0, axis_index_groups=wide_groups)
            part = part.reshape(here.wide, 2, 4 * own_rows, cols).swapaxes(0, 1)
        part = part.reshape(-1, cols)
        return lax.all_gather(part, "seq", axis=0, tiled=True, axis_index_groups=deep_groups)

    own_bias = gate_bias.shape[0]
    marks = small_rows(width, tokens, own_bias)
    pad_to = lambda row: jnp.pad(row.astype(F32).reshape(1, -1), ((0, 0), (0, width - row.size)))
    small = [inputs[0, -1:].astype(F32), pad_to(1 - boundary[0]), pad_to(gate_bias.astype(BF16))]
    small = jnp.concatenate(small + [start_state, final_cotangent])

    own = inputs[0]
    own_copy = copied(own, weight_pairs[3])
    packed_cot = pack_channels(cotangent[0], small, marks, member, own_copy, weight_pairs[3])
    cot_first = here.pair_up(*packed_cot[:2])
    got_first = here.send_pairs(cot_first)
    placed = place_weight(weight_got, member, 8 * LANES, *cot_first[1:])
    weights = [all_rows(part) for part in placed]
    own_sibling = here.flip(own, 1)
    sent = after(own_copy, *got_first[1:])
    middle = (tokens // 32) * 16
    from_y = here.flip(sent, here.member_mask(2))
    from_x = here.flip(sent, here.member_mask(4))
    low_part, high_part = from_y[:middle], from_x[middle:]
    both_low = here.flip(low_part, here.member_mask(4))
    both_high = here.flip(high_part, here.member_mask(2))
    y_sibling, x_sibling = here.flip(from_y, 1), here.flip(from_x, 1)
    cots = [jnp.concatenate(got_first, axis=0)]
    pieces = [own, own_sibling, from_y, y_sibling, from_x, x_sibling]
    pieces += [both_low, here.flip(both_low, 1), both_high, here.flip(both_high, 1)]

    smalls = cots[0][:, tokens + tokens * rest // LANES :].astype(F32)
    lower = ((jnp.arange(MEMBERS) >> 2) ^ (here.seq % 2)) == 0
    lasts = smalls[:, : marks[0]].reshape(MEMBERS, width).astype(BF16)
    plane = 2 * here.n_stream
    behind = lax.ppermute(lasts, AXES, [(n, n + plane) for n in range(here.count - plane)])
    swap = lambda rows: jnp.concatenate([rows[4:], rows[:4]], axis=0)
    edges = jnp.where(lower[:, None], swap(behind), swap(lasts))
    edges = jnp.pad(edges, ((0, TAIL - MEMBERS), (0, 0)))
    keep = smalls[:, marks[0] : marks[1]].reshape(MEMBERS, tokens).T
    keep = jnp.pad(keep, ((0, TAIL), (0, 0)))
    keep = jnp.broadcast_to(keep[:, :, None], (length, MEMBERS, LANES))
    states = jnp.sum(smalls[:, marks[2] : marks[3]].reshape(MEMBERS, 2, 3, 3, LANES), axis=3)
    starts, finals = ([states[:, i, tile] for tile in range(3)] for i in range(2))
    all_bits = [1 << b for b in range(here.count.bit_length() - 1)]
    bias_all = smalls[:, marks[1] : marks[2]].reshape(1, MEMBERS, -1)[:, :, :own_bias].astype(BF16)
    bias_all = here.gather_flips(bias_all, here.deep_bits + here.wide_bits).astype(F32)
    bias_all = bias_all.reshape(here.wide, here.depth, MEMBERS, own_bias)
    every_member = here.member ^ jnp.arange(MEMBERS)
    bias_all = jnp.take(bias_all, (here.stream // 4) ^ jnp.arange(here.wide), axis=0)
    bias_all = jnp.take(bias_all, here.high ^ jnp.arange(here.depth), axis=1)
    bias_all = jnp.take(bias_all, every_member, axis=2)
    bias_all = bias_all.reshape(here.wide, here.depth, 2, 4, own_bias).transpose(1, 2, 0, 3, 4).reshape(3, width)
    cot_second = here.pair_up(packed_cot[2], after(packed_cot[3], behind))
    got_second = here.send_pairs([after(pair, pieces[7], pieces[9]) for pair in cot_second])
    bias_parts = channel_tiles(bias_all, here.member, rest)
    biases = [
        jnp.concatenate([bias_parts[0].reshape(1, 3 * LANES), widen(bias_parts[2].reshape(1, 3 * rest))], axis=1),
        bias_parts[1].reshape(1, 3 * LANES),
    ]

    def both_halves(value):
        other = jnp.concatenate([value[4:], value[:4]], axis=0)
        mask = lower[:, None]
        return jnp.where(mask, value, other), jnp.where(mask, other, value)

    def back_pairs(first, second, start, count, *others):
        even, odd = input_gradients(first, second, weights[0], weights[1], start, count, *others)
        return even, here.flip(odd, 1)

    halfway = (length // 32) * 16
    gradients, outs, hidden_got = [], [], []
    acts, summaries = [], []
    for chunk in range(2):
        source = [x_all] if chunk else pieces
        act, summary, *whole = forward(source, edges, weights[chunk], biases[chunk], keep, cots[chunk], 2 - chunk, rest)
        acts.append(act)
        summaries.append(summary)
        if whole:
            got_second = [after(got, summary) for got in got_second]
            cots.append(jnp.concatenate(got_second, axis=0))
            behind = jnp.pad(edges[:MEMBERS, None], ((0, 0), (0, TAIL - 1), (0, 0)))
            x_all = lax.dynamic_update_slice(whole[0], behind, (0, tokens, 0))
    both_every = here.gather_flips(jnp.concatenate(summaries)[None], here.deep_bits)

    for chunk in range(2):
        tiles = 2 - chunk
        act = acts[chunk]
        every = both_every[:, :6] if chunk == 0 else both_every[:, 6:]
        enters, arrives, ends = [], [], []
        for tile in range(tiles):
            where = (0, 2, 1)[2 * chunk + tile]
            state, back = starts[where], finals[where]
            enter, arrive = state, back
            for z in range(here.depth):
                part = jnp.take(every, z ^ here.high, axis=0)
                a_low, a_high = both_halves(part[3 * tile])
                b_low, b_high = both_halves(part[3 * tile + 1])
                between = a_low * state + b_low
                enter = jnp.where(z == here.high, jnp.where(lower[:, None], state, between), enter)
                state = a_high * between + b_high
            for z in reversed(range(here.depth)):
                part = jnp.take(every, z ^ here.high, axis=0)
                a_low, a_high = both_halves(part[3 * tile])
                c_low, c_high = both_halves(part[3 * tile + 2])
                between = a_high * back + c_high
                arrive = jnp.where(z == here.high, jnp.where(lower[:, None], between, back), arrive)
                back = a_low * between + c_low
            enters.append(enter)
            arrives.append(arrive)
            ends.append(state)
        others = (outs[0][4],) if chunk else ()
        even, odd, grads, bias_grad, edge_grad = backward(
            act, keep, cots[chunk], jnp.stack(enters), jnp.stack(arrives), jnp.stack(ends), tiles, rest, *others
        )
        half = edge_grad.shape[1]
        edge_grad = jnp.pad(edge_grad.astype(BF16)[:, None], ((0, 0), (0, TAIL - 1), (half, 0)))
        grads = lax.dynamic_update_slice(grads, edge_grad, (0, tokens, 0))
        hidden_got += here.send_pairs(here.pair_up(even, odd))
        if chunk == 1:
            far_low, far_high = far_sum(*back_pairs(outs[0][2], grads, 3, 1, *hidden_got[1:4]), halfway)
            grads = after(grads, far_low, *hidden_got[5:])
        flat = grads.reshape(MEMBERS * length, -1)
        local = dot_f32(x_all.reshape(MEMBERS * length, width), flat, ((0,), (0,))).astype(BF16)
        cols = local.shape[-1]
        local = after(local, gradients[0]) if gradients else local
        summed = lax.psum_scatter(local, "seq", scatter_dimension=0, tiled=True, axis_index_groups=deep_groups)
        if here.wide > 1:
            summed = summed.reshape(2, here.wide, 4 * own_rows, cols).swapaxes(0, 1).reshape(-1, cols)
            summed = lax.psum_scatter(summed, "stream", scatter_dimension=0, tiled=True, axis_index_groups=wide_groups)
        gradients.append(summed.reshape(MEMBERS, own_rows, cols))
        outs.append((even, odd, grads, jnp.sum(bias_grad, axis=0), local))

    low_half = here.flip(far_low, here.member_mask(4))
    high_half = here.flip(far_high, here.member_mask(2))
    grads = outs[0][2], outs[1][2]
    even, odd = back_pairs(*grads, 1, 2, low_half, high_half, outs[1][4], gradients[0])
    y_low, y_high, x_low, x_high = near_sums(even, odd, low_half, high_half, halfway)
    highs = here.flip(y_high, here.member_mask(2)), here.flip(x_high, here.member_mask(4))
    hidden_own, final_rows = place_channels(hidden_got, member, width)
    hidden = hidden_own[None]
    whole_final = jnp.sum(final_rows[:3].astype(F32), axis=0, keepdims=True)
    own_columns = width // here.n_seq
    final_state = lax.dynamic_slice_in_dim(whole_final, here.seq * own_columns, own_columns, 1)
    even, odd = back_pairs(*grads, 0, 1, y_high, hidden_own)
    gradients = [after(gradient, even, *highs) for gradient in gradients]
    *picked, squares = pick_rows(*gradients, member)
    post_pairs = here.pair_up(*picked)
    edge_parts = even[0, tokens : tokens + 1], odd[0, tokens : tokens + 1], *(part[-TAIL : 1 - TAIL] for part in highs)
    edge_sum = sum(part.astype(F32) for part in edge_parts)
    from_next = lax.ppermute(edge_sum, "seq", [(i + 1, i) for i in range(here.n_seq - 1)])
    received = here.send_pairs(post_pairs)

    vector = jnp.concatenate([outs[0][3], outs[1][3], squares[0]]).reshape(1, -1)
    vector = here.sum_flips(after(vector, *post_pairs[1:]), here.deep_bits + here.wide_bits)
    vector = here.gather_flips(vector, here.group_bits[:1])
    vector = after(vector, *received[1:])
    y_low, x_low = after(y_low, *received[1:]), after(x_low, *received[1:])
    lows = here.flip(y_low, here.member_mask(2)), here.flip(x_low, here.member_mask(4))
    from_next = after(from_next, vector)
    input_gradient = last_sum(even, odd, lows, highs, from_next, tokens)[None]
    vectors = [vector] + [here.flip(vector, here.member_mask(2 * i)) for i in (1, 2, 3)]
    vectors = jnp.concatenate(vectors, axis=0)
    gradient_norm = jnp.sqrt(jnp.sum(vectors[:, -LANES:]) + jnp.sum(jnp.square(vectors[:, :-LANES])))
    bias_raw = bias_columns(vectors, here, width, own_bias)

    clip_factor = jnp.minimum(1.0, CLIP_NORM / (gradient_norm + 1e-06))
    raw = place_gradient(received, member, weight.shape)
    weight_gradient = clip_factor * raw.astype(F32)
    bias_gradient = clip_factor * bias_raw
    new_weight, new_first_weight, new_second_weight = adamw(
        weight, weight_gradient, first_weight, second_weight, RATE_WEIGHT
    )
    new_bias, new_first_bias, new_second_bias = adamw(
        gate_bias, bias_gradient, first_bias, second_bias, RATE_BIAS
    )
    return (
        hidden,
        final_state,
        input_gradient,
        weight_gradient,
        bias_gradient,
        gradient_norm,
        new_weight,
        new_first_weight,
        new_second_weight,
        new_bias,
        new_first_bias,
        new_second_bias,
    )


def solution(mesh):
    placed = (
        P("stream", "seq", None),
        P("stream", "seq"),
        P("stream", None),
        P(None, ("seq", "stream"), None),
        P(("seq", "stream")),
        P(None, ("seq", "stream"), None),
        P(None, ("seq", "stream"), None),
        P(("seq", "stream")),
        P(("seq", "stream")),
        P("stream", "seq", None),
        P("stream", None),
    )
    return jax.shard_map(
        on_device,
        mesh=mesh,
        in_specs=placed,
        out_specs=(
            P("stream", "seq", None),
            P("stream", "seq"),
            P("stream", "seq", None),
            P(None, ("seq", "stream"), None),
            P(("seq", "stream")),
            P(),
            P(None, ("seq", "stream"), None),
            P(None, ("seq", "stream"), None),
            P(None, ("seq", "stream"), None),
            P(("seq", "stream")),
            P(("seq", "stream")),
            P(("seq", "stream")),
        ),
        check_vma=False,
    )
```
